32 devices in a mesh: docs: 16 (over z, y, x), lists: 2 (over core).
Axes of the slice: x: 2, y: 2, z: 4, core: 2. Of those that a mesh axis runs over, the one named last changes fastest.
Arguments:
- tokens: float32 [2, 32, 512, 768], P('lists', 'docs'), may hold values from -6 to 6
- pair_lengths: int32 [2, 32, 6], P('lists', 'docs'), may hold values from 1 to 128, 480 in all within a row
- list_ids: int32 [2, 192], P('lists'), may hold values from 0 to 7
- relevance: int32 [2, 192], P('lists'), may hold values from 0 to 3
- first_gain: float32 [768], replicated, may hold values from 0.5 to 1.5
- query_weight: float32 [768, 768], replicated, may hold values from -0.02734375 to 0.02734375
- key_weight: float32 [768, 768], replicated, may hold values from -0.21875 to 0.21875
- value_weight: float32 [768, 768], replicated, may hold values from -0.21875 to 0.21875
- output_weight: float32 [768, 768], replicated, may hold values from -0.875 to 0.875
- bias_table: float32 [32, 12], replicated, may hold values from -4 to 4
- second_gain: float32 [768], replicated, may hold values from 0.5 to 1.5
- inner_weight: float32 [768, 3072], replicated, may hold values from -0.21875 to 0.21875
- outer_weight: float32 [3072, 768], replicated, may hold values from -0.109375 to 0.109375
- final_gain: float32 [768], replicated, may hold values from 0.5 to 1.5
- score_vector: float32 [768], replicated, may hold values from -0.625 to 0.625
Outputs:
- encoded: float32 [2, 32, 512, 768], P('lists', 'docs')
- scores: float32 [2, 32, 6], P('lists', 'docs')
- tokens_grad: float32 [2, 32, 512, 768], P('lists', 'docs')
- first_gain_grad: float32 [768], replicated
- query_weight_grad: float32 [768, 768], replicated
- key_weight_grad: float32 [768, 768], replicated
- value_weight_grad: float32 [768, 768], replicated
- output_weight_grad: float32 [768, 768], replicated
- bias_table_grad: float32 [32, 12], replicated
- second_gain_grad: float32 [768], replicated
- inner_weight_grad: float32 [768, 3072], replicated
- outer_weight_grad: float32 [3072, 768], replicated
- final_gain_grad: float32 [768], replicated
- score_vector_grad: float32 [768], replicated
The draws below stay inside these ranges and needn't reach their ends.
Inputs may be any that keep to these rules, and one draw needn't show every extreme that they name: `pair_lengths`: in every row the 6 lengths add up to 480 and the largest is exactly 128; the last 32 positions of a row are padding.
All inputs are finite; a program needn't handle non-finite values.
Results may differ from the reference program's by a relative error of at most 0.02.
Values may be sent and summed in bfloat16 or wider, within the bound.
No kernel may reach another device: no remote copies, remote signals or barrier semaphores. Data moves between devices by JAX's collectives and lax.ppermute only.
A program may use at most 256 MiB of HBM per device.

```python
import math
import jax
import jax.numpy as jnp
import numpy as np
from jax import lax

D = 768
HEADS = 12
HEAD_DIM = 64
FF = 3072
BUCKETS = 32
SEQ = 512
PAIRS_ROW = 6
MOST = 128
FILL = 480
LIST_GROUP = 8
GROUP_ROWS = 32
GROUP_PAIRS = 192
N_LISTS = 2


def place_ends(drawn, key, smallest, largest):
    index_at = [jax.random.randint(jax.random.fold_in(key, axis), (), 0, length) for axis, length in enumerate(drawn.shape)]
    widest = drawn.shape.index(max(drawn.shape))
    beside = index_at[:widest] + [(index_at[widest] + 1) % drawn.shape[widest]] + index_at[widest + 1:]
    return drawn.at[tuple(index_at)].set(smallest).at[tuple(beside)].set(largest)


def levels(own_key, dims, split, smallest, top_value):
    def one(position, blocks):
        steps = jax.random.uniform(jax.random.fold_in(jax.random.fold_in(own_key, 6), position), (blocks,), jnp.float32, smallest / len(split), top_value / len(split))
        return jnp.repeat(jnp.exp(steps), dims[position] // blocks).reshape((-1,) + (1,) * (len(dims) - position - 1))

    level = one(*split[0])
    for cut in split[1:]:
        level = level * one(*cut)
    return level


def length_profile(amount, total, bound, slope):
    loads = [(1 << 20) // math.isqrt(rank ** slope) + 1 for rank in range(2, amount + 1)]
    spare, holding = total - bound - (amount - 1), [1] * (amount - 1)
    while spare > 0:
        candidates = [i for i in range(amount - 1) if holding[i] < bound]
        mass, budget = sum([loads[i] for i in candidates]), spare
        for i in candidates:
            addition = min(bound - holding[i], max(1, budget * loads[i] // mass), spare)
            holding[i] = holding[i] + addition
            spare = spare - addition
    return np.array([bound] + holding)


def ragged_sizes(stream_key, number_of, total, most, skew):
    if number_of == 2:
        one = jax.random.randint(stream_key, (), max(1, total - most), min(most, total - 1) + 1)
        return jnp.stack([one, total - one])
    sizes = jnp.asarray(length_profile(number_of, total, most, skew), jnp.int32)
    couples = (number_of - 1) // 2
    donor, taker = sizes[1:1 + 2 * couples:2], sizes[2:2 + 2 * couples:2]
    margin = jnp.minimum(donor - 1, most - taker)
    moved = jax.random.randint(jax.random.fold_in(stream_key, 1), (couples,), 0, 1 << 20) % (margin + 1)
    sizes = sizes.at[1:1 + 2 * couples:2].set(donor - moved).at[2:2 + 2 * couples:2].set(taker + moved)
    return sizes[jax.random.permutation(jax.random.fold_in(stream_key, 2), number_of)]


def noise(own_key, shape, spread, reach, cuts=(), held_as=jnp.bfloat16):
    loudness = levels(own_key, shape, cuts, -0.22, 0.18) if cuts else 1.0
    values = jax.random.normal(own_key, shape, jnp.float32) * spread * loudness
    return jnp.minimum(jnp.maximum(values, -reach), reach).astype(held_as)


def setup_inputs(seed: int = 0) -> dict:
    key_of = jax.random.split(jax.random.key(seed), 16)
    return {
        "tokens": noise(key_of[0], (N_LISTS, GROUP_ROWS, SEQ, D), 1.0, 6.0, ((0, 2), (1, 16)), jnp.float32),
        "pair_lengths": jax.vmap(lambda own: ragged_sizes(own, PAIRS_ROW, FILL, MOST, 1))(jax.random.split(key_of[1], N_LISTS * GROUP_ROWS)).reshape((N_LISTS, GROUP_ROWS, PAIRS_ROW)).astype(jnp.int32),
        "list_ids": place_ends(jax.random.randint(key_of[2], (N_LISTS, GROUP_PAIRS), 0, LIST_GROUP), jax.random.fold_in(key_of[2], 1), 0, LIST_GROUP - 1).astype(jnp.int32),
        "relevance": place_ends(jax.random.randint(key_of[3], (N_LISTS, GROUP_PAIRS), 0, 4), jax.random.fold_in(key_of[3], 1), 0, 3).astype(jnp.int32),
        "first_gain": jnp.clip(1.0 + 0.1 * jax.random.normal(key_of[4], (D,), jnp.float32), 0.5, 1.5),
        "query_weight": noise(key_of[5], (D, D), (D * HEAD_DIM) ** -0.5, 0.02734375, (), jnp.float32),
        "key_weight": noise(key_of[6], (D, D), D ** -0.5, 0.21875, (), jnp.float32),
        "value_weight": noise(key_of[7], (D, D), D ** -0.5, 0.21875, (), jnp.float32),
        "output_weight": noise(key_of[8], (D, D), (D // 16) ** -0.5, 0.875, (), jnp.float32),
        "bias_table": noise(key_of[9], (BUCKETS, HEADS), 0.8, 4.0, (), jnp.float32),
        "second_gain": jnp.clip(1.0 + 0.1 * jax.random.normal(key_of[10], (D,), jnp.float32), 0.5, 1.5),
        "inner_weight": noise(key_of[11], (D, FF), D ** -0.5, 0.21875, (), jnp.float32),
        "outer_weight": noise(key_of[12], (FF, D), FF ** -0.5, 0.109375, (), jnp.float32),
        "final_gain": jnp.clip(1.0 + 0.1 * jax.random.normal(key_of[13], (D,), jnp.float32), 0.5, 1.5),
        "score_vector": noise(key_of[14], (D,), (D // 8) ** -0.5, 0.625, (), jnp.float32),
    }


epsilon = 1e-06
negative = -1000000000.0
highest = lax.Precision.HIGHEST
limits = (12, 16, 23, 32, 46, 64, 91)

@jax.custom_vjp
def low(v):
    return lax.optimization_barrier(v.astype(jnp.bfloat16)).astype(jnp.float32)

@jax.custom_vjp
def low_back(v):
    return v

def low_keep(v):
    return (low(v), None)

def low_pass(kept, grad):
    return (grad,)

def back_keep(v):
    return (v, None)

def back_low(kept, grad):
    return (low(grad),)
low.defvjp(low_keep, low_pass)
low_back.defvjp(back_keep, back_low)

def smooth_gate(values):
    return jax.nn.gelu(values, approximate=True)

def bucket_of(offsets):
    upper_half = jnp.where(offsets > 0, 16, 0).astype(jnp.int32)
    distance = jnp.abs(offsets).astype(jnp.int32)
    passed = jnp.stack([(distance >= border).astype(jnp.int32) for border in limits], axis=0)
    beyond = (8 + lax.optimization_barrier(jnp.sum(passed, axis=0, dtype=jnp.int32))).astype(jnp.int32)
    return (upper_half + jnp.where(distance < 8, distance, beyond)).astype(jnp.int32)

def rms_norm(inputs, gain):
    return inputs * lax.rsqrt(lax.optimization_barrier(jnp.mean(inputs * inputs, axis=-1, keepdims=True)) + epsilon) * gain

def matmul(left_rows, right_rows):
    return jnp.dot(left_rows, right_rows, precision=highest)

def encode_row(token_row, lengths, weight_set):
    first_gain, query_weight, key_weight, value_weight, output_weight, bias_table, second_gain, inner_weight, outer_weight, final_gain, score_vector = weight_set
    lengths = lengths.astype(jnp.int32)
    pair_ends = jnp.cumsum(lengths, dtype=jnp.int32).astype(jnp.int32)
    starts = (pair_ends - lengths).astype(jnp.int32)
    positions = jnp.arange(SEQ, dtype=jnp.int32)
    segment = lax.optimization_barrier(jnp.sum((positions[:, None] >= pair_ends[None, :]).astype(jnp.int32), axis=1, dtype=jnp.int32)).astype(jnp.int32)
    allowed = segment[:, None] == segment[None, :]
    position_bias = jnp.transpose(bias_table[bucket_of(positions[None, :] - positions[:, None])], (2, 0, 1))
    normed_one = low(rms_norm(token_row, first_gain))
    queries = low(low_back(matmul(normed_one, query_weight))).reshape(SEQ, HEADS, HEAD_DIM)
    key_rows = low(low_back(matmul(normed_one, key_weight))).reshape(SEQ, HEADS, HEAD_DIM)
    value_rows = low(low_back(matmul(normed_one, value_weight))).reshape(SEQ, HEADS, HEAD_DIM)
    logits = jnp.einsum('qhd,khd->hqk', queries, key_rows, precision=highest) + position_bias
    logits = jnp.where(allowed[None], low_back(logits), negative)
    row_peak = lax.optimization_barrier(jnp.max(logits, axis=-1, keepdims=True))
    log_total = row_peak + jnp.log(lax.optimization_barrier(jnp.sum(jnp.exp(logits - row_peak), axis=-1, keepdims=True)))
    probs = jnp.exp(logits - log_total)
    context = jnp.einsum('hqk,khd->qhd', low(probs), value_rows, precision=highest).reshape(SEQ, D)
    context = low(low_back(context))
    attended = token_row + low_back(matmul(context, output_weight))
    normed_two = low(rms_norm(attended, second_gain))
    preact = low_back(matmul(normed_two, inner_weight))
    hidden = low(smooth_gate(preact))
    encoded_row = attended + low_back(matmul(hidden, outer_weight))
    row_scores = matmul(rms_norm(encoded_row[starts], final_gain), score_vector)
    return (encoded_row, row_scores)

def reference(tokens, pair_lengths, list_ids, relevance, first_gain, query_weight, key_weight, value_weight, output_weight, bias_table, second_gain, inner_weight, outer_weight, final_gain, score_vector):
    weight_set = (first_gain, query_weight, key_weight, value_weight, output_weight, bias_table, second_gain, inner_weight, outer_weight, final_gain, score_vector)
    token_rows = tokens.reshape(-1, SEQ, D)
    row_lengths = pair_lengths.reshape(-1, PAIRS_ROW).astype(jnp.int32)
    list_range = jnp.arange(LIST_GROUP, dtype=jnp.int32)
    member = list_ids.astype(jnp.int32)[:, :, None] == list_range[None, None, :]
    labels = relevance.astype(jnp.float32)
    member_count = lax.optimization_barrier(jnp.sum(member.astype(jnp.float32), axis=1))

    def forward(token_arg, weight_arg):
        rounded = (weight_arg[0], low(weight_arg[1]), low(weight_arg[2]), low(weight_arg[3]), low(weight_arg[4]), weight_arg[5], weight_arg[6], low(weight_arg[7]), low(weight_arg[8]), weight_arg[9], weight_arg[10])
        checked = jax.checkpoint(lambda token_row, lengths: encode_row(token_row, lengths, rounded))
        encoded_rows, row_scores = lax.map(lambda row_item: checked(row_item[0], row_item[1]), (token_arg, row_lengths))
        group_scores = row_scores.reshape(N_LISTS, GROUP_PAIRS)
        list_top = lax.optimization_barrier(jnp.max(jnp.where(member, group_scores[:, :, None], negative), axis=1))
        shifted = jnp.where(member, group_scores[:, :, None] - list_top[:, None, :], negative)
        list_total = jnp.where(member_count > 0, lax.optimization_barrier(jnp.sum(jnp.exp(shifted), axis=1)), 1.0)
        log_list = list_top + jnp.log(list_total)
        pair_log = lax.optimization_barrier(jnp.sum(jnp.where(member, log_list[:, None, :], 0.0), axis=2))
        list_loss = jnp.sum(labels * (pair_log - group_scores))
        return (list_loss, (encoded_rows, row_scores))
    list_loss, pullback, outputs_aux = jax.vjp(forward, token_rows, weight_set, has_aux=True)
    token_grad, weight_grads = pullback(jnp.ones_like(list_loss))
    encoded_rows, row_scores = outputs_aux
    return (encoded_rows.reshape(tokens.shape), row_scores.reshape(N_LISTS, GROUP_ROWS, PAIRS_ROW), token_grad.reshape(tokens.shape), weight_grads[0], weight_grads[1], weight_grads[2], weight_grads[3], weight_grads[4], weight_grads[5], weight_grads[6], weight_grads[7], weight_grads[8], weight_grads[9], weight_grads[10])
```

```python
import functools
import math

import jax
import jax.numpy as jnp
from jax import lax
from jax.experimental import pallas as pl
from jax.experimental.pallas import tpu as pltpu
from jax.sharding import PartitionSpec as P

epsilon = 1e-06
negative = -1000000000.0
highest = lax.Precision.HIGHEST
limits = (12, 16, 23, 32, 46, 64, 91)
f32 = jnp.float32
bf16 = jnp.bfloat16
window = 128
reach = 144
lanes_path = 256
group = 16
curve = math.sqrt(2.0 / math.pi)
cubic = 0.044715
whole = pl.BlockSpec(memory_space=pltpu.VMEM)
scalars = pl.BlockSpec(memory_space=pltpu.SMEM)
anywhere = pl.BlockSpec(memory_space=pl.ANY)


def mm(a, b):
    return lax.dot_general(a, b, (((1,), (0,)), ((), ())), preferred_element_type=f32)


def mm_nt(a, b):
    return lax.dot_general(a, b, (((1,), (1,)), ((), ())), preferred_element_type=f32)


def mm_tn(a, b):
    return lax.dot_general(a, b, (((0,), (0,)), ((), ())), preferred_element_type=f32)


def iota(shape, axis):
    return lax.broadcasted_iota(jnp.int32, shape, axis)


def bucket_of(offsets):
    upper_half = jnp.where(offsets > 0, 16, 0)
    distance = jnp.abs(offsets)
    beyond = jnp.full(offsets.shape, 8, jnp.int32)
    for border in limits:
        beyond = beyond + jnp.where(distance >= border, 1, 0)
    return upper_half + jnp.where(distance < 8, distance, beyond)


def rms_factor(values):
    return lax.rsqrt(jnp.mean(values * values, axis=-1, keepdims=True) + epsilon)


def norm_back(normed, factor, upstream):
    return factor * (upstream - normed * jnp.mean(upstream * normed, axis=-1, keepdims=True))


def gelu(values):
    inner = curve * (values + cubic * (values * values * values))
    return 0.5 * values * (1.0 + jnp.tanh(inner))


def gelu_pair(values):
    square = values * values
    bent = jnp.tanh(curve * (values + cubic * (square * values)))
    half = 0.5 * (1.0 + bent)
    slope = half + 0.5 * values * (1.0 - bent * bent) * (curve * (1.0 + (3.0 * cubic) * square))
    return half * values, slope


def bias_vector(table, lanes, origin):
    buckets = table.shape[0]
    buckets_at = bucket_of(iota((buckets, lanes), 1) - origin)
    chosen = jnp.where(buckets_at == iota((buckets, lanes), 0), 1.0, 0.0)
    return lax.dot_general(
        table, chosen, (((0,), (0,)), ((), ())), precision=highest, preferred_element_type=f32
    )


def cast_rows(target, source, chunk):
    rows = source.shape[0]

    def step(i, carry):
        at = pl.ds(pl.multiple_of(i * chunk, chunk), chunk)
        target[at, :] = source[at, :].astype(bf16)
        return carry

    lax.fori_loop(0, rows // chunk, step, 0)


def starts_of(lengths, row, count):
    out, at = [], 0
    for i in range(count):
        out.append((at, lengths[row, i]))
        at = at + lengths[row, i]
    return out


def path_kernel(
    dims,
    lengths, ids, labels,
    tokens, first_gain, second_gain, final_gain, score_vector, table,
    wq_in, wk_in, wv_in, wo_in, wi_in, wf_in,
    pay, factors, n1_out, probs_out, dl_out, turned_out, yk_out, yv_out, qf_out, gctx_out, z_out, vz_out,
    ga_out, a2_out, fhat_out, yq_out,
    wq_out, wk_out, wv_out, wo_out, wi_out, wf_out,
    square, wide, wq, wk, wv, wo, wi, wf, padded, first, gather_z, logits, expand, wide_z,
    in_sems, out_sems,
):
    rows, length, width, pairs, heads, docs = dims
    count = rows * pairs
    n_in = [wq_in, wk_in, wv_in, wo_in]
    n_low = [wq, wk, wv, wo]
    n_out = [wq_out, wk_out, wv_out, wo_out]
    hidden = wi.shape[1]
    parts = hidden // width
    loads = [pltpu.make_async_copy(n_in[i], square.at[i], in_sems.at[i]) for i in range(4)]
    wide_load = pltpu.make_async_copy(wi_in, wide, in_sems.at[4])
    for load in loads:
        load.start()
    wide_load.start()

    gain = first_gain[...]
    for r in range(rows):
        padded[r, length:, :] = jnp.zeros((reach, width), bf16)

        def norm_step(i, carry, r=r):
            at = pl.ds(pl.multiple_of(i * 64, 64), 64)
            x = tokens[r, at, :]
            n = (x * rms_factor(x) * gain).astype(bf16)
            n1_out[r, at, :] = n
            padded[r, at, :] = n
            return carry

        lax.fori_loop(0, length // 64, norm_step, 0)
    first[...] = jnp.zeros(first.shape, f32)
    pieces = []
    for r in range(rows):
        for at, size in starts_of(lengths, r, pairs):
            p = len(pieces)
            shift = at & (group - 1)
            pieces.append((r, pl.multiple_of(at - shift, group), shift, size))
            first[p : p + 1, :] = tokens[r, pl.ds(at, 1), :]

    def nearby(p):
        r, base, _, _ = pieces[p]
        return padded[r, pl.ds(base, reach), :]

    spots = [slice(p * group, (p + 1) * group) for p in range(count)]
    head_rows = iota((group, width), 0) == lax.shift_right_logical(
        iota((group, width), 1), int(math.log2(width // heads))
    )

    def widen(values):
        for p in range(count):
            expand[p * group : (p + 1) * group, :] = jnp.where(
                head_rows, values[p : p + 1, :], 0.0
            ).astype(bf16)

    def narrow(target):
        target[...] = jnp.zeros(target.shape, f32)
        for p in range(count):
            block = wide_z[p * group : (p + 1) * group, :]
            target[p : p + 1, :] = jnp.sum(
                jnp.where(head_rows, block, 0.0), axis=0, keepdims=True
            )

    stores = []

    def take(i):
        loads[i].wait()
        cast_rows(n_low[i], square.at[i], 64)
        store = pltpu.make_async_copy(n_low[i], n_out[i], out_sems.at[i])
        store.start()
        stores.append(store)
        if i < parts:
            part = pltpu.make_async_copy(
                wf_in.at[pl.ds(i * width, width), :], square.at[i], in_sems.at[5 + i]
            )
            part.start()
            return part

    wf_loads = [take(0)]
    n1_first = (first[...] * rms_factor(first[...]) * gain).astype(bf16)
    q_first = mm(n1_first, wq[...]).astype(bf16)
    qf_out[...] = q_first
    widen(q_first.astype(f32))
    wf_loads.append(take(1))
    yk_out[...] = mm_nt(expand[...], wk[...]).astype(bf16)
    position = bias_vector(table[...], lanes_path, 0)
    position = jnp.concatenate([position, jnp.zeros((group - heads, lanes_path), f32)], axis=0)
    lane = iota((group, lanes_path), 1)
    for p, (_, _, shift, size) in enumerate(pieces):
        logits[spots[p], :reach] = mm_nt(yk_out[spots[p], :], nearby(p))
        block = logits[spots[p], :] + pltpu.roll(position, shift, 1)
        inside = jnp.logical_and(lane >= shift, lane < shift + size)
        logits[spots[p], :] = jnp.where(inside, block, negative)
    wf_loads.append(take(2))
    wf_loads.append(take(3))
    scores_in = logits[...]
    peak = jnp.max(scores_in, axis=-1, keepdims=True)
    raised = jnp.exp(scores_in - peak)
    probs = raised / jnp.sum(raised, axis=-1, keepdims=True)
    probs_out[...] = probs.astype(bf16)
    for p in range(count):
        vz_out[spots[p], :] = mm(probs_out[spots[p], :reach], nearby(p)).astype(bf16)
    wide_z[...] = mm(vz_out[...], wv[...])
    narrow(gather_z)
    context = gather_z[...].astype(bf16)
    attended = first[...] + mm(context, wo[...])
    scale_two = rms_factor(attended)
    second = attended * scale_two
    normed_two = (second * second_gain[...]).astype(bf16)
    wide_load.wait()
    cast_rows(wi, wide, 32)
    store = pltpu.make_async_copy(wi, wi_out, out_sems.at[4])
    store.start()
    stores.append(store)
    value, slope = gelu_pair(mm(normed_two, wi[...]))
    for i, load in enumerate(wf_loads):
        load.wait()
        cast_rows(wf.at[pl.ds(i * width, width), :], square.at[i], 64)
    store = pltpu.make_async_copy(wf, wf_out, out_sems.at[5])
    store.start()
    stores.append(store)
    encoded = attended + mm(value.astype(bf16), wf[...])
    scale_final = rms_factor(encoded)
    final_hat = encoded * scale_final
    fhat_out[...] = final_hat
    unit = score_vector[...] * final_gain[...]
    score_col = jnp.sum(final_hat * unit, axis=-1, keepdims=True)
    square_lane = iota((group, 128), 1)
    row = jnp.sum(
        jnp.where(square_lane == iota((group, 128), 0), score_col, 0.0), axis=0, keepdims=True
    )
    row_lane = iota((1, 128), 1)
    place = lax.axis_index("docs") * count
    for i in range(count):
        row = jnp.where(row_lane == group + i, ids[0, place + i].astype(f32), row)
        row = jnp.where(row_lane == 2 * group + i, labels[0, place + i].astype(f32), row)
    pay[...] = row

    grad_encoded = norm_back(final_hat, scale_final, jnp.broadcast_to(unit, final_hat.shape))
    grad_branch = grad_encoded.astype(bf16)
    grad_preact = (mm_nt(grad_branch, wf[...]) * slope).astype(bf16)
    grad_normed_two = mm_nt(grad_preact, wi[...])
    a2_out[...] = second * grad_normed_two
    grad_attended = grad_encoded + norm_back(second, scale_two, grad_normed_two * second_gain[...])
    ga_out[...] = grad_attended
    grad_attn = grad_attended.astype(bf16)
    grad_context = mm_nt(grad_attn, wo[...])
    gctx_out[...] = grad_context
    widen(grad_context)
    yv_out[...] = mm_nt(expand[...], wv[...]).astype(bf16)
    logits[...] = jnp.zeros(logits.shape, f32)
    for p in range(count):
        logits[spots[p], :reach] = mm_nt(yv_out[spots[p], :], nearby(p))
    grad_probs = logits[...]
    grad_logits = probs * (grad_probs - jnp.sum(probs * grad_probs, axis=-1, keepdims=True))
    dl_out[...] = grad_logits.astype(bf16)
    for p, (_, _, shift, _) in enumerate(pieces):
        rounded = dl_out[spots[p], :]
        z_out[spots[p], :] = mm(rounded[:, :reach], nearby(p))
        turned = pltpu.roll(rounded.astype(f32), (lanes_path - shift) & (lanes_path - 1), 1)
        turned_out[spots[p], :] = turned[:, :window]
    wide_z[...] = mm(z_out[...].astype(bf16), wk[...])
    narrow(gather_z)
    grad_query = gather_z[...].astype(bf16)
    yq_out[...] = mm_nt(grad_query, wq[...])
    for i, member in enumerate((n1_first, grad_query, context, grad_attn, normed_two, grad_branch)):
        factors[:, i * width : (i + 1) * width] = member
    for store in stores:
        store.wait()


def path_call(tokens, lengths, ids, labels, gains, table, weights):
    rows, length, width = tokens.shape
    pairs = lengths.shape[1]
    heads = table.shape[1]
    hidden = weights[4].shape[1]
    combos = rows * pairs * group
    shape = jax.ShapeDtypeStruct
    outs = [
        shape((1, 128), f32),
        shape((group, 6 * width), bf16),
        shape((rows, length, width), bf16),
        shape((combos, lanes_path), bf16),
        shape((combos, lanes_path), bf16),
        shape((combos, window), f32),
        shape((combos, width), bf16),
        shape((combos, width), bf16),
        shape((group, width), bf16),
        shape((group, width), f32),
        shape((combos, width), f32),
        shape((combos, width), bf16),
        shape((group, width), f32),
        shape((group, width), f32),
        shape((group, width), f32),
        shape((group, width), f32),
    ]
    low = [shape(w.shape, bf16) for w in weights]
    square_low = pltpu.VMEM((width, width), bf16)
    return pl.pallas_call(
        functools.partial(path_kernel, (rows, length, width, pairs, heads, None)),
        out_shape=outs + low,
        in_specs=[scalars] * 3 + [whole] * 6 + [anywhere] * 6,
        out_specs=[whole] * len(outs) + [anywhere] * 6,
        scratch_shapes=[
            pltpu.VMEM((4, width, width), f32),
            pltpu.VMEM((width, hidden), f32),
            square_low, square_low, square_low, square_low,
            pltpu.VMEM((width, hidden), bf16),
            pltpu.VMEM((hidden, width), bf16),
            pltpu.VMEM((rows, length + reach, width), bf16),
            pltpu.VMEM((group, width), f32),
            pltpu.VMEM((group, width), f32),
            pltpu.VMEM((combos, lanes_path), f32),
            pltpu.VMEM((combos, width), bf16),
            pltpu.VMEM((combos, width), f32),
            pltpu.SemaphoreType.DMA((9,)),
            pltpu.SemaphoreType.DMA((6,)),
        ],
        compiler_params=pltpu.CompilerParams(vmem_limit_bytes=58 << 20),
        cost_estimate=pl.CostEstimate(flops=int(9e9), bytes_accessed=int(5e7), transcendentals=0),
        name="path",
    )(lengths, ids, labels, tokens, *gains, table, *weights)


def code_of(stages, indices):
    total = len(stages)
    code = 0
    for s, (axis, mask) in enumerate(stages):
        bit = jnp.where((indices[axis] & mask) != 0, 1, 0) if not isinstance(
            indices[axis], int
        ) else (1 if indices[axis] & mask else 0)
        code = code + bit * (1 << (total - 1 - s))
    return code


def cut_stages(stages, width):
    count = 0
    while count < len(stages) and (2 * width) % (group << (count + 1)) == 0:
        count += 1
    return stages[:count]


def own_code(stages):
    return code_of(stages, {axis: lax.axis_index(axis) for axis in ("docs", "lists")})


def terms_kernel(
    dims,
    pay, z, vz, qf, gctx, dl, a2, fhat, final_gain, score_vector,
    keep, send, g_all, g_own, smalls,
    ranked, term, left, right,
):
    stages, docs, lists, list_count, count, heads, buckets = dims
    devices = docs * lists
    width = z.shape[1]
    me = own_code(stages)
    everything = pay[...]
    lane = iota(everything.shape, 1)
    score = everything
    names = pltpu.roll(everything, 128 - group, 1)
    label = pltpu.roll(everything, 128 - 2 * group, 1)
    used = lane < count
    part = lax.shift_right_logical(iota(everything.shape, 0), int(math.log2(docs)))
    key = jnp.where(used, part * list_count + names.astype(jnp.int32), -1)

    def total_of(values):
        return jnp.sum(jnp.sum(values, axis=1, keepdims=True), axis=0, keepdims=True)

    def top_step(k, top):
        member = key == k
        best = jnp.max(
            jnp.max(jnp.where(member, score, negative), axis=1, keepdims=True),
            axis=0, keepdims=True,
        )
        return jnp.where(member, best, top)

    keys = lists * list_count
    unroll = keys if keys <= 16 else 4
    top = lax.fori_loop(0, keys, top_step, score, unroll=unroll)
    raised = jnp.exp(score - top)

    def sum_step(k, carry):
        total, gain = carry
        member = key == k
        return (
            jnp.where(member, total_of(jnp.where(member, raised, 0.0)), total),
            jnp.where(member, total_of(jnp.where(member, label, 0.0)), gain),
        )

    ones = jnp.ones(everything.shape, f32)
    total, gain = lax.fori_loop(0, keys, sum_step, (ones, ones), unroll=unroll)
    grads = jnp.where(used, raised / total * gain - label, 0.0)
    ranked[...] = grads
    for d in range(devices):
        code = code_of(stages, {"docs": d // lists, "lists": d % lists})
        g_all[d : d + 1, :] = ranked[pl.ds(me ^ code, 1), :]
    own = ranked[0:1, :]
    g_own[...] = jnp.broadcast_to(own, g_own.shape)

    combos = count * group
    pair_of = lax.shift_right_logical(iota((combos, 128), 0), int(math.log2(group)))
    g_combo = jnp.sum(jnp.where(iota((combos, 128), 1) == pair_of, own, 0.0), axis=1, keepdims=True)
    g_pair = jnp.sum(
        jnp.where(iota((group, 128), 1) == iota((group, 128), 0), own, 0.0), axis=1, keepdims=True
    )
    head_rows = iota((group, width), 0) == lax.shift_right_logical(
        iota((group, width), 1), int(math.log2(width // heads))
    )
    queries = qf[...].astype(f32)
    upstream = gctx[...] * g_pair
    for p in range(count):
        at = slice(p * group, (p + 1) * group)
        right[0, at, :] = jnp.where(head_rows, queries[p : p + 1, :], 0.0).astype(bf16)
        right[1, at, :] = jnp.where(head_rows, upstream[p : p + 1, :], 0.0).astype(bf16)
    left[...] = (z[...] * g_combo).astype(bf16)
    term[0:width, :] = mm_tn(left[...], right[0])
    term[width : 2 * width, :] = mm_tn(vz[...], right[1])

    half, piece = keep.shape[0], keep.shape[1]
    blocks = width // piece
    mine = own_code(stages[: half.bit_length()])

    def piece_step(r, carry, target, base):
        owner = mine ^ (base + r)
        side = lax.shift_right_logical(owner, int(math.log2(blocks)))
        at = side * width + (owner & (blocks - 1)) * piece
        target[r] = term[pl.ds(pl.multiple_of(at, group), piece), :].astype(bf16)
        return carry

    lax.fori_loop(0, half, functools.partial(piece_step, target=send, base=half), 0)
    lax.fori_loop(0, half, functools.partial(piece_step, target=keep, base=0), 0)

    smalls[...] = jnp.zeros(smalls.shape, f32)
    smalls[0:1, :] = jnp.sum(a2[...] * g_pair, axis=0, keepdims=True)
    hats = jnp.sum(fhat[...] * g_pair, axis=0, keepdims=True)
    smalls[1:2, :] = hats * score_vector[...]
    smalls[2:3, :] = hats * final_gain[...]
    weighted = dl[...] * g_combo
    summed = weighted[0:group, :]
    for p in range(1, count):
        summed = summed + weighted[p * group : (p + 1) * group, :]
    spots = iota((window, width), 1)
    hot = jnp.where(bucket_of(iota((window, width), 0)) == (spots & (buckets - 1)), 1.0, 0.0)
    spread = lax.dot_general(
        summed, hot, (((1,), (0,)), ((), ())), precision=highest, preferred_element_type=f32
    )
    row_of = lax.shift_right_logical(iota((group, width), 1), int(math.log2(buckets)))
    smalls[3:4, :] = jnp.sum(
        jnp.where(row_of == iota((group, width), 0), spread, 0.0), axis=0, keepdims=True
    )


def terms_call(dims, pay, z, vz, qf, gctx, dl, a2, fhat, final_gain, score_vector):
    stages, docs, lists, list_count, count, heads, buckets = dims
    devices = docs * lists
    combos, width = z.shape
    pieces = 1 << len(cut_stages(stages, width))
    piece = 2 * width // pieces
    shape = jax.ShapeDtypeStruct
    half = shape((pieces // 2, piece, width), bf16)
    return pl.pallas_call(
        functools.partial(terms_kernel, dims),
        out_shape=[
            half, half,
            shape((devices, 128), f32),
            shape((8, 128), f32),
            shape((8, width), f32),
        ],
        in_specs=[whole] * 10,
        out_specs=[whole] * 5,
        scratch_shapes=[
            pltpu.VMEM((devices, 128), f32),
            pltpu.VMEM((2 * width, width), f32),
            pltpu.VMEM((combos, width), bf16),
            pltpu.VMEM((2, combos, width), bf16),
        ],
        compiler_params=pltpu.CompilerParams(vmem_limit_bytes=24 << 20),
        cost_estimate=pl.CostEstimate(flops=int(4e9), bytes_accessed=int(1e7), transcendentals=0),
        name="terms",
    )(pay, z, vz, qf, gctx, dl, a2, fhat, final_gain, score_vector)


def attention_kernel(
    dims,
    lengths, n1, tokens, table, wq_in, wk_in, wv_in, wo_in,
    out,
    wq, wk, wv, wo, q, k, v, ctx, bias, sems,
):
    row, heads, pairs = dims
    length, width = n1.shape[1], n1.shape[2]
    names = ((wq_in, wq), (wk_in, wk), (wv_in, wv), (wo_in, wo))
    loads = [pltpu.make_async_copy(a, b, sems.at[i]) for i, (a, b) in enumerate(names)]
    for load in loads:
        load.start()
    lanes = 4 * window
    vector = bias_vector(table[...], lanes, window)
    for h in range(heads):
        bias[h] = pltpu.roll(
            jnp.broadcast_to(vector[h : h + 1, :], (window, lanes)), 0, 1, stride=1, stride_axis=0
        )[:, : 3 * window]
    x = n1[0]
    for load, target, low in ((loads[0], q, wq), (loads[1], k, wk), (loads[2], v, wv)):
        load.wait()
        target[...] = mm(x, low[...]).astype(bf16)
    tiles = length // window
    half = iota((2 * window, window), 1) < (width // heads)
    left = half[:window]
    upper = iota((2 * window, window), 0) < window
    chosen = half == upper
    ends = []
    at = 0
    for i in range(pairs):
        at = at + lengths[row, i]
        ends.append(at)

    def segment(positions):
        total = jnp.zeros(positions.shape, jnp.int32)
        for end in ends:
            total = total + jnp.where(positions >= end, 1, 0)
        return total

    for j in range(tiles):
        t0 = j * window
        k0 = max(j - 1, 0) * window
        k1 = min(j + 2, tiles) * window
        off = k0 - (t0 - window)
        span = k1 - k0
        seg_q = segment(t0 + iota((window, 1), 0))
        seg_k = segment(k0 + iota((1, span), 1))
        allowed = seg_q == seg_k
        for pair in range(heads // 2):
            cols = slice(pair * window, (pair + 1) * window)
            both = q[t0 : t0 + window, cols]
            stacked = jnp.concatenate([both, both], axis=0)
            stacked = jnp.where(chosen, stacked, jnp.zeros_like(stacked))
            raw = mm_nt(stacked, k[k0:k1, cols])
            probs, sums = [], []
            for side in range(2):
                part = raw[side * window : (side + 1) * window]
                part = part + bias[2 * pair + side, :, off : off + span]
                part = jnp.where(allowed, part, negative)
                peak = jnp.max(part, axis=-1, keepdims=True)
                raised = jnp.exp(part - peak)
                sums.append(jnp.sum(raised, axis=-1, keepdims=True))
                probs.append(raised.astype(bf16))
            mixed = mm(jnp.concatenate(probs, axis=0), v[k0:k1, cols])
            ctx[t0 : t0 + window, cols] = jnp.where(
                left, mixed[:window] / sums[0], mixed[window:] / sums[1]
            ).astype(bf16)
    loads[3].wait()
    out[0] = tokens[0] + mm(ctx[...], wo[...])


def attention_call(row, lengths, n1, tokens, table, weights):
    rows, length, width = tokens.shape
    heads = table.shape[1]
    pairs = lengths.shape[1]
    square = pltpu.VMEM((width, width), bf16)
    tall = pltpu.VMEM((length, width), bf16)
    block = pl.BlockSpec((1, length, width), lambda i: (row, 0, 0))
    return pl.pallas_call(
        functools.partial(attention_kernel, (row, heads, pairs)),
        grid=(1,),
        out_shape=jax.ShapeDtypeStruct((1, length, width), f32),
        in_specs=[scalars, block, block, whole] + [anywhere] * 4,
        out_specs=pl.BlockSpec((1, length, width), lambda i: (0, 0, 0)),
        scratch_shapes=[square] * 4 + [tall] * 4 + [
            pltpu.VMEM((heads, window, 3 * window), f32),
            pltpu.SemaphoreType.DMA((4,)),
        ],
        compiler_params=pltpu.CompilerParams(vmem_limit_bytes=32 << 20),
        cost_estimate=pl.CostEstimate(flops=int(9e9), bytes_accessed=int(1e7), transcendentals=0),
        name=f"attention_{row}",
    )(lengths, n1, tokens, table, *weights)


def feed_kernel(attended, gain, wi, wf, held, out, normed, total):
    step = pl.program_id(0)

    @pl.when(step == 0)
    def _():
        x = attended[0]
        normed[...] = (x * rms_factor(x) * gain[...]).astype(bf16)
        total[...] = x

    value = gelu(mm(normed[...], wi[...])).astype(bf16)
    total[...] += mm(value, wf[...])

    @pl.when(step == pl.num_programs(0) - 1)
    def _():
        out[0] = total[...]


def feed_call(row, shape, attended, gain, wi, wf, held):
    rows, length, width = shape
    hidden = wi.shape[1]
    chunk = 768
    still = lambda i: (0, 0, 0)
    extra = [] if held is None else [held]
    kernel = feed_kernel
    if held is None:
        kernel = lambda a, g, i, f, o, n, t: feed_kernel(a, g, i, f, None, o, n, t)
    return pl.pallas_call(
        kernel,
        grid=(hidden // chunk,),
        out_shape=jax.ShapeDtypeStruct(shape, f32),
        in_specs=[
            pl.BlockSpec((1, length, width), still),
            pl.BlockSpec((1, width), lambda i: (0, 0)),
            pl.BlockSpec((width, chunk), lambda i: (0, i)),
            pl.BlockSpec((chunk, width), lambda i: (i, 0)),
        ] + [anywhere] * len(extra),
        out_specs=pl.BlockSpec((1, length, width), lambda i: (row, 0, 0)),
        input_output_aliases={4: 0} if extra else {},
        scratch_shapes=[pltpu.VMEM((length, width), bf16), pltpu.VMEM((length, width), f32)],
        compiler_params=pltpu.CompilerParams(vmem_limit_bytes=32 << 20),
        cost_estimate=pl.CostEstimate(flops=int(6e9), bytes_accessed=int(1e7), transcendentals=0),
        name=f"feed_{row}",
    )(attended, gain, wi, wf, *extra)


def tokens_grad_kernel(
    dims, lengths, tokens, g_own, probs, dl, yk, yv, yq, ga, gain, out, first_sum, spread
):
    length, width, pairs = dims
    row = pl.program_id(0)
    spread[...] = jnp.zeros(spread.shape, f32)
    own = g_own[0:1, :]
    lane = iota((1, 128), 1)
    starts = starts_of(lengths, row, pairs)
    amounts = []
    for i, (at, size) in enumerate(starts):
        pair = row * pairs + i
        amount = jnp.sum(jnp.where(lane == pair, own, 0.0), axis=1, keepdims=True)
        amounts.append(amount)
        here = pl.ds(pl.multiple_of(pair * group, group), group)
        left = jnp.concatenate([dl[here, :], probs[here, :]], axis=0)
        right = jnp.concatenate([yk[here, :], yv[here, :]], axis=0)
        base = pl.multiple_of(at - (at & (group - 1)), group)
        spread[pl.ds(base, reach), :] += mm_tn(left, right)[:reach] * amount
    for i, (at, size) in enumerate(starts):
        pair = row * pairs + i
        spread[pl.ds(at, 1), :] += yq[pl.ds(pair, 1), :] * amounts[i]

    @pl.when(row == 0)
    def _():
        first_sum[...] = jnp.zeros(first_sum.shape, f32)

    def step(i, carry):
        at = pl.ds(pl.multiple_of(i * 64, 64), 64)
        x = tokens[0, at, :]
        factor = rms_factor(x)
        hat = x * factor
        upstream = spread[at, :]
        out[0, at, :] = norm_back(hat, factor, upstream * gain[...])
        return carry + jnp.sum(hat * upstream, axis=0, keepdims=True)

    first_sum[...] += lax.fori_loop(0, length // 64, step, jnp.zeros((1, width), f32))
    for i, (at, size) in enumerate(starts):
        pair = row * pairs + i
        out[0, pl.ds(at, 1), :] += ga[pl.ds(pair, 1), :] * amounts[i]


def tokens_grad_call(lengths, tokens, g_own, probs, dl, yk, yv, yq, ga, gain):
    rows, length, width = tokens.shape
    pairs = lengths.shape[1]
    block = pl.BlockSpec((1, length, width), lambda i: (i, 0, 0))
    return pl.pallas_call(
        functools.partial(tokens_grad_kernel, (length, width, pairs)),
        grid=(rows,),
        out_shape=[
            jax.ShapeDtypeStruct(tokens.shape, f32),
            jax.ShapeDtypeStruct((1, width), f32),
        ],
        in_specs=[scalars, block] + [whole] * 8,
        out_specs=[block, pl.BlockSpec((1, width), lambda i: (0, 0))],
        scratch_shapes=[pltpu.VMEM((length + reach, width), f32)],
        compiler_params=pltpu.CompilerParams(vmem_limit_bytes=32 << 20),
        cost_estimate=pl.CostEstimate(flops=int(2e9), bytes_accessed=int(1e7), transcendentals=0),
        name="tokens_grad",
    )(lengths, tokens, g_own, probs, dl, yk, yv, yq, ga, gain)


def outer_kernel(
    blocks, factors, g, wi, wf, inner_out, outer_out, output_out, query_out, branch, normed
):
    step, block = pl.program_id(0), pl.program_id(1)
    width = branch.shape[1]

    def member(i):
        return factors[:, i * width : (i + 1) * width]

    def put(target, values):
        if blocks == 1:
            target[...] = values
        else:
            target[...] = jnp.where(block == 0, values, target[...] + values)

    def prepare():
        branch[...] = (member(5).astype(f32) * g[...]).astype(bf16)
        normed[...] = member(4)

    @pl.when(step == 0)
    def _():
        if blocks == 1:
            prepare()
        put(query_out, mm_tn(member(0), (member(1).astype(f32) * g[...]).astype(bf16)))
        put(output_out, mm_tn(member(2), (member(3).astype(f32) * g[...]).astype(bf16)))

    if blocks > 1:
        prepare()
    value, slope = gelu_pair(mm(normed[...], wi[...]))
    grad = (mm_nt(branch[...], wf[...]) * slope).astype(bf16)
    put(inner_out, mm_tn(normed[...], grad))
    put(outer_out, mm_tn(value.astype(bf16), branch[...]))


def outer_call(factors, g, wi, wf):
    rows = factors.shape[0]
    width, hidden = wi.shape
    chunk = 384
    block = min(rows, 512)
    blocks = rows // block
    shape = jax.ShapeDtypeStruct
    fixed = lambda i, b: (0, 0)
    return pl.pallas_call(
        functools.partial(outer_kernel, blocks),
        grid=(hidden // chunk, blocks),
        out_shape=[
            shape((width, hidden), f32),
            shape((hidden, width), f32),
            shape((width, width), f32),
            shape((width, width), f32),
        ],
        in_specs=[
            pl.BlockSpec((block, 6 * width), lambda i, b: (b, 0)),
            pl.BlockSpec((block, 1), lambda i, b: (b, 0)),
            pl.BlockSpec((width, chunk), lambda i, b: (0, i)),
            pl.BlockSpec((chunk, width), lambda i, b: (i, 0)),
        ],
        out_specs=[
            pl.BlockSpec((width, chunk), lambda i, b: (0, i)),
            pl.BlockSpec((chunk, width), lambda i, b: (i, 0)),
            pl.BlockSpec((width, width), fixed),
            pl.BlockSpec((width, width), fixed),
        ],
        scratch_shapes=[pltpu.VMEM((block, width), bf16), pltpu.VMEM((block, width), bf16)],
        compiler_params=pltpu.CompilerParams(vmem_limit_bytes=48 << 20),
        cost_estimate=pl.CostEstimate(flops=int(11e9), bytes_accessed=int(4e7), transcendentals=0),
        name="outer",
    )(factors, g, wi, wf)


def last_kernel(dims, gathered, key_out, value_out, small_out):
    stages, devices, piece = dims
    width = key_out.shape[1]
    me = own_code(stages)
    blocks = width // piece
    sides = (key_out, value_out)

    def step(i, carry):
        at = pl.ds(pl.multiple_of(i * piece, group), piece)
        for side in range(2):
            slot = me ^ (side * blocks + i)
            sides[side][at, :] = gathered[slot, :piece, :].astype(f32)
        return carry

    lax.fori_loop(0, blocks, step, 0)

    def add(i, carry):
        return carry + gathered[i, piece:, :].astype(f32)

    small_out[...] = lax.fori_loop(0, devices, add, jnp.zeros(small_out.shape, f32))


def last_call(stages, gathered, piece):
    devices, rows, width = gathered.shape
    shape = jax.ShapeDtypeStruct
    return pl.pallas_call(
        functools.partial(last_kernel, (stages, devices, piece)),
        out_shape=[
            shape((width, width), f32),
            shape((width, width), f32),
            shape((rows - piece, width), f32),
        ],
        in_specs=[whole],
        out_specs=[whole] * 3,
        compiler_params=pltpu.CompilerParams(vmem_limit_bytes=32 << 20),
        cost_estimate=pl.CostEstimate(flops=int(1e7), bytes_accessed=int(1e7), transcendentals=0),
        name="last",
    )(gathered)


def shards(
    docs, lists,
    tokens, pair_lengths, list_ids, relevance,
    first_gain, query_weight, key_weight, value_weight, output_weight, bias_table,
    second_gain, inner_weight, outer_weight, final_gain, score_vector,
):
    row_count, length, width = tokens.shape[1:]
    pairs = pair_lengths.shape[2]
    buckets, heads = bias_table.shape
    devices = docs * lists
    sizes = {"docs": docs, "lists": lists}
    stages = tuple(("lists", 1 << b) for b in range(lists.bit_length() - 1)) + tuple(
        ("docs", 1 << b) for b in range(docs.bit_length() - 1)
    )

    def swap(values, stage):
        axis, mask = stage
        return lax.ppermute(values, axis, [(i, i ^ mask) for i in range(sizes[axis])])

    rows = tokens.reshape(row_count, length, width)
    lengths = pair_lengths.reshape(row_count, pairs)
    flat = lambda vector: vector.reshape(1, width)
    gains = (flat(first_gain), flat(second_gain), flat(final_gain), flat(score_vector))
    outs = path_call(
        rows, lengths, list_ids, relevance, gains, bias_table,
        (query_weight, key_weight, value_weight, output_weight, inner_weight, outer_weight),
    )
    pay, factors, n1, probs, dl, turned, yk, yv, qf, gctx, z, vz, ga, a2, fhat, yq = outs[:16]
    wq, wk, wv, wo, wi, wf = outs[16:]

    gathered_rows = lax.all_gather(factors, ("docs", "lists"), axis=0, tiled=True)

    for stage in reversed(stages):
        pay = jnp.concatenate([pay, swap(pay, stage)], axis=0)
    count = row_count * pairs
    dims = (stages, docs, lists, docs // 2, count, heads, buckets)
    keep, send, g_all, g_own, smalls = terms_call(
        dims, pay, z, vz, qf, gctx, turned, a2, fhat, gains[2], gains[3]
    )
    piece = keep.shape[1]
    g_rows = g_all[:, :group].reshape(devices * group, 1)

    cut = cut_stages(stages, width)
    for i, stage in enumerate(cut):
        if i:
            half = keep.shape[0] // 2
            keep, send = keep[:half], keep[half:]
        keep = keep + swap(send, stage)
    for stage in stages[len(cut) :]:
        keep = keep + swap(keep, stage)

    weights = (wq, wk, wv, wo)
    grads, first_sum = tokens_grad_call(
        lengths, rows, g_own, probs, dl, yk, yv, yq, ga, gains[0]
    )
    encoded = None
    for r in range(row_count):
        attended = attention_call(r, lengths, n1, rows, bias_table, weights)
        encoded = feed_call(r, rows.shape, attended, gains[1], wi, wf, encoded)
    inner_grad, outer_grad, output_grad, query_grad = outer_call(gathered_rows, g_rows, wi, wf)

    smalls = jnp.concatenate([smalls[:4], first_sum, smalls[5:]], axis=0)
    for stage in stages[len(cut) :]:
        smalls = smalls + swap(smalls, stage)
    gathered = jnp.concatenate([keep, smalls.astype(bf16)[None]], axis=1)
    for stage in reversed(cut):
        gathered = jnp.concatenate([gathered, swap(gathered, stage)], axis=0)
    key_grad, value_grad, small_sums = last_call(cut, gathered, piece)
    table_grad = small_sums[3, : heads * buckets].reshape(heads, buckets).T
    scores = outs[0][:, :count]
    return (
        encoded.reshape(tokens.shape),
        scores.reshape(1, row_count, pairs),
        grads.reshape(tokens.shape),
        small_sums[4],
        query_grad,
        key_grad,
        value_grad,
        output_grad,
        table_grad,
        small_sums[0],
        inner_grad,
        outer_grad,
        small_sums[1],
        small_sums[2],
    )


def solution(mesh):
    placed = P("lists", "docs", None, None)
    return jax.shard_map(
        functools.partial(shards, mesh.shape["docs"], mesh.shape["lists"]),
        mesh=mesh,
        in_specs=(placed, P("lists", "docs", None), P("lists", None), P("lists", None)) + (P(),) * 11,
        out_specs=(placed, P("lists", "docs", None), placed) + (P(),) * 11,
        check_vma=False,
    )
```

```python
import functools
import math

import jax
import jax.numpy as jnp
from jax import lax
from jax.experimental import pallas as pl
from jax.experimental.pallas import tpu as pltpu
from jax.sharding import PartitionSpec as P

epsilon = 1e-06
negative = -1000000000.0
highest = lax.Precision.HIGHEST
limits = (12, 16, 23, 32, 46, 64, 91)
f32 = jnp.float32
bf16 = jnp.bfloat16
window = 128
reach = 144
lanes_path = 256
group = 16
mega = 1 << 20
curve = math.sqrt(2.0 / math.pi)
cubic = 0.044715
whole = pl.BlockSpec(memory_space=pltpu.VMEM)
scalars = pl.BlockSpec(memory_space=pltpu.SMEM)
outside = pl.BlockSpec(memory_space=pl.ANY)


def mm(a, b):
    return lax.dot_general(a, b, (((1,), (0,)), ((), ())), preferred_element_type=f32)


def mm_nt(a, b):
    return lax.dot_general(a, b, (((1,), (1,)), ((), ())), preferred_element_type=f32)


def mm_tn(a, b):
    return lax.dot_general(a, b, (((0,), (0,)), ((), ())), preferred_element_type=f32)


def as_row(vector):
    return vector[...].reshape(1, vector.shape[0])


def iota(shape, axis):
    return lax.broadcasted_iota(jnp.int32, shape, axis)


def bucket_of(offsets):
    upper_half = jnp.where(offsets > 0, 16, 0)
    distance = jnp.abs(offsets)
    beyond = jnp.full(offsets.shape, 8, jnp.int32)
    for border in limits:
        beyond = beyond + jnp.where(distance >= border, 1, 0)
    return upper_half + jnp.where(distance < 8, distance, beyond)


def rms_factor(values):
    return lax.rsqrt(jnp.mean(values * values, axis=-1, keepdims=True) + epsilon)


def norm_back(normed, factor, upstream):
    return factor * (upstream - normed * jnp.mean(upstream * normed, axis=-1, keepdims=True))


def half_bent(values, square):
    return 0.5 * jnp.tanh(values * (square * (curve * cubic) + curve)) + 0.5


def gelu(values):
    return values * half_bent(values, values * values)


def gelu_pair(values):
    square = values * values
    half = half_bent(values, square)
    value = half * values
    steep = (value - value * half) * (square * (6.0 * curve * cubic) + 2.0 * curve)
    return value, half + steep


def bias_vector(table, lanes, origin):
    buckets = table.shape[1]
    buckets_at = bucket_of(iota((buckets, lanes), 1) - origin)
    chosen = jnp.where(buckets_at == iota((buckets, lanes), 0), 1.0, 0.0)
    return lax.dot_general(
        table, chosen, (((1,), (0,)), ((), ())), precision=highest, preferred_element_type=f32
    )


def cast_rows(target, source, chunk):
    rows = source.shape[0]

    def step(i, carry):
        at = pl.ds(pl.multiple_of(i * chunk, chunk), chunk)
        target[at, :] = source[at, :].astype(bf16)
        return carry

    lax.fori_loop(0, rows // chunk, step, 0)


def starts_of(lengths, row, count):
    out, at = [], 0
    for i in range(count):
        out.append((at, lengths[row, i]))
        at = at + lengths[row, i]
    return out


def path_kernel(
    dims,
    lengths, ids, labels,
    tokens_in, first_gain, second_gain, final_gain, score_vector, table,
    wq_in, wk_in, wv_in, wo_in, wi_in, wf_in,
    pay, factors, n1_out, probs_out, dl_out, turned_out, yk_out, yv_out, qf_out, gctx_out, z_out, vz_out,
    ga_out, a2_out, fhat_out, yq_out,
    wq, wk, wv, wo, wi, wf, scores_out,
    tokens, square, padded, first, gather_z, logits, expand, wide_z,
    in_sems, tokens_sem,
):
    rows, length, width, pairs, heads = dims
    count = rows * pairs
    parts = wi.shape[1] // width
    slots = square.shape[0]
    chunks = [(wq_in, wq), (wk_in, wk), (wv_in, wv), (wo_in, wo)]
    for i in range(parts):
        at = pl.ds(i * width, width)
        chunks.append((wi_in.at[:, at], wi.at[:, at]))
    for i in range(parts):
        at = pl.ds(i * width, width)
        chunks.append((wf_in.at[at, :], wf.at[at, :]))

    def load_of(i):
        return pltpu.make_async_copy(chunks[i][0], square.at[i % slots], in_sems.at[i % slots])

    tokens_load = pltpu.make_async_copy(tokens_in, tokens, tokens_sem)
    tokens_load.start()
    for i in range(slots):
        load_of(i).start()
    tokens_load.wait()

    gain = as_row(first_gain)
    for r in range(rows):
        padded[r, length:, :] = jnp.zeros((reach, width), bf16)

        def norm_step(i, carry, r=r):
            at = pl.ds(pl.multiple_of(i * 64, 64), 64)
            x = tokens[r, at, :]
            n = (x * rms_factor(x) * gain).astype(bf16)
            n1_out[r, at, :] = n
            padded[r, at, :] = n
            return carry

        lax.fori_loop(0, length // 64, norm_step, 0)
    first[...] = jnp.zeros(first.shape, f32)
    pieces = []
    for r in range(rows):
        for at, size in starts_of(lengths, r, pairs):
            p = len(pieces)
            shift = at & (group - 1)
            pieces.append((r, pl.multiple_of(at - shift, group), shift, size))
            first[p : p + 1, :] = tokens[r, pl.ds(at, 1), :]

    def nearby(p):
        r, base, _, _ = pieces[p]
        return padded[r, pl.ds(base, reach), :]

    spots = [slice(p * group, (p + 1) * group) for p in range(count)]
    head_rows = iota((group, width), 0) == lax.shift_right_logical(
        iota((group, width), 1), int(math.log2(width // heads))
    )

    def widen(values):
        for p in range(count):
            expand[p * group : (p + 1) * group, :] = jnp.where(
                head_rows, values[p : p + 1, :], 0.0
            ).astype(bf16)

    def narrow(target):
        target[...] = jnp.zeros(target.shape, f32)
        for p in range(count):
            block = wide_z[p * group : (p + 1) * group, :]
            target[p : p + 1, :] = jnp.sum(
                jnp.where(head_rows, block, 0.0), axis=0, keepdims=True
            )

    def take(i):
        load_of(i).wait()
        cast_rows(chunks[i][1], square.at[i % slots], 64)
        if i + slots < len(chunks):
            load_of(i + slots).start()

    take(0)
    n1_first = (first[...] * rms_factor(first[...]) * gain).astype(bf16)
    q_first = mm(n1_first, wq[...]).astype(bf16)
    qf_out[...] = q_first
    widen(q_first.astype(f32))
    take(1)
    yk_out[...] = mm_nt(expand[...], wk[...]).astype(bf16)
    position = bias_vector(table[...], lanes_path, 0)
    position = jnp.concatenate([position, jnp.zeros((group - heads, lanes_path), f32)], axis=0)
    lane = iota((group, lanes_path), 1)
    for p, (_, _, shift, size) in enumerate(pieces):
        logits[spots[p], :reach] = mm_nt(yk_out[spots[p], :], nearby(p))
        block = logits[spots[p], :] + pltpu.roll(position, shift, 1)
        inside = jnp.logical_and(lane >= shift, lane < shift + size)
        logits[spots[p], :] = jnp.where(inside, block, negative)
    take(2)
    take(3)
    scores_in = logits[...]
    peak = jnp.max(scores_in, axis=-1, keepdims=True)
    raised = jnp.exp(scores_in - peak)
    probs = raised / jnp.sum(raised, axis=-1, keepdims=True)
    probs_out[...] = probs.astype(bf16)
    for p in range(count):
        vz_out[spots[p], :] = mm(probs_out[spots[p], :reach], nearby(p)).astype(bf16)
    wide_z[...] = mm(vz_out[...], wv[...])
    narrow(gather_z)
    context = gather_z[...].astype(bf16)
    attended = first[...] + mm(context, wo[...])
    scale_two = rms_factor(attended)
    second = attended * scale_two
    normed_two = (second * as_row(second_gain)).astype(bf16)
    for i in range(parts):
        take(4 + i)
    value, slope = gelu_pair(mm(normed_two, wi[...]))
    for i in range(parts):
        take(4 + parts + i)
    encoded = attended + mm(value.astype(bf16), wf[...])
    scale_final = rms_factor(encoded)
    final_hat = encoded * scale_final
    fhat_out[...] = final_hat
    unit = as_row(score_vector) * as_row(final_gain)
    score_col = jnp.sum(final_hat * unit, axis=-1, keepdims=True)
    square_lane = iota((group, 128), 1)
    row = jnp.sum(
        jnp.where(square_lane == iota((group, 128), 0), score_col, 0.0), axis=0, keepdims=True
    )
    for r in range(rows):
        scores_out[r : r + 1, :] = row[:, r * pairs : (r + 1) * pairs]
    row_lane = iota((1, 128), 1)
    place = lax.axis_index("docs") * count
    for i in range(count):
        row = jnp.where(row_lane == group + i, ids[0, place + i].astype(f32), row)
        row = jnp.where(row_lane == 2 * group + i, labels[0, place + i].astype(f32), row)
    pay[...] = row

    grad_encoded = norm_back(final_hat, scale_final, jnp.broadcast_to(unit, final_hat.shape))
    grad_branch = grad_encoded.astype(bf16)
    grad_preact = (mm_nt(grad_branch, wf[...]) * slope).astype(bf16)
    grad_normed_two = mm_nt(grad_preact, wi[...])
    a2_out[...] = second * grad_normed_two
    grad_attended = grad_encoded + norm_back(second, scale_two, grad_normed_two * as_row(second_gain))
    ga_out[...] = grad_attended
    grad_attn = grad_attended.astype(bf16)
    grad_context = mm_nt(grad_attn, wo[...])
    gctx_out[...] = grad_context
    widen(grad_context)
    yv_out[...] = mm_nt(expand[...], wv[...]).astype(bf16)
    logits[...] = jnp.zeros(logits.shape, f32)
    for p in range(count):
        logits[spots[p], :reach] = mm_nt(yv_out[spots[p], :], nearby(p))
    grad_probs = logits[...]
    grad_logits = probs * (grad_probs - jnp.sum(probs * grad_probs, axis=-1, keepdims=True))
    dl_out[...] = grad_logits.astype(bf16)
    for p, (_, _, shift, _) in enumerate(pieces):
        rounded = dl_out[spots[p], :]
        z_out[spots[p], :] = mm(rounded[:, :reach], nearby(p))
        turned = pltpu.roll(rounded.astype(f32), (lanes_path - shift) & (lanes_path - 1), 1)
        turned_out[spots[p], :] = turned[:, :window]
    wide_z[...] = mm(z_out[...].astype(bf16), wk[...])
    narrow(gather_z)
    grad_query = gather_z[...].astype(bf16)
    yq_out[...] = mm_nt(grad_query, wq[...])
    span, half = 3 * width // 2, width // 2
    for i, member in enumerate((n1_first, grad_query, context, grad_attn, normed_two, grad_branch)):
        member = member.astype(f32)
        tail = member[8:, :]
        tail = jnp.where(
            iota((8, half), 0) < 4, tail[:, :half], pltpu.roll(tail[:, half:], 4, 0)
        )
        factors[0, :, i * span : i * span + width] = member[:8].astype(bf16)
        factors[0, :, i * span + width : (i + 1) * span] = tail.astype(bf16)


def path_call(tokens, lengths, ids, labels, gains, table, weights):
    rows, length, width = tokens.shape
    pairs = lengths.shape[1]
    heads = table.shape[0]
    combos = rows * pairs * group
    shape = jax.ShapeDtypeStruct
    outs = [
        shape((1, 128), f32),
        shape((1, 8, 9 * width), bf16),
        shape((rows, length, width), bf16),
        shape((combos, lanes_path), bf16),
        shape((combos, lanes_path), bf16),
        shape((combos, window), f32),
        shape((combos, width), bf16),
        shape((combos, width), bf16),
        shape((group, width), bf16),
        shape((group, width), f32),
        shape((combos, width), f32),
        shape((combos, width), bf16),
        shape((group, width), f32),
        shape((group, width), f32),
        shape((group, width), f32),
        shape((group, width), f32),
    ]
    low = [shape(w.shape, bf16) for w in weights] + [shape((rows, pairs), f32)]
    return pl.pallas_call(
        functools.partial(path_kernel, (rows, length, width, pairs, heads)),
        out_shape=outs + low,
        in_specs=[scalars] * 3 + [outside] + [whole] * 5 + [outside] * 6,
        out_specs=[whole] * (len(outs) + len(low)),
        scratch_shapes=[
            pltpu.VMEM(tokens.shape, f32),
            pltpu.VMEM((12, width, width), f32),
            pltpu.VMEM((rows, length + reach, width), bf16),
            pltpu.VMEM((group, width), f32),
            pltpu.VMEM((group, width), f32),
            pltpu.VMEM((combos, lanes_path), f32),
            pltpu.VMEM((combos, width), bf16),
            pltpu.VMEM((combos, width), f32),
            pltpu.SemaphoreType.DMA((12,)),
            pltpu.SemaphoreType.DMA,
        ],
        compiler_params=pltpu.CompilerParams(vmem_limit_bytes=45 * mega),
        cost_estimate=pl.CostEstimate(flops=int(9e9), bytes_accessed=int(5e7), transcendentals=0),
        name="path",
    )(lengths, ids, labels, tokens, *gains, table, *weights)


def code_of(stages, indices):
    total = len(stages)
    code = 0
    for s, (axis, mask) in enumerate(stages):
        bit = jnp.where((indices[axis] & mask) != 0, 1, 0) if not isinstance(
            indices[axis], int
        ) else (1 if indices[axis] & mask else 0)
        code = code + bit * (1 << (total - 1 - s))
    return code


def cut_stages(stages, width):
    count = 2 + sum(axis == "lists" for axis, _ in stages)
    while (2 * width) % (group << count):
        count -= 1
    return stages[:count]


def own_code(stages):
    return code_of(stages, {axis: lax.axis_index(axis) for axis in ("docs", "lists")})


def terms_kernel(
    dims,
    pay, z, vz, qf, gctx, dl, a2, fhat, final_gain, score_vector,
    keep, send, g_all, g_own, smalls,
    term, left, right,
):
    stages, docs, lists, list_count, count, heads, buckets = dims
    width = z.shape[1]
    everything = pay[...]
    lane = iota(everything.shape, 1)
    score = everything
    names = pltpu.roll(everything, 128 - group, 1)
    label = pltpu.roll(everything, 128 - 2 * group, 1)
    used = lane < count
    part = lax.shift_right_logical(iota(everything.shape, 0), int(math.log2(docs)))
    key = jnp.where(used, part * list_count + names.astype(jnp.int32), -1)

    def total_of(values):
        return jnp.sum(jnp.sum(values, axis=1, keepdims=True), axis=0, keepdims=True)

    def top_step(k, top):
        member = key == k
        best = jnp.max(
            jnp.max(jnp.where(member, score, negative), axis=1, keepdims=True),
            axis=0, keepdims=True,
        )
        return jnp.where(member, best, top)

    keys = lists * list_count
    unroll = keys if keys <= 16 else 4
    top = lax.fori_loop(0, keys, top_step, score, unroll=unroll)
    raised = jnp.exp(score - top)

    def sum_step(k, carry):
        total, gain = carry
        member = key == k
        return (
            jnp.where(member, total_of(jnp.where(member, raised, 0.0)), total),
            jnp.where(member, total_of(jnp.where(member, label, 0.0)), gain),
        )

    ones = jnp.ones(everything.shape, f32)
    total, gain = lax.fori_loop(0, keys, sum_step, (ones, ones), unroll=unroll)
    grads = jnp.where(used, raised / total * gain - label, 0.0)
    g_all[...] = grads
    own = grads[0:1, :]
    g_own[...] = jnp.broadcast_to(own, g_own.shape)

    combos = count * group
    pair_of = lax.shift_right_logical(iota((combos, 128), 0), int(math.log2(group)))
    g_combo = jnp.sum(jnp.where(iota((combos, 128), 1) == pair_of, own, 0.0), axis=1, keepdims=True)
    g_pair = jnp.sum(
        jnp.where(iota((group, 128), 1) == iota((group, 128), 0), own, 0.0), axis=1, keepdims=True
    )
    head_rows = iota((group, width), 0) == lax.shift_right_logical(
        iota((group, width), 1), int(math.log2(width // heads))
    )
    queries = qf[...].astype(f32)
    upstream = gctx[...] * g_pair
    for p in range(count):
        at = slice(p * group, (p + 1) * group)
        right[0, at, :] = jnp.where(head_rows, queries[p : p + 1, :], 0.0).astype(bf16)
        right[1, at, :] = jnp.where(head_rows, upstream[p : p + 1, :], 0.0).astype(bf16)
    left[...] = (z[...] * g_combo).astype(bf16)
    term[0:width, :] = mm_tn(left[...], right[0])
    term[width : 2 * width, :] = mm_tn(vz[...], right[1])

    half, piece = keep.shape[0], keep.shape[1]
    blocks = width // piece
    mine = own_code(stages[: half.bit_length()])

    def piece_step(r, carry, target, base):
        owner = mine ^ (base + r)
        side = lax.shift_right_logical(owner, int(math.log2(blocks)))
        at = side * width + (owner & (blocks - 1)) * piece
        target[r] = term[pl.ds(pl.multiple_of(at, group), piece), :].astype(bf16)
        return carry

    lax.fori_loop(0, half, functools.partial(piece_step, target=send, base=half), 0)
    lax.fori_loop(0, half, functools.partial(piece_step, target=keep, base=0), 0)

    smalls[...] = jnp.zeros(smalls.shape, f32)
    smalls[0:1, :] = jnp.sum(a2[...] * g_pair, axis=0, keepdims=True)
    hats = jnp.sum(fhat[...] * g_pair, axis=0, keepdims=True)
    smalls[1:2, :] = hats * as_row(score_vector)
    smalls[2:3, :] = hats * as_row(final_gain)
    weighted = dl[...] * g_combo
    summed = weighted[0:group, :]
    for p in range(1, count):
        summed = summed + weighted[p * group : (p + 1) * group, :]
    spots = iota((window, width), 1)
    hot = jnp.where(bucket_of(iota((window, width), 0)) == (spots & (buckets - 1)), 1.0, 0.0)
    spread = lax.dot_general(
        summed, hot, (((1,), (0,)), ((), ())), precision=highest, preferred_element_type=f32
    )
    row_of = lax.shift_right_logical(iota((group, width), 1), int(math.log2(buckets)))
    smalls[3:4, :] = jnp.sum(
        jnp.where(row_of == iota((group, width), 0), spread, 0.0), axis=0, keepdims=True
    )


def terms_call(dims, pay, z, vz, qf, gctx, dl, a2, fhat, final_gain, score_vector):
    stages, docs, lists, list_count, count, heads, buckets = dims
    devices = docs * lists
    combos, width = z.shape
    pieces = 1 << len(cut_stages(stages, width))
    piece = 2 * width // pieces
    shape = jax.ShapeDtypeStruct
    half = shape((pieces // 2, piece, width), bf16)
    return pl.pallas_call(
        functools.partial(terms_kernel, dims),
        out_shape=[
            half, half,
            shape((devices, 128), f32),
            shape((8, 128), f32),
            shape((8, width), f32),
        ],
        in_specs=[whole] * 10,
        out_specs=[whole] * 5,
        scratch_shapes=[
            pltpu.VMEM((2 * width, width), f32),
            pltpu.VMEM((combos, width), bf16),
            pltpu.VMEM((2, combos, width), bf16),
        ],
        compiler_params=pltpu.CompilerParams(vmem_limit_bytes=10 * mega),
        cost_estimate=pl.CostEstimate(flops=int(4e9), bytes_accessed=int(1e7), transcendentals=0),
        name="terms",
    )(pay, z, vz, qf, gctx, dl, a2, fhat, final_gain, score_vector)


def attention_kernel(
    lengths, n1, tokens_in, table, wq, wk, wv, wo,
    out,
    tokens, q, k, v, ctx, bias, sem,
):
    rows, length, width = tokens.shape
    heads = table.shape[0]
    pairs = lengths.shape[1]
    load = pltpu.make_async_copy(tokens_in, tokens, sem)
    load.start()
    lanes = 4 * window
    vector = bias_vector(table[...], lanes, window)
    for h in range(heads):
        bias[h] = pltpu.roll(
            jnp.broadcast_to(vector[h : h + 1, :], (window, lanes)), 0, 1, stride=1, stride_axis=0
        )[:, : 3 * window]
    tiles = length // window
    half = iota((2 * window, window), 1) < (width // heads)
    left = half[:window]
    upper = iota((2 * window, window), 0) < window
    chosen = half == upper

    def segment(positions, ends):
        total = jnp.zeros(positions.shape, jnp.int32)
        for end in ends:
            total = total + jnp.where(positions >= end, 1, 0)
        return total

    for row in range(rows):
        ends = [at + size for at, size in starts_of(lengths, row, pairs)]
        for target, low in ((q, wq), (k, wk), (v, wv)):
            target[...] = mm(n1[row], low[...]).astype(bf16)
        for j in range(tiles):
            t0 = j * window
            k0 = max(j - 1, 0) * window
            k1 = min(j + 2, tiles) * window
            off = k0 - (t0 - window)
            span = k1 - k0
            seg_q = segment(t0 + iota((window, 1), 0), ends)
            seg_k = segment(k0 + iota((1, span), 1), ends)
            allowed = seg_q == seg_k
            for pair in range(heads // 2):
                cols = slice(pair * window, (pair + 1) * window)
                both = q[t0 : t0 + window, cols]
                stacked = jnp.concatenate([both, both], axis=0)
                stacked = jnp.where(chosen, stacked, jnp.zeros_like(stacked))
                raw = mm_nt(stacked, k[k0:k1, cols])
                probs, sums = [], []
                for side in range(2):
                    part = raw[side * window : (side + 1) * window]
                    part = part + bias[2 * pair + side, :, off : off + span]
                    part = jnp.where(allowed, part, negative)
                    peak = jnp.max(part, axis=-1, keepdims=True)
                    raised = jnp.exp(part - peak)
                    sums.append(jnp.sum(raised, axis=-1, keepdims=True))
                    probs.append(raised.astype(bf16))
                mixed = mm(jnp.concatenate(probs, axis=0), v[k0:k1, cols])
                ctx[t0 : t0 + window, cols] = jnp.where(
                    left, mixed[:window] / sums[0], mixed[window:] / sums[1]
                ).astype(bf16)
        if row == 0:
            load.wait()
        out[row] = tokens[row] + mm(ctx[...], wo[...])


def attention_call(lengths, n1, tokens, table, weights):
    rows, length, width = tokens.shape
    heads = table.shape[0]
    tall = pltpu.VMEM((length, width), bf16)
    return pl.pallas_call(
        attention_kernel,
        out_shape=jax.ShapeDtypeStruct(tokens.shape, f32),
        in_specs=[scalars, whole, outside, whole] + [whole] * 4,
        out_specs=whole,
        scratch_shapes=[pltpu.VMEM(tokens.shape, f32)]
        + [tall] * 4
        + [pltpu.VMEM((heads, window, 3 * window), f32), pltpu.SemaphoreType.DMA],
        compiler_params=pltpu.CompilerParams(vmem_limit_bytes=20 * mega),
        cost_estimate=pl.CostEstimate(
            flops=int(2e10), bytes_accessed=int(1e7), transcendentals=int(8e6)
        ),
        name="attention",
    )(lengths, n1, tokens, table, *weights)


def feed_kernel(row, attended, gain, wi, wf, held, out, normed, total, sem):
    length, width = total.shape
    tile, chunk = 256, 512
    x = attended[row]
    normed[...] = (x * rms_factor(x) * as_row(gain)).astype(bf16)
    total[...] = x

    def finish(t, c, ahead):
        total[t, :] += mm(gelu(ahead).astype(bf16), wf[c, :])

    last = None
    for c in range(wi.shape[1] // chunk):
        for t in range(length // tile):
            t_at, c_at = slice(t * tile, (t + 1) * tile), slice(c * chunk, (c + 1) * chunk)
            ahead = mm(normed[t_at, :], wi[:, c_at])
            if last is not None:
                finish(*last)
            last = (t_at, c_at, ahead)
    finish(*last)
    store = pltpu.make_async_copy(total, out.at[row], sem)
    store.start()
    store.wait()


def feed_call(row, attended, gain, wi, wf, held):
    rows, length, width = attended.shape
    extra = [] if held is None else [held]
    kernel = functools.partial(feed_kernel, row)
    if held is None:
        kernel = lambda a, g, i, f, *rest: feed_kernel(row, a, g, i, f, None, *rest)
    return pl.pallas_call(
        kernel,
        out_shape=jax.ShapeDtypeStruct(attended.shape, f32),
        in_specs=[whole] * 4 + [outside] * len(extra),
        out_specs=outside,
        input_output_aliases={4: 0} if extra else {},
        scratch_shapes=[
            pltpu.VMEM((length, width), bf16),
            pltpu.VMEM((length, width), f32),
            pltpu.SemaphoreType.DMA,
        ],
        compiler_params=pltpu.CompilerParams(vmem_limit_bytes=12 * mega),
        cost_estimate=pl.CostEstimate(
            flops=int(1e10), bytes_accessed=int(1e7), transcendentals=int(3e6)
        ),
        name=f"feed_{row}",
    )(attended, gain, wi, wf, *extra)


def tokens_grad_kernel(
    dims, lengths, tokens_in, g_own, probs, dl, yk, yv, yq, ga, gain,
    out, first_sum, tokens, spread, sems,
):
    rows, length, width, pairs = dims
    loads = [
        pltpu.make_async_copy(tokens_in.at[r], tokens.at[r], sems.at[r]) for r in range(rows)
    ]
    for load in loads:
        load.start()
    own = g_own[0:1, :]
    lane = iota((1, 128), 1)
    total = jnp.zeros((1, width), f32)
    stores = []
    for r in range(rows):
        spread[...] = jnp.zeros(spread.shape, f32)
        starts = starts_of(lengths, r, pairs)
        amounts = []
        for i, (at, size) in enumerate(starts):
            pair = r * pairs + i
            amount = jnp.sum(jnp.where(lane == pair, own, 0.0), axis=1, keepdims=True)
            amounts.append(amount)
            here = slice(pair * group, (pair + 1) * group)
            left = jnp.concatenate([dl[here, :], probs[here, :]], axis=0)
            right = jnp.concatenate([yk[here, :], yv[here, :]], axis=0)
            base = pl.multiple_of(at - (at & (group - 1)), group)
            spread[pl.ds(base, reach), :] += mm_tn(left, right)[:reach] * amount
        for i, (at, size) in enumerate(starts):
            pair = r * pairs + i
            spread[pl.ds(at, 1), :] += yq[pair : pair + 1, :] * amounts[i]
        loads[r].wait()
        gain_row = as_row(gain)

        def step(i, carry, r=r, gain_row=gain_row):
            at = pl.ds(pl.multiple_of(i * 64, 64), 64)
            x = tokens[r, at, :]
            factor = rms_factor(x)
            hat = x * factor
            upstream = spread[at, :]
            tokens[r, at, :] = norm_back(hat, factor, upstream * gain_row)
            return carry + jnp.sum(hat * upstream, axis=0, keepdims=True)

        total = lax.fori_loop(0, length // 64, step, total)
        for i, (at, size) in enumerate(starts):
            pair = r * pairs + i
            tokens[r, pl.ds(at, 1), :] += ga[pair : pair + 1, :] * amounts[i]
        store = pltpu.make_async_copy(tokens.at[r], out.at[r], sems.at[r])
        store.start()
        stores.append(store)
    first_sum[...] = total
    for store in stores:
        store.wait()


def tokens_grad_call(lengths, tokens, g_own, probs, dl, yk, yv, yq, ga, gain):
    rows, length, width = tokens.shape
    pairs = lengths.shape[1]
    return pl.pallas_call(
        functools.partial(tokens_grad_kernel, (rows, length, width, pairs)),
        out_shape=[
            jax.ShapeDtypeStruct(tokens.shape, f32),
            jax.ShapeDtypeStruct((1, width), f32),
        ],
        in_specs=[scalars, outside] + [whole] * 8,
        out_specs=[outside, whole],
        scratch_shapes=[
            pltpu.VMEM(tokens.shape, f32),
            pltpu.VMEM((length + reach, width), f32),
            pltpu.SemaphoreType.DMA((rows,)),
        ],
        compiler_params=pltpu.CompilerParams(vmem_limit_bytes=12 * mega),
        cost_estimate=pl.CostEstimate(flops=int(2e9), bytes_accessed=int(1e7), transcendentals=0),
        name="tokens_grad",
    )(lengths, tokens, g_own, probs, dl, yk, yv, yq, ga, gain)


def outer_kernel(dims, low_in, high_in, g_all, wi, wf, *rest):
    part, chunk, blocks = dims
    if part:
        rest = rest[2:]
    inner_out, outer_out = rest[0], rest[1]
    output_out, query_out = (None, None) if part else rest[2:4]
    factors, g, branch, inner, outer, flat, out_sems = rest[2 if part else 4 :][:7]
    width, hidden = wi.shape
    steps = hidden // chunk
    mine = range(part * steps // 2, (part + 1) * steps // 2)
    needed = (4, 5) if part else (4, 5, 0, 1, 2, 3)
    members = factors.shape[1] // 12
    main = members * 8
    span, half = 3 * width // 2, width // 2

    def scaled(i):
        return (factors[i].astype(f32) * g[...]).astype(bf16)

    def unpack(sources, b):
        near = iota((8, half), 0) < 4
        for i in needed:
            held = [
                source[d, :, i * span : (i + 1) * span].astype(f32)
                for source in sources
                for d in range(source.shape[0])
            ]
            for k in range(0, members, 2):
                even, odd = held[k], held[k + 1]
                factors[i, k * 8 : (k + 2) * 8, :] = jnp.concatenate(
                    [even[:, :width], odd[:, :width]], axis=0
                ).astype(bf16)
            for k in range(0, members, 4):
                tiles = []
                for j in (k, k + 2):
                    even, odd = held[j][:, width:], held[j + 1][:, width:]
                    tiles.append(
                        jnp.concatenate(
                            [
                                jnp.where(near, even, pltpu.roll(odd, 4, 0)),
                                jnp.where(near, pltpu.roll(even, 4, 0), odd),
                            ],
                            axis=1,
                        )
                    )
                at = main + k * 4
                factors[i, at : at + 16, :] = jnp.concatenate(tiles, axis=0).astype(bf16)
        same = iota((8, 128), 1) == iota((8, 128), 0)
        more = iota((8, 128), 1) == 8 + (iota((8, 128), 0) & 3)
        for d in range(members):
            here = g_all[pl.ds(b * members + d, 1), :]
            g[d * 8 : (d + 1) * 8, :] = jnp.sum(jnp.where(same, here, 0.0), axis=1, keepdims=True)
        for d in range(0, members, 2):
            both = jnp.where(
                iota((8, 128), 0) < 4,
                g_all[pl.ds(b * members + d, 1), :],
                g_all[pl.ds(b * members + d + 1, 1), :],
            )
            at = main + d * 4
            g[at : at + 8, :] = jnp.sum(jnp.where(more, both, 0.0), axis=1, keepdims=True)
        branch[...] = scaled(5)

    def put(target, values, b):
        if blocks == 1:
            target[...] = values
        else:
            target[...] = jnp.where(b == 0, values, target[...] + values)

    def each_block(one):
        if blocks == 1:
            one(0, 0)
        else:
            arrived, sem = rest[-2], rest[-1]

            def step(b, carry):
                for side, source in enumerate((low_in, high_in)):

                    @pl.when((b < blocks // 2) == (side == 0))
                    def _(side=side, source=source):
                        at = b - side * (blocks // 2)
                        load = pltpu.make_async_copy(
                            source.at[pl.ds(at * members, members)], arrived, sem
                        )
                        load.start()
                        load.wait()

                unpack([arrived], b)
                return one(b, carry)

            lax.fori_loop(0, blocks, step, 0)

    stores = {}

    def save(source, target, sem):
        store = pltpu.make_async_copy(source, target, out_sems.at[sem])
        store.start()
        stores[sem] = store

    if blocks == 1:
        unpack([low_in, high_in], 0)
    if not part:
        for i, j, slot, target in ((0, 1, 0, query_out), (2, 3, 1, output_out)):

            def square(b, carry, i=i, j=j, slot=slot):
                put(flat.at[slot], mm_tn(factors[i], scaled(j)), b)
                return carry

            each_block(square)
            save(flat.at[slot], target, 4 + slot)
    for c in mine:
        slot = c % 2
        at = slice(c * chunk, (c + 1) * chunk)

        def one(b, carry, slot=slot, at=at):
            value, slope = gelu_pair(mm(factors[4], wi[:, at]))
            grad = (mm_nt(branch[...], wf[at, :]) * slope).astype(bf16)
            put(inner.at[slot], mm_tn(factors[4], grad), b)
            put(outer.at[slot], mm_tn(value.astype(bf16), branch[...]), b)
            return carry

        each_block(one)
        save(inner.at[slot], inner_out.at[:, pl.ds(c * chunk, chunk)], slot)
        save(outer.at[slot], outer_out.at[pl.ds(c * chunk, chunk), :], 2 + slot)
    for store in stores.values():
        store.wait()


def outer_call(part, low, high, g_all, wi, wf, held):
    devices = 2 * low.shape[0]
    width, hidden = wi.shape
    chunk = hidden // 4
    members = min(devices, 32)
    blocks = devices // members
    block = members * 12
    shape = jax.ShapeDtypeStruct
    wide = [shape((width, hidden), f32), shape((hidden, width), f32)]
    flat = [shape((width, width), f32)] * 2
    place = whole if blocks == 1 else outside
    more = [] if blocks == 1 else [
        pltpu.VMEM((members,) + low.shape[1:], bf16), pltpu.SemaphoreType.DMA
    ]
    return pl.pallas_call(
        functools.partial(outer_kernel, (part, chunk, blocks)),
        out_shape=wide if part else wide + flat,
        in_specs=[place] * 2 + [whole] * 3 + [outside] * len(held),
        out_specs=[outside] * (2 if part else 4),
        input_output_aliases={5: 0, 6: 1} if part else {},
        scratch_shapes=[
            pltpu.VMEM((6, block, width), bf16),
            pltpu.VMEM((block, 1), f32),
            pltpu.VMEM((block, width), bf16),
            pltpu.VMEM((2, width, chunk), f32),
            pltpu.VMEM((2, chunk, width), f32),
            pltpu.VMEM((2, width, width), f32),
            pltpu.SemaphoreType.DMA((6,)),
        ] + more,
        compiler_params=pltpu.CompilerParams(vmem_limit_bytes=28 * mega),
        cost_estimate=pl.CostEstimate(
            flops=int(1e10), bytes_accessed=int(2e7), transcendentals=int(1e6)
        ),
        name=f"outer_{part}",
    )(low, high, g_all, wi, wf, *held)


def small_call(kernel, name, outs, *args):
    return pl.pallas_call(
        kernel,
        out_shape=outs,
        in_specs=[whole] * len(args),
        out_specs=[whole] * len(outs) if isinstance(outs, (list, tuple)) else whole,
        compiler_params=pltpu.CompilerParams(vmem_limit_bytes=8 * mega),
        cost_estimate=pl.CostEstimate(flops=1000, bytes_accessed=int(1e6), transcendentals=0),
        name=name,
    )(*args)


def join(mine, come):
    if mine.size > 1 << 21:
        return jnp.concatenate([mine, come], axis=0)

    def kernel(a, b, out):
        out[: a.shape[0]] = a[...]
        out[a.shape[0] :] = b[...]

    shape = (2 * mine.shape[0],) + mine.shape[1:]
    return small_call(kernel, "join", jax.ShapeDtypeStruct(shape, mine.dtype), mine, come)


def fold(keep, come):
    half = keep.shape[0] // 2

    def kernel(a, b, first, second):
        for i in range(half):
            first[i] = a[i] + b[i]
            second[i] = a[half + i] + b[half + i]

    out = jax.ShapeDtypeStruct((half,) + keep.shape[1:], keep.dtype)
    return small_call(kernel, "fold", [out, out], keep, come)


def close(keep, come, smalls, first_sum):
    rows = keep.shape[1]

    def kernel(a, b, c, d, out):
        out[0, :rows, :] = a[0] + b[0]
        low = jnp.where(iota(c.shape, 0) == 4, d[...], c[...])
        tail = jnp.concatenate([low, jnp.zeros_like(low)], axis=0)
        out[0, rows:, :] = tail.astype(bf16)

    out = jax.ShapeDtypeStruct((1, rows + group, keep.shape[2]), keep.dtype)
    return small_call(kernel, "close", out, keep, come, smalls, first_sum)


def add(mine, come):
    def kernel(a, b, out):
        out[...] = a[...] + b[...]

    return small_call(kernel, "add", jax.ShapeDtypeStruct(mine.shape, mine.dtype), mine, come)


def last_kernel(
    dims, low, high, key_out, value_out, first_out, second_out, final_out, vector_out, table_out
):
    stages, piece, heads = dims
    half, _, width = low.shape
    buckets = table_out.shape[0]
    me = own_code(stages)
    blocks = width // piece
    sides = (key_out, value_out)
    total = jnp.zeros((8, width), f32)
    for part, held in enumerate((low, high)):
        total = total + sum(held[i, piece:, :].astype(f32)[:8] for i in range(half))

        def step(i, carry, part=part, held=held):
            owner = me ^ (part * half + i)
            at = pl.multiple_of((owner & (blocks - 1)) * piece, group)
            values = held[i, :piece, :].astype(f32)
            for side in range(2):

                @pl.when(lax.shift_right_logical(owner, int(math.log2(blocks))) == side)
                def _(side=side):
                    sides[side][pl.ds(at, piece), :] = values

            return carry

        lax.fori_loop(0, half, step, 0)
    for i, out in enumerate((second_out, final_out, vector_out, None, first_out)):
        if out is not None:
            out[...] = total[i : i + 1, :].reshape(width)
    spots = iota((buckets, width), 1)
    by_bucket = jnp.where((spots & (buckets - 1)) == iota((buckets, width), 0), total[3:4, :], 0.0)
    by_head = jnp.where(
        lax.shift_right_logical(iota((width, 128), 0), int(math.log2(buckets))) == iota((width, 128), 1),
        1.0, 0.0,
    )
    table = lax.dot_general(
        by_bucket, by_head, (((1,), (0,)), ((), ())), precision=highest, preferred_element_type=f32
    )
    table_out[...] = table[:, :heads]


def last_call(stages, low, high, piece, buckets, heads):
    width = low.shape[2]
    shape = jax.ShapeDtypeStruct
    return pl.pallas_call(
        functools.partial(last_kernel, (stages, piece, heads)),
        out_shape=[shape((width, width), f32)] * 2
        + [shape((width,), f32)] * 4
        + [shape((buckets, heads), f32)],
        in_specs=[whole] * 2,
        out_specs=[whole] * 7,
        compiler_params=pltpu.CompilerParams(vmem_limit_bytes=12 * mega),
        cost_estimate=pl.CostEstimate(flops=int(1e7), bytes_accessed=int(1e7), transcendentals=0),
        name="last",
    )(low, high)


def shards(
    docs, lists,
    tokens, pair_lengths, list_ids, relevance,
    first_gain, query_weight, key_weight, value_weight, output_weight, bias_table,
    second_gain, inner_weight, outer_weight, final_gain, score_vector,
):
    row_count, length, width = tokens.shape[1:]
    pairs = pair_lengths.shape[2]
    buckets, heads = bias_table.shape
    devices = docs * lists
    sizes = {"docs": docs, "lists": lists}
    stages = tuple(("lists", 1 << b) for b in range(lists.bit_length() - 1)) + tuple(
        ("docs", 1 << b) for b in range(docs.bit_length() - 1)
    )

    def swap(values, stage):
        axis, mask = stage
        return lax.ppermute(values, axis, [(i, i ^ mask) for i in range(sizes[axis])])

    rows = tokens.reshape(row_count, length, width)
    lengths = pair_lengths.reshape(row_count, pairs)
    gains = (first_gain, second_gain, final_gain, score_vector)
    table = bias_table.T
    outs = path_call(
        rows, lengths, list_ids, relevance, gains, table,
        (query_weight, key_weight, value_weight, output_weight, inner_weight, outer_weight),
    )
    pay, factors, n1, probs, dl, turned, yk, yv, qf, gctx, z, vz, ga, a2, fhat, yq = outs[:16]
    wq, wk, wv, wo, wi, wf, scores = outs[16:]

    tie = lax.optimization_barrier
    gather_order = tuple(reversed(stages))

    rows_left = list(gather_order)
    come = None
    for i, stage in enumerate(gather_order):
        pay = join(pay, swap(pay, stage))
        if i == 0:
            factors, pay = tie((factors, pay))
            come = swap(factors, rows_left.pop(0))
        elif i == 2:
            come, pay = tie((come, pay))
            factors = join(factors, come)
            come = swap(factors, rows_left.pop(0))
    count = row_count * pairs
    dims = (stages, docs, lists, docs // 2, count, heads, buckets)
    keep, send, g_all, g_own, smalls = terms_call(
        dims, pay, z, vz, qf, gctx, turned, a2, fhat, gains[2], gains[3]
    )
    piece = keep.shape[1]
    cut = cut_stages(stages, width)
    rest = stages[len(cut) :]
    for stage in cut[:-2]:
        keep, send = fold(keep, swap(send, stage))

    come, send = tie((come, send))
    factors = join(factors, come)
    n1, send, factors = tie((n1, send, factors))
    arrived = swap(send, cut[-2])
    come = swap(factors, rows_left.pop(0))
    attended = attention_call(lengths, n1, rows, table, (wq, wk, wv, wo))
    arrived, come, attended = tie((arrived, come, attended))
    keep, send = fold(keep, arrived)
    factors = join(factors, come)

    probs, send, factors = tie((probs, send, factors))
    arrived = swap(send, cut[-1])
    come = swap(factors, rows_left.pop(0))
    grads, first_sum = tokens_grad_call(
        lengths, rows, g_own, probs, dl, yk, yv, yq, ga, gains[0]
    )
    arrived, grads, first_sum = tie((arrived, grads, first_sum))
    held = close(keep, arrived, smalls, first_sum)

    encoded = None
    for i, stage in enumerate(rest):
        if i == len(rest) - 2:
            attended, held = tie((attended, held))
            arrived = swap(held, stage)
            encoded = feed_call(0, attended, gains[1], wi, wf, None)
            arrived, encoded = tie((arrived, encoded))
        elif i == len(rest) - 1:
            come, held, encoded = tie((come, held, encoded))
            arrived = swap(held, stage)
            while True:
                factors, last_come = join(factors, come), None
                last_come = swap(factors, rows_left.pop(0))
                if not rows_left:
                    break
                come = last_come
            encoded = feed_call(1, attended, gains[1], wi, wf, encoded)
            arrived, encoded, last_come = tie((arrived, encoded, last_come))
        else:
            arrived = swap(held, stage)
        held = add(held, arrived)

    wide = ()
    for i, stage in reversed(tuple(enumerate(cut))):
        if i == len(cut) - 1:
            held, last_come = tie((held, last_come))
            come = swap(held, stage)
            outs = outer_call(0, factors, last_come, g_all, wi, wf, ())
            wide, (output_grad, query_grad) = tuple(outs[:2]), outs[2:]
            wide, come = tie((wide, come))
        elif i == len(cut) - 2:
            wide, held = tie((wide, held))
            come = swap(held, stage)
            wide = tuple(outer_call(1, factors, last_come, g_all, wi, wf, wide))
            wide, come = tie((wide, come))
        else:
            come = swap(held, stage)
        if i:
            held = join(held, come)
    inner_grad, outer_grad = wide
    key_grad, value_grad, first_grad, second_grad, final_grad, vector_grad, table_grad = last_call(
        cut, held, come, piece, buckets, heads
    )
    return (
        encoded.reshape(tokens.shape),
        scores.reshape(1, row_count, pairs),
        grads.reshape(tokens.shape),
        first_grad,
        query_grad,
        key_grad,
        value_grad,
        output_grad,
        table_grad,
        second_grad,
        inner_grad,
        outer_grad,
        final_grad,
        vector_grad,
    )


def solution(mesh):
    placed = P("lists", "docs", None, None)
    return jax.shard_map(
        functools.partial(shards, mesh.shape["docs"], mesh.shape["lists"]),
        mesh=mesh,
        in_specs=(placed, P("lists", "docs", None), P("lists", None), P("lists", None)) + (P(),) * 11,
        out_specs=(placed, P("lists", "docs", None), placed) + (P(),) * 11,
        check_vma=False,
    )
```

```python
import functools
import math

import jax
import jax.numpy as jnp
from jax import lax
from jax.experimental import pallas as pl
from jax.experimental.pallas import tpu as pltpu
from jax.sharding import PartitionSpec as P

epsilon = 1e-06
negative = -1000000000.0
highest = lax.Precision.HIGHEST
limits = (12, 16, 23, 32, 46, 64, 91)
f32 = jnp.float32
bf16 = jnp.bfloat16
window = 128
reach = 144
lanes_path = 256
group = 16
mega = 1 << 20
curve = math.sqrt(2.0 / math.pi)
cubic = 0.044715
whole = pl.BlockSpec(memory_space=pltpu.VMEM)
scalars = pl.BlockSpec(memory_space=pltpu.SMEM)
outside = pl.BlockSpec(memory_space=pl.ANY)


def mm(a, b):
    return lax.dot_general(a, b, (((1,), (0,)), ((), ())), preferred_element_type=f32)


def mm_nt(a, b):
    return lax.dot_general(a, b, (((1,), (1,)), ((), ())), preferred_element_type=f32)


def mm_tn(a, b):
    return lax.dot_general(a, b, (((0,), (0,)), ((), ())), preferred_element_type=f32)


def as_row(gains, i):
    return gains[i : i + 1, :]


def iota(shape, axis):
    return lax.broadcasted_iota(jnp.int32, shape, axis)


def bucket_of(offsets):
    upper_half = jnp.where(offsets > 0, 16, 0)
    distance = jnp.abs(offsets)
    beyond = jnp.full(offsets.shape, 8, jnp.int32)
    for border in limits:
        beyond = beyond + jnp.where(distance >= border, 1, 0)
    return upper_half + jnp.where(distance < 8, distance, beyond)


def rms_factor(values):
    return lax.rsqrt(jnp.mean(values * values, axis=-1, keepdims=True) + epsilon)


def norm_back(normed, factor, upstream):
    return factor * (upstream - normed * jnp.mean(upstream * normed, axis=-1, keepdims=True))


def half_bent(values, square):
    return 0.5 * jnp.tanh(values * (square * (curve * cubic) + curve)) + 0.5


def gelu(values):
    return values * half_bent(values, values * values)


def gelu_pair(values):
    square = values * values
    half = half_bent(values, square)
    value = half * values
    steep = (value - value * half) * (square * (6.0 * curve * cubic) + 2.0 * curve)
    return value, half + steep


def bias_vector(table, lanes, origin):
    buckets = table.shape[1]
    buckets_at = bucket_of(iota((buckets, lanes), 1) - origin)
    chosen = jnp.where(buckets_at == iota((buckets, lanes), 0), 1.0, 0.0)
    return lax.dot_general(
        table, chosen, (((1,), (0,)), ((), ())), precision=highest, preferred_element_type=f32
    )


def cast_rows(target, source, chunk):
    rows = source.shape[0]

    def step(i, carry):
        at = pl.ds(pl.multiple_of(i * chunk, chunk), chunk)
        target[at, :] = source[at, :].astype(bf16)
        return carry

    lax.fori_loop(0, rows // chunk, step, 0)


def starts_of(lengths, row, count):
    out, at = [], 0
    for i in range(count):
        out.append((at, lengths[row, i]))
        at = at + lengths[row, i]
    return out


def path_kernel(
    dims,
    lengths, known,
    tokens_in, gains,
    wq_in, wk_in, wv_in, wo_in, wi_in, wf_in,
    pay, factors, n1_out, probs_out, dl_out, turned_out, yk_out, yv_out, qf_out, gctx_out, z_out, vz_out,
    ga_out, a2_out, fhat_out, yq_out,
    wq, wk, wv, wo, wi, wf, scores_out,
    tokens, square, padded, first, gather_z, logits, expand, wide_z,
    in_sems, tokens_sem,
):
    rows, length, width, pairs, heads, buckets = dims
    members = known.shape[1] // 2
    count = rows * pairs
    parts = wi.shape[1] // width
    slots = square.shape[0]
    chunks = [(wq_in, wq), (wk_in, wk), (wv_in, wv), (wo_in, wo)]
    for i in range(parts):
        at = pl.ds(i * width, width)
        chunks.append((wi_in.at[:, at], wi.at[:, at]))
    for i in range(parts):
        at = pl.ds(i * width, width)
        chunks.append((wf_in.at[at, :], wf.at[at, :]))

    def load_of(i):
        return pltpu.make_async_copy(chunks[i][0], square.at[i % slots], in_sems.at[i % slots])

    tokens_load = pltpu.make_async_copy(tokens_in, tokens, tokens_sem)
    tokens_load.start()
    order = iter(range(slots))

    def request(count):
        for _ in range(count):
            load_of(next(order)).start()

    request(2)
    tokens_load.wait()
    request(2)

    gain = as_row(gains, 0)
    for r in range(rows):
        padded[r, length:, :] = jnp.zeros((reach, width), bf16)

        def norm_step(i, carry, r=r):
            at = pl.ds(pl.multiple_of(i * 64, 64), 64)
            x = tokens[r, at, :]
            n = (x * rms_factor(x) * gain).astype(bf16)
            n1_out[r, at, :] = n
            padded[r, at, :] = n
            return carry

        lax.fori_loop(0, length // 64, norm_step, 0)
        request(2)
    first[...] = jnp.zeros(first.shape, f32)
    pieces = []
    for r in range(rows):
        for at, size in starts_of(lengths, r, pairs):
            p = len(pieces)
            shift = at & (group - 1)
            pieces.append((r, pl.multiple_of(at - shift, group), shift, size))
            first[p : p + 1, :] = tokens[r, pl.ds(at, 1), :]

    def nearby(p):
        r, base, _, _ = pieces[p]
        return padded[r, pl.ds(base, reach), :]

    spots = [slice(p * group, (p + 1) * group) for p in range(count)]
    head_rows = iota((group, width), 0) == lax.shift_right_logical(
        iota((group, width), 1), int(math.log2(width // heads))
    )

    def widen(values):
        for p in range(count):
            expand[p * group : (p + 1) * group, :] = jnp.where(
                head_rows, values[p : p + 1, :], 0.0
            ).astype(bf16)

    def narrow(target):
        target[...] = jnp.zeros(target.shape, f32)
        for p in range(count):
            block = wide_z[p * group : (p + 1) * group, :]
            target[p : p + 1, :] = jnp.sum(
                jnp.where(head_rows, block, 0.0), axis=0, keepdims=True
            )

    def take(i):
        load_of(i).wait()
        cast_rows(chunks[i][1], square.at[i % slots], 64)
        if i < 4:
            request(1)

    take(0)
    n1_first = (first[...] * rms_factor(first[...]) * gain).astype(bf16)
    q_first = mm(n1_first, wq[...]).astype(bf16)
    qf_out[...] = q_first
    widen(q_first.astype(f32))
    take(1)
    yk_out[...] = mm_nt(expand[...], wk[...]).astype(bf16)
    position = bias_vector(gains[4 : 4 + heads, :buckets], lanes_path, 0)
    position = jnp.concatenate([position, jnp.zeros((group - heads, lanes_path), f32)], axis=0)
    lane = iota((group, lanes_path), 1)
    for p, (_, _, shift, size) in enumerate(pieces):
        logits[spots[p], :reach] = mm_nt(yk_out[spots[p], :], nearby(p))
        block = logits[spots[p], :] + pltpu.roll(position, shift, 1)
        inside = jnp.logical_and(lane >= shift, lane < shift + size)
        logits[spots[p], :] = jnp.where(inside, block, negative)
    take(2)
    take(3)
    scores_in = logits[...]
    peak = jnp.max(scores_in, axis=-1, keepdims=True)
    raised = jnp.exp(scores_in - peak)
    probs = raised / jnp.sum(raised, axis=-1, keepdims=True)
    probs_out[...] = probs.astype(bf16)
    for p in range(count):
        vz_out[spots[p], :] = mm(probs_out[spots[p], :reach], nearby(p)).astype(bf16)
    wide_z[...] = mm(vz_out[...], wv[...])
    narrow(gather_z)
    context = gather_z[...].astype(bf16)
    attended = first[...] + mm(context, wo[...])
    scale_two = rms_factor(attended)
    second = attended * scale_two
    normed_two = (second * as_row(gains, 1)).astype(bf16)
    for i in range(parts):
        take(4 + i)
    value, slope = gelu_pair(mm(normed_two, wi[...]))
    for i in range(parts):
        take(4 + parts + i)
    encoded = attended + mm(value.astype(bf16), wf[...])
    scale_final = rms_factor(encoded)
    final_hat = encoded * scale_final
    fhat_out[...] = final_hat
    unit = as_row(gains, 3) * as_row(gains, 2)
    score_col = jnp.sum(final_hat * unit, axis=-1, keepdims=True)
    square_lane = iota((group, 128), 1)
    row = jnp.sum(
        jnp.where(square_lane == iota((group, 128), 0), score_col, 0.0), axis=0, keepdims=True
    )
    for r in range(rows):
        scores_out[r : r + 1, :] = row[:, r * pairs : (r + 1) * pairs]
    row_lane = iota((1, 128), 1)
    place = lax.axis_index("docs") * count
    for i in range(count):
        row = jnp.where(row_lane == group + i, known[0, place + i].astype(f32), row)
        row = jnp.where(row_lane == 2 * group + i, known[0, members + place + i].astype(f32), row)
    pay[...] = row

    grad_encoded = norm_back(final_hat, scale_final, jnp.broadcast_to(unit, final_hat.shape))
    grad_branch = grad_encoded.astype(bf16)
    grad_preact = (mm_nt(grad_branch, wf[...]) * slope).astype(bf16)
    grad_normed_two = mm_nt(grad_preact, wi[...])
    a2_out[...] = second * grad_normed_two
    grad_attended = grad_encoded + norm_back(second, scale_two, grad_normed_two * as_row(gains, 1))
    ga_out[...] = grad_attended
    grad_attn = grad_attended.astype(bf16)
    grad_context = mm_nt(grad_attn, wo[...])
    gctx_out[...] = grad_context
    widen(grad_context)
    yv_out[...] = mm_nt(expand[...], wv[...]).astype(bf16)
    logits[...] = jnp.zeros(logits.shape, f32)
    for p in range(count):
        logits[spots[p], :reach] = mm_nt(yv_out[spots[p], :], nearby(p))
    grad_probs = logits[...]
    grad_logits = probs * (grad_probs - jnp.sum(probs * grad_probs, axis=-1, keepdims=True))
    dl_out[...] = grad_logits.astype(bf16)
    for p, (_, _, shift, _) in enumerate(pieces):
        rounded = dl_out[spots[p], :]
        z_out[spots[p], :] = mm(rounded[:, :reach], nearby(p))
        turned = pltpu.roll(rounded.astype(f32), (lanes_path - shift) & (lanes_path - 1), 1)
        turned_out[spots[p], :] = turned[:, :window]
    wide_z[...] = mm(z_out[...].astype(bf16), wk[...])
    narrow(gather_z)
    grad_query = gather_z[...].astype(bf16)
    yq_out[...] = mm_nt(grad_query, wq[...])
    span, half = 3 * width // 2, width // 2
    for i, member in enumerate((n1_first, grad_query, context, grad_attn, normed_two, grad_branch)):
        member = member.astype(f32)
        tail = member[8:, :]
        tail = jnp.where(
            iota((8, half), 0) < 4, tail[:, :half], pltpu.roll(tail[:, half:], 4, 0)
        )
        factors[0, :, i * span : i * span + width] = member[:8].astype(bf16)
        factors[0, :, i * span + width : (i + 1) * span] = tail.astype(bf16)


def path_call(tokens, lengths, known, gains, heads, buckets, weights):
    rows, length, width = tokens.shape
    pairs = lengths.shape[1]
    combos = rows * pairs * group
    shape = jax.ShapeDtypeStruct
    outs = [
        shape((1, 128), f32),
        shape((1, 8, 9 * width), bf16),
        shape((rows, length, width), bf16),
        shape((combos, lanes_path), bf16),
        shape((combos, lanes_path), bf16),
        shape((combos, window), f32),
        shape((combos, width), bf16),
        shape((combos, width), bf16),
        shape((group, width), bf16),
        shape((group, width), f32),
        shape((combos, width), f32),
        shape((combos, width), bf16),
        shape((group, width), f32),
        shape((group, width), f32),
        shape((group, width), f32),
        shape((group, width), f32),
    ]
    low = [shape(w.shape, bf16) for w in weights] + [shape((rows, pairs), f32)]
    return pl.pallas_call(
        functools.partial(path_kernel, (rows, length, width, pairs, heads, buckets)),
        out_shape=outs + low,
        in_specs=[scalars] * 2 + [outside, whole] + [outside] * 6,
        out_specs=[whole] * (len(outs) + len(low)),
        scratch_shapes=[
            pltpu.VMEM(tokens.shape, f32),
            pltpu.VMEM((12, width, width), f32),
            pltpu.VMEM((rows, length + reach, width), bf16),
            pltpu.VMEM((group, width), f32),
            pltpu.VMEM((group, width), f32),
            pltpu.VMEM((combos, lanes_path), f32),
            pltpu.VMEM((combos, width), bf16),
            pltpu.VMEM((combos, width), f32),
            pltpu.SemaphoreType.DMA((12,)),
            pltpu.SemaphoreType.DMA,
        ],
        compiler_params=pltpu.CompilerParams(vmem_limit_bytes=45 * mega),
        cost_estimate=pl.CostEstimate(flops=int(9e9), bytes_accessed=int(5e7), transcendentals=0),
        name="path",
    )(lengths, known, tokens, gains, *weights)


def code_of(stages, indices):
    total = len(stages)
    code = 0
    for s, (axis, mask) in enumerate(stages):
        bit = jnp.where((indices[axis] & mask) != 0, 1, 0) if not isinstance(
            indices[axis], int
        ) else (1 if indices[axis] & mask else 0)
        code = code + bit * (1 << (total - 1 - s))
    return code


def cut_stages(stages, width):
    count = 3 + sum(axis == "lists" for axis, _ in stages)
    while (2 * width) % (group << count):
        count -= 1
    return stages[:count]


def own_code(stages):
    return code_of(stages, {axis: lax.axis_index(axis) for axis in ("docs", "lists")})


def terms_kernel(
    dims,
    pay, z, vz, qf, gctx, dl, a2, fhat, gains,
    keep, send, g_all, g_own, smalls,
    term, left, right,
):
    stages, docs, lists, list_count, count, heads, buckets = dims
    width = z.shape[1]
    everything = pay[...]
    lane = iota(everything.shape, 1)
    score = everything
    names = pltpu.roll(everything, 128 - group, 1)
    label = pltpu.roll(everything, 128 - 2 * group, 1)
    used = lane < count
    part = lax.shift_right_logical(iota(everything.shape, 0), int(math.log2(docs)))
    key = jnp.where(used, part * list_count + names.astype(jnp.int32), -1)

    def total_of(values):
        return jnp.sum(jnp.sum(values, axis=1, keepdims=True), axis=0, keepdims=True)

    def top_step(k, top):
        member = key == k
        best = jnp.max(
            jnp.max(jnp.where(member, score, negative), axis=1, keepdims=True),
            axis=0, keepdims=True,
        )
        return jnp.where(member, best, top)

    keys = lists * list_count
    unroll = keys if keys <= 16 else 4
    top = lax.fori_loop(0, keys, top_step, score, unroll=unroll)
    raised = jnp.exp(score - top)

    def sum_step(k, carry):
        total, gain = carry
        member = key == k
        return (
            jnp.where(member, total_of(jnp.where(member, raised, 0.0)), total),
            jnp.where(member, total_of(jnp.where(member, label, 0.0)), gain),
        )

    ones = jnp.ones(everything.shape, f32)
    total, gain = lax.fori_loop(0, keys, sum_step, (ones, ones), unroll=unroll)
    grads = jnp.where(used, raised / total * gain - label, 0.0)
    g_all[...] = grads
    own = grads[0:1, :]
    g_own[...] = jnp.broadcast_to(own, g_own.shape)

    combos = count * group
    pair_of = lax.shift_right_logical(iota((combos, 128), 0), int(math.log2(group)))
    g_combo = jnp.sum(jnp.where(iota((combos, 128), 1) == pair_of, own, 0.0), axis=1, keepdims=True)
    g_pair = jnp.sum(
        jnp.where(iota((group, 128), 1) == iota((group, 128), 0), own, 0.0), axis=1, keepdims=True
    )
    head_rows = iota((group, width), 0) == lax.shift_right_logical(
        iota((group, width), 1), int(math.log2(width // heads))
    )
    queries = qf[...].astype(f32)
    upstream = gctx[...] * g_pair
    for p in range(count):
        at = slice(p * group, (p + 1) * group)
        right[0, at, :] = jnp.where(head_rows, queries[p : p + 1, :], 0.0).astype(bf16)
        right[1, at, :] = jnp.where(head_rows, upstream[p : p + 1, :], 0.0).astype(bf16)
    left[...] = (z[...] * g_combo).astype(bf16)
    term[0:width, :] = mm_tn(left[...], right[0])
    term[width : 2 * width, :] = mm_tn(vz[...], right[1])

    half, piece = keep.shape[0], keep.shape[1]
    blocks = width // piece
    mine = own_code(stages[: half.bit_length()])

    def piece_step(r, carry, target, base):
        owner = mine ^ (base + r)
        side = lax.shift_right_logical(owner, int(math.log2(blocks)))
        at = side * width + (owner & (blocks - 1)) * piece
        target[r] = term[pl.ds(pl.multiple_of(at, group), piece), :].astype(bf16)
        return carry

    lax.fori_loop(0, half, functools.partial(piece_step, target=send, base=half), 0)
    lax.fori_loop(0, half, functools.partial(piece_step, target=keep, base=0), 0)

    smalls[...] = jnp.zeros(smalls.shape, f32)
    smalls[0:1, :] = jnp.sum(a2[...] * g_pair, axis=0, keepdims=True)
    hats = jnp.sum(fhat[...] * g_pair, axis=0, keepdims=True)
    smalls[1:2, :] = hats * as_row(gains, 3)
    smalls[2:3, :] = hats * as_row(gains, 2)
    weighted = dl[...] * g_combo
    summed = weighted[0:group, :]
    for p in range(1, count):
        summed = summed + weighted[p * group : (p + 1) * group, :]
    spots = iota((window, width), 1)
    hot = jnp.where(bucket_of(iota((window, width), 0)) == (spots & (buckets - 1)), 1.0, 0.0)
    spread = lax.dot_general(
        summed, hot, (((1,), (0,)), ((), ())), precision=highest, preferred_element_type=f32
    )
    row_of = lax.shift_right_logical(iota((group, width), 1), int(math.log2(buckets)))
    smalls[3:4, :] = jnp.sum(
        jnp.where(row_of == iota((group, width), 0), spread, 0.0), axis=0, keepdims=True
    )


def terms_call(dims, pay, z, vz, qf, gctx, dl, a2, fhat, gains):
    stages, docs, lists, list_count, count, heads, buckets = dims
    devices = docs * lists
    combos, width = z.shape
    pieces = 1 << len(cut_stages(stages, width))
    piece = 2 * width // pieces
    shape = jax.ShapeDtypeStruct
    half = shape((pieces // 2, piece, width), bf16)
    return pl.pallas_call(
        functools.partial(terms_kernel, dims),
        out_shape=[
            half, half,
            shape((devices, 128), f32),
            shape((8, 128), f32),
            shape((8, width), f32),
        ],
        in_specs=[whole] * 9,
        out_specs=[whole] * 5,
        scratch_shapes=[
            pltpu.VMEM((2 * width, width), f32),
            pltpu.VMEM((combos, width), bf16),
            pltpu.VMEM((2, combos, width), bf16),
        ],
        compiler_params=pltpu.CompilerParams(vmem_limit_bytes=10 * mega),
        cost_estimate=pl.CostEstimate(flops=int(4e9), bytes_accessed=int(1e7), transcendentals=0),
        name="terms",
    )(pay, z, vz, qf, gctx, dl, a2, fhat, gains)


def attention_kernel(
    dims, lengths, n1, tokens_in, gains, wq, wk, wv, wo,
    out,
    tokens, q, k, v, ctx, qseg, kseg, bias, sem,
):
    rows, length, width = tokens.shape
    heads, buckets = dims
    pairs = lengths.shape[1]
    load = pltpu.make_async_copy(tokens_in, tokens, sem)
    load.start()
    lanes = 4 * window
    vector = bias_vector(gains[4 : 4 + heads, :buckets], lanes, window)
    for h in range(heads):
        bias[h] = pltpu.roll(
            jnp.broadcast_to(vector[h : h + 1, :], (window, lanes)), 0, 1, stride=1, stride_axis=0
        )[:, : 3 * window]
    tiles = length // window
    half = iota((2 * window, window), 1) < (width // heads)
    left = half[:window]
    upper = iota((2 * window, window), 0) < window
    chosen = half == upper

    def segment(positions, ends):
        total = jnp.zeros(positions.shape, jnp.int32)
        for end in ends:
            total = total + jnp.where(positions >= end, 1, 0)
        return total

    wide = iota((length, window), 1)
    units = []
    for row in range(rows):
        for j in range(tiles):
            for pair in range(heads // 2):
                units.append((row, j, pair))
    ones = jnp.ones((3 * window, window), bf16)

    def begin(row):
        ends = [at + size for at, size in starts_of(lengths, row, pairs)]
        seg = segment(iota((length, 1), 0), ends)
        qseg[...] = jnp.where(seg == wide, 1.0, 0.0).astype(bf16)
        kseg[...] = jnp.where(jnp.logical_and(seg != wide, wide <= pairs), negative, 0.0).astype(bf16)
        for target, low in ((q, wq), (k, wk), (v, wv)):
            target[...] = mm(n1[row], low[...]).astype(bf16)

    def spans(j):
        t0 = j * window
        k0 = max(j - 1, 0) * window
        k1 = min(j + 2, tiles) * window
        return t0, k0, k1

    def raw_of(row, j, pair):
        t0, k0, k1 = spans(j)
        cols = slice(pair * window, (pair + 1) * window)
        both = q[t0 : t0 + window, cols]
        stacked = jnp.concatenate([both, both], axis=0)
        stacked = jnp.where(chosen, stacked, jnp.zeros_like(stacked))
        mark = qseg[t0 : t0 + window, :]
        return mm_nt(
            jnp.concatenate([stacked, jnp.concatenate([mark, mark], axis=0)], axis=1),
            jnp.concatenate([k[k0:k1, cols], kseg[k0:k1, :]], axis=1),
        )

    def finish(row, j, pair, raw):
        t0, k0, k1 = spans(j)
        off = k0 - (t0 - window)
        cols = slice(pair * window, (pair + 1) * window)
        probs = []
        for side in range(2):
            part = raw[side * window : (side + 1) * window]
            part = part + bias[2 * pair + side, :, off : off + k1 - k0]
            peak = jnp.max(part, axis=-1, keepdims=True)
            probs.append(jnp.exp(part - peak).astype(bf16))
        mixed = mm(
            jnp.concatenate(probs, axis=0),
            jnp.concatenate([v[k0:k1, cols], ones[: k1 - k0]], axis=1),
        )
        ctx[t0 : t0 + window, cols] = jnp.where(
            left,
            mixed[:window, :window] / mixed[:window, window:],
            mixed[window:, :window] / mixed[window:, window:],
        ).astype(bf16)

    def close_row(row):
        if row == 0:
            load.wait()
        out[row] = tokens[row] + mm(ctx[...], wo[...])

    for row in range(rows):
        begin(row)
        last = None
        for unit in units:
            if unit[0] != row:
                continue
            raw = raw_of(*unit)
            if last is not None:
                finish(*last)
            last = unit + (raw,)
        finish(*last)
        close_row(row)


def attention_call(dims, lengths, n1, tokens, gains, weights):
    rows, length, width = tokens.shape
    heads = dims[0]
    tall = pltpu.VMEM((length, width), bf16)
    return pl.pallas_call(
        functools.partial(attention_kernel, dims),
        out_shape=jax.ShapeDtypeStruct(tokens.shape, f32),
        in_specs=[scalars, whole, outside, whole] + [whole] * 4,
        out_specs=whole,
        scratch_shapes=[pltpu.VMEM(tokens.shape, f32)]
        + [tall] * 4
        + [pltpu.VMEM((length, window), bf16)] * 2
        + [pltpu.VMEM((heads, window, 3 * window), f32), pltpu.SemaphoreType.DMA],
        compiler_params=pltpu.CompilerParams(vmem_limit_bytes=20 * mega),
        cost_estimate=pl.CostEstimate(
            flops=int(2e10), bytes_accessed=int(1e7), transcendentals=int(8e6)
        ),
        name="attention",
    )(lengths, n1, tokens, gains, *weights)


def feed_kernel(row, attended, gains, wi, wf, held, out, normed, total, sem):
    length, width = total.shape
    tile, chunk = 256, 512
    x = attended[row]
    normed[...] = (x * rms_factor(x) * as_row(gains, 1)).astype(bf16)
    total[...] = x

    def finish(t, c, ahead):
        total[t, :] += mm(gelu(ahead).astype(bf16), wf[c, :])

    last = None
    for c in range(wi.shape[1] // chunk):
        for t in range(length // tile):
            t_at, c_at = slice(t * tile, (t + 1) * tile), slice(c * chunk, (c + 1) * chunk)
            ahead = mm(normed[t_at, :], wi[:, c_at])
            if last is not None:
                finish(*last)
            last = (t_at, c_at, ahead)
    finish(*last)
    store = pltpu.make_async_copy(total, out.at[row], sem)
    store.start()
    store.wait()


def feed_call(row, attended, gain, wi, wf, held):
    rows, length, width = attended.shape
    extra = [] if held is None else [held]
    kernel = functools.partial(feed_kernel, row)
    if held is None:
        kernel = lambda a, g, i, f, *rest: feed_kernel(row, a, g, i, f, None, *rest)
    return pl.pallas_call(
        kernel,
        out_shape=jax.ShapeDtypeStruct(attended.shape, f32),
        in_specs=[whole] * 4 + [outside] * len(extra),
        out_specs=outside,
        input_output_aliases={4: 0} if extra else {},
        scratch_shapes=[
            pltpu.VMEM((length, width), bf16),
            pltpu.VMEM((length, width), f32),
            pltpu.SemaphoreType.DMA,
        ],
        compiler_params=pltpu.CompilerParams(vmem_limit_bytes=12 * mega),
        cost_estimate=pl.CostEstimate(
            flops=int(1e10), bytes_accessed=int(1e7), transcendentals=int(3e6)
        ),
        name=f"feed_{row}",
    )(attended, gain, wi, wf, *extra)


def tokens_grad_kernel(
    dims, lengths, tokens_in, g_own, probs, dl, yk, yv, yq, ga, gains,
    out, first_sum, tokens, spread, sems,
):
    rows, length, width, pairs = dims
    loads = [
        pltpu.make_async_copy(tokens_in.at[r], tokens.at[r], sems.at[r]) for r in range(rows)
    ]
    for load in loads:
        load.start()
    own = g_own[0:1, :]
    lane = iota((1, 128), 1)
    total = jnp.zeros((1, width), f32)
    stores = []
    for r in range(rows):
        spread[...] = jnp.zeros(spread.shape, f32)
        starts = starts_of(lengths, r, pairs)
        amounts = []
        for i, (at, size) in enumerate(starts):
            pair = r * pairs + i
            amount = jnp.sum(jnp.where(lane == pair, own, 0.0), axis=1, keepdims=True)
            amounts.append(amount)
            here = slice(pair * group, (pair + 1) * group)
            left = jnp.concatenate([dl[here, :], probs[here, :]], axis=0)
            right = jnp.concatenate([yk[here, :], yv[here, :]], axis=0)
            base = pl.multiple_of(at - (at & (group - 1)), group)
            spread[pl.ds(base, reach), :] += mm_tn(left, right)[:reach] * amount
        for i, (at, size) in enumerate(starts):
            pair = r * pairs + i
            spread[pl.ds(at, 1), :] += yq[pair : pair + 1, :] * amounts[i]
        loads[r].wait()
        gain_row = as_row(gains, 0)

        def step(i, carry, r=r, gain_row=gain_row):
            at = pl.ds(pl.multiple_of(i * 64, 64), 64)
            x = tokens[r, at, :]
            factor = rms_factor(x)
            hat = x * factor
            upstream = spread[at, :]
            tokens[r, at, :] = norm_back(hat, factor, upstream * gain_row)
            return carry + jnp.sum(hat * upstream, axis=0, keepdims=True)

        total = lax.fori_loop(0, length // 64, step, total)
        for i, (at, size) in enumerate(starts):
            pair = r * pairs + i
            tokens[r, pl.ds(at, 1), :] += ga[pair : pair + 1, :] * amounts[i]
        store = pltpu.make_async_copy(tokens.at[r], out.at[r], sems.at[r])
        store.start()
        stores.append(store)
    first_sum[...] = total
    for store in stores:
        store.wait()


def tokens_grad_call(lengths, tokens, g_own, probs, dl, yk, yv, yq, ga, gain):
    rows, length, width = tokens.shape
    pairs = lengths.shape[1]
    return pl.pallas_call(
        functools.partial(tokens_grad_kernel, (rows, length, width, pairs)),
        out_shape=[
            jax.ShapeDtypeStruct(tokens.shape, f32),
            jax.ShapeDtypeStruct((1, width), f32),
        ],
        in_specs=[scalars, outside] + [whole] * 8,
        out_specs=[outside, whole],
        scratch_shapes=[
            pltpu.VMEM(tokens.shape, f32),
            pltpu.VMEM((length + reach, width), f32),
            pltpu.SemaphoreType.DMA((rows,)),
        ],
        compiler_params=pltpu.CompilerParams(vmem_limit_bytes=12 * mega),
        cost_estimate=pl.CostEstimate(flops=int(2e9), bytes_accessed=int(1e7), transcendentals=0),
        name="tokens_grad",
    )(lengths, tokens, g_own, probs, dl, yk, yv, yq, ga, gain)


def outer_kernel(dims, low_in, high_in, g_all, wi, wf, *rest):
    part, chunk, blocks = dims
    if part == 2:
        rest = rest[2:]
    factors, g, branch, inner, outer, flat, out_sems = rest[2:9]
    width, hidden = wi.shape
    steps = hidden // chunk
    mine = range((part - 1) * steps // 2, part * steps // 2) if part else ()
    needed = (4, 5) if part else (0, 1, 2, 3)
    members = factors.shape[1] // 12
    main = members * 8
    span, half = 3 * width // 2, width // 2

    def scaled(i):
        return (factors[i].astype(f32) * g[...]).astype(bf16)

    def unpack(sources, b):
        near = iota((8, half), 0) < 4
        for i in needed:
            held = [
                source[d, :, i * span : (i + 1) * span].astype(f32)
                for source in sources
                for d in range(source.shape[0])
            ]
            for k in range(0, members, 2):
                even, odd = held[k], held[k + 1]
                factors[i, k * 8 : (k + 2) * 8, :] = jnp.concatenate(
                    [even[:, :width], odd[:, :width]], axis=0
                ).astype(bf16)
            for k in range(0, members, 4):
                tiles = []
                for j in (k, k + 2):
                    even, odd = held[j][:, width:], held[j + 1][:, width:]
                    tiles.append(
                        jnp.concatenate(
                            [
                                jnp.where(near, even, pltpu.roll(odd, 4, 0)),
                                jnp.where(near, pltpu.roll(even, 4, 0), odd),
                            ],
                            axis=1,
                        )
                    )
                at = main + k * 4
                factors[i, at : at + 16, :] = jnp.concatenate(tiles, axis=0).astype(bf16)
        same = iota((8, 128), 1) == iota((8, 128), 0)
        more = iota((8, 128), 1) == 8 + (iota((8, 128), 0) & 3)
        for d in range(members):
            here = g_all[pl.ds(b * members + d, 1), :]
            g[d * 8 : (d + 1) * 8, :] = jnp.sum(jnp.where(same, here, 0.0), axis=1, keepdims=True)
        for d in range(0, members, 2):
            both = jnp.where(
                iota((8, 128), 0) < 4,
                g_all[pl.ds(b * members + d, 1), :],
                g_all[pl.ds(b * members + d + 1, 1), :],
            )
            at = main + d * 4
            g[at : at + 8, :] = jnp.sum(jnp.where(more, both, 0.0), axis=1, keepdims=True)
        if part:
            branch[...] = scaled(5)

    def put(target, values, b):
        if blocks == 1:
            target[...] = values
        else:
            target[...] = jnp.where(b == 0, values, target[...] + values)

    def each_block(one):
        if blocks == 1:
            one(0, 0)
        else:
            arrived, sem = rest[-2], rest[-1]

            def step(b, carry):
                for side, source in enumerate((low_in, high_in)):

                    @pl.when((b < blocks // 2) == (side == 0))
                    def _(side=side, source=source):
                        at = b - side * (blocks // 2)
                        load = pltpu.make_async_copy(
                            source.at[pl.ds(at * members, members)], arrived, sem
                        )
                        load.start()
                        load.wait()

                unpack([arrived], b)
                return one(b, carry)

            lax.fori_loop(0, blocks, step, 0)

    stores = {}

    def save(source, target, sem):
        store = pltpu.make_async_copy(source, target, out_sems.at[sem])
        store.start()
        stores[sem] = store

    if blocks == 1:
        unpack([low_in, high_in], 0)
    if not part:
        for i, j, slot, target in ((0, 1, 0, rest[0]), (2, 3, 1, rest[1])):

            def square(b, carry, i=i, j=j, slot=slot):
                put(flat.at[slot], mm_tn(factors[i], scaled(j)), b)
                return carry

            each_block(square)
            save(flat.at[slot], target, 4 + slot)
    for c in mine:
        slot = c % 2
        at = slice(c * chunk, (c + 1) * chunk)

        def one(b, carry, slot=slot, at=at):
            value, slope = gelu_pair(mm(factors[4], wi[:, at]))
            grad = (mm_nt(branch[...], wf[at, :]) * slope).astype(bf16)
            put(inner.at[slot], mm_tn(factors[4], grad), b)
            put(outer.at[slot], mm_tn(value.astype(bf16), branch[...]), b)
            return carry

        each_block(one)
        save(inner.at[slot], rest[0].at[:, pl.ds(c * chunk, chunk)], slot)
        save(outer.at[slot], rest[1].at[pl.ds(c * chunk, chunk), :], 2 + slot)
    for store in stores.values():
        store.wait()


def outer_call(part, low, high, g_all, wi, wf, held):
    devices = 2 * low.shape[0]
    width, hidden = wi.shape
    chunk = hidden // 4
    members = min(devices, 32)
    blocks = devices // members
    block = members * 12
    shape = jax.ShapeDtypeStruct
    wide = [shape((width, hidden), f32), shape((hidden, width), f32)]
    flat = [shape((width, width), f32)] * 2
    place = whole if blocks == 1 else outside
    more = [] if blocks == 1 else [
        pltpu.VMEM((members,) + low.shape[1:], bf16), pltpu.SemaphoreType.DMA
    ]
    return pl.pallas_call(
        functools.partial(outer_kernel, (part, chunk, blocks)),
        out_shape=wide if part else flat,
        in_specs=[place] * 2 + [whole] * 3 + [outside] * len(held),
        out_specs=[outside] * 2,
        input_output_aliases={5: 0, 6: 1} if held else {},
        scratch_shapes=[
            pltpu.VMEM((6, block, width), bf16),
            pltpu.VMEM((block, 1), f32),
            pltpu.VMEM((block, width), bf16),
            pltpu.VMEM((2, width, chunk), f32),
            pltpu.VMEM((2, chunk, width), f32),
            pltpu.VMEM((2, width, width), f32),
            pltpu.SemaphoreType.DMA((6,)),
        ] + more,
        compiler_params=pltpu.CompilerParams(vmem_limit_bytes=28 * mega),
        cost_estimate=pl.CostEstimate(
            flops=int(1e10), bytes_accessed=int(2e7), transcendentals=int(1e6)
        ),
        name=f"outer_{part}",
    )(low, high, g_all, wi, wf, *held)


def small_call(kernel, name, outs, *args):
    return pl.pallas_call(
        kernel,
        out_shape=outs,
        in_specs=[whole] * len(args),
        out_specs=[whole] * len(outs) if isinstance(outs, (list, tuple)) else whole,
        compiler_params=pltpu.CompilerParams(vmem_limit_bytes=8 * mega),
        cost_estimate=pl.CostEstimate(flops=1000, bytes_accessed=int(1e6), transcendentals=0),
        name=name,
    )(*args)


def join(mine, come):
    if mine.size > 1 << 21:
        return jnp.concatenate([mine, come], axis=0)

    def kernel(a, b, out):
        out[: a.shape[0]] = a[...]
        out[a.shape[0] :] = b[...]

    shape = (2 * mine.shape[0],) + mine.shape[1:]
    return small_call(kernel, "join", jax.ShapeDtypeStruct(shape, mine.dtype), mine, come)


def fold(keep, come):
    half = keep.shape[0] // 2

    def kernel(a, b, first, second):
        for i in range(half):
            first[i] = a[i] + b[i]
            second[i] = a[half + i] + b[half + i]

    out = jax.ShapeDtypeStruct((half,) + keep.shape[1:], keep.dtype)
    return small_call(kernel, "fold", [out, out], keep, come)


def split(mine, come):
    half = mine.shape[2] // 2

    def kernel(a, b, left, right):
        for i, part in enumerate((a, b)):
            left[i] = part[0, :, :half]
            right[i] = part[0, :, half:]

    out = jax.ShapeDtypeStruct((2, mine.shape[1], half), mine.dtype)
    return small_call(kernel, "split", [out, out], mine, come)


def weave(left, come_left, right, come_right):
    half = left.shape[2]

    def kernel(a, b, c, d, out):
        for i in range(8):
            first, second, third = i >> 2, (i >> 1) & 1, i & 1
            out[i, :, :half] = (b if first else a)[2 * second + third]
            out[i, :, half:] = (d if second else c)[2 * first + third]

    out = jax.ShapeDtypeStruct((8,) + left.shape[1:2] + (2 * half,), left.dtype)
    return small_call(kernel, "weave", out, left, come_left, right, come_right)


def close(keep, come, smalls, first_sum):
    rows = keep.shape[1]

    def kernel(a, b, c, d, out):
        out[0, :rows, :] = a[0] + b[0]
        low = jnp.where(iota(c.shape, 0) == 4, d[...], c[...])
        tail = jnp.concatenate([low, jnp.zeros_like(low)], axis=0)
        out[0, rows:, :] = tail.astype(bf16)

    out = jax.ShapeDtypeStruct((1, rows + group, keep.shape[2]), keep.dtype)
    return small_call(kernel, "close", out, keep, come, smalls, first_sum)


def add(mine, come):
    def kernel(a, b, out):
        out[...] = a[...] + b[...]

    return small_call(kernel, "add", jax.ShapeDtypeStruct(mine.shape, mine.dtype), mine, come)


def last_kernel(dims, held, *rest):
    stages, part, piece, heads, buckets = dims
    half, _, width = held.shape
    if part:
        earlier, rest = rest[0], rest[3:]
    sides = rest[:2]
    values, sems = rest[-2:]
    me = own_code(stages)
    blocks = width // piece
    for i in range(half):
        owner = me ^ (part * half + i)
        at = pl.multiple_of((owner & (blocks - 1)) * piece, group)
        side_of = lax.shift_right_logical(owner, int(math.log2(blocks)))
        values[i] = held[i, :piece, :].astype(f32)
        for side in range(2):

            @pl.when(side_of == side)
            def _(side=side, at=at, i=i):
                pltpu.make_async_copy(
                    values.at[i], sides[side].at[pl.ds(at, piece), :], sems.at[i]
                ).start()

    total = sum(held[i, piece:, :].astype(f32)[:8] for i in range(half))
    if part:
        total = total + earlier[...]
        for i, out in zip((4, 0, 1, 2), rest[2:6]):
            out[...] = total[i : i + 1, :].reshape(width)
        spots = iota((width, 128), 0)
        by_bucket = jnp.where((spots & (buckets - 1)) == iota((width, 128), 1), 1.0, 0.0)
        by_head = jnp.where(
            lax.shift_right_logical(iota((group, width), 1), int(math.log2(buckets)))
            == iota((group, width), 0),
            total[3:4, :], 0.0,
        )
        table = lax.dot_general(
            by_head, by_bucket, (((1,), (0,)), ((), ())),
            precision=highest, preferred_element_type=f32,
        )
        rest[6][...] = table[:heads, :buckets]
    else:
        rest[2][...] = total
    for i in range(half):
        pltpu.make_async_copy(values.at[i], sides[0].at[pl.ds(0, piece), :], sems.at[i]).wait()


def last_call(stages, part, held, piece, buckets, heads, earlier):
    half, _, width = held.shape
    shape = jax.ShapeDtypeStruct
    squares = [shape((width, width), f32)] * 2
    more = (
        [shape((width,), f32)] * 4 + [shape((heads, buckets), f32)] if part else [shape((8, width), f32)]
    )
    return pl.pallas_call(
        functools.partial(last_kernel, (stages, part, piece, heads, buckets)),
        out_shape=squares + more,
        in_specs=[whole] * (2 if part else 1) + [outside] * (2 if part else 0),
        out_specs=[outside] * 2 + [whole] * len(more),
        input_output_aliases={2: 0, 3: 1} if part else {},
        scratch_shapes=[pltpu.VMEM((half, piece, width), f32), pltpu.SemaphoreType.DMA((half,))],
        compiler_params=pltpu.CompilerParams(vmem_limit_bytes=12 * mega),
        cost_estimate=pl.CostEstimate(flops=int(1e7), bytes_accessed=int(5e6), transcendentals=0),
        name=f"last_{part}",
    )(held, *earlier)


def shards(
    docs, lists,
    tokens, pair_lengths, list_ids, relevance,
    first_gain, query_weight, key_weight, value_weight, output_weight, bias_table,
    second_gain, inner_weight, outer_weight, final_gain, score_vector,
):
    row_count, length, width = tokens.shape[1:]
    pairs = pair_lengths.shape[2]
    buckets, heads = bias_table.shape
    devices = docs * lists
    sizes = {"docs": docs, "lists": lists}
    stages = tuple(("lists", 1 << b) for b in range(lists.bit_length() - 1)) + tuple(
        ("docs", 1 << b) for b in range(docs.bit_length() - 1)
    )

    def swap(values, stage):
        axis, mask = stage
        return lax.ppermute(values, axis, [(i, i ^ mask) for i in range(sizes[axis])])

    rows = tokens.reshape(row_count, length, width)
    lengths = pair_lengths.reshape(row_count, pairs)
    spot = lax.broadcasted_iota(jnp.int32, (group, width), 0)
    gains = jnp.pad(bias_table.T, ((4, group - 4 - heads), (0, width - buckets)))
    for i, vector in enumerate((first_gain, second_gain, final_gain, score_vector)):
        gains = jnp.where(spot == i, vector[None, :], gains)
    members = list_ids.shape[1]
    known = jnp.pad(list_ids, ((0, 0), (0, members))) + jnp.pad(relevance, ((0, 0), (members, 0)))
    outs = path_call(
        rows, lengths, known, gains, heads, buckets,
        (query_weight, key_weight, value_weight, output_weight, inner_weight, outer_weight),
    )
    pay, factors, n1, probs, dl, turned, yk, yv, qf, gctx, z, vz, ga, a2, fhat, yq = outs[:16]
    wq, wk, wv, wo, wi, wf, scores = outs[16:]

    tie = lax.optimization_barrier
    gather_order = tuple(reversed(stages))

    rows_left = list(gather_order)
    come = None
    for i, stage in enumerate(gather_order):
        pay = join(pay, swap(pay, stage))
        if i == 0:
            factors, pay = tie((factors, pay))
            come = swap(factors, rows_left.pop(0))
        elif i == 2:
            come, pay = tie((come, pay))
            factors = join(factors, come)
            come = swap(factors, rows_left.pop(0))
    count = row_count * pairs
    dims = (stages, docs, lists, docs // 2, count, heads, buckets)
    keep, send, g_all, g_own, smalls = terms_call(
        dims, pay, z, vz, qf, gctx, turned, a2, fhat, gains
    )
    piece = keep.shape[1]
    cut = cut_stages(stages, width)
    rest = stages[len(cut) :]
    for stage in cut[:-3]:
        keep, send = fold(keep, swap(send, stage))

    come, send = tie((come, send))
    factors = join(factors, come)
    n1, send, factors = tie((n1, send, factors))
    arrived = swap(send, cut[-3])
    come = swap(factors, rows_left.pop(0))
    attended = attention_call((heads, buckets), lengths, n1, rows, gains, (wq, wk, wv, wo))
    arrived, come, attended = tie((arrived, come, attended))
    keep, send = fold(keep, arrived)
    factors = join(factors, come)

    attended, send, factors = tie((attended, send, factors))
    arrived = swap(send, cut[-2])
    come = swap(factors, rows_left.pop(0))
    encoded = feed_call(0, attended, gains, wi, wf, None)
    arrived, encoded = tie((arrived, encoded))
    keep, send = fold(keep, arrived)

    probs, send, encoded = tie((probs, send, encoded))
    arrived = swap(send, cut[-1])
    grads, first_sum = tokens_grad_call(
        lengths, rows, g_own, probs, dl, yk, yv, yq, ga, gains
    )
    arrived, grads, first_sum = tie((arrived, grads, first_sum))
    held = close(keep, arrived, smalls, first_sum)

    for stage in rest[:-1]:
        held = add(held, swap(held, stage))
    attended, held = tie((attended, held))
    arrived = swap(held, rest[-1])
    encoded = feed_call(1, attended, gains, wi, wf, encoded)
    arrived, encoded = tie((arrived, encoded))
    held = add(held, arrived)

    come, held = tie((come, held))
    while True:
        factors = join(factors, come)
        come = swap(factors, rows_left.pop(0))
        if not rows_left:
            break
    arrived = swap(held, cut[-1])
    last_come, arrived = tie((come, arrived))
    left, right = split(held, arrived)

    left, right, last_come = tie((left, right, last_come))
    come = swap(left, cut[-2]), swap(right, cut[-3])
    products = tuple(outer_call(0, factors, last_come, g_all, wi, wf, ()))
    wide = tuple(outer_call(1, factors, last_come, g_all, wi, wf, ()))
    products, wide, come = tie((products, wide, come))
    query_grad, output_grad = products
    left, right = join(left, come[0]), join(right, come[1])

    left, right, wide = tie((left, right, wide))
    come = swap(left, cut[-3]), swap(right, cut[-2])
    wide = outer_call(2, factors, last_come, g_all, wi, wf, wide)
    wide, come = tie((tuple(wide), come))
    held = weave(left, come[0], right, come[1])

    for stage in reversed(cut[1:-3]):
        held = join(held, swap(held, stage))
    come = swap(held, cut[0])
    key_grad, value_grad, small_sums = last_call(cut, 0, held, piece, buckets, heads, ())
    (
        key_grad, value_grad, first_grad, second_grad, final_grad, vector_grad, table_grad
    ) = last_call(cut, 1, come, piece, buckets, heads, (small_sums, key_grad, value_grad))
    inner_grad, outer_grad = wide
    return (
        encoded.reshape(tokens.shape),
        scores.reshape(1, row_count, pairs),
        grads.reshape(tokens.shape),
        first_grad,
        query_grad,
        key_grad,
        value_grad,
        output_grad,
        table_grad.T,
        second_grad,
        inner_grad,
        outer_grad,
        final_grad,
        vector_grad,
    )


def solution(mesh):
    placed = P("lists", "docs", None, None)
    return jax.shard_map(
        functools.partial(shards, mesh.shape["docs"], mesh.shape["lists"]),
        mesh=mesh,
        in_specs=(placed, P("lists", "docs", None), P("lists", None), P("lists", None)) + (P(),) * 11,
        out_specs=(placed, P("lists", "docs", None), placed) + (P(),) * 11,
        check_vma=False,
    )
```

```python
import functools
import math

import jax
import jax.numpy as jnp
from jax import lax
from jax.experimental import pallas as pl
from jax.experimental.pallas import tpu as pltpu
from jax.sharding import PartitionSpec as P

epsilon = 1e-06
negative = -1000000000.0
highest = lax.Precision.HIGHEST
limits = (12, 16, 23, 32, 46, 64, 91)
f32 = jnp.float32
bf16 = jnp.bfloat16
window = 128
reach = 144
lanes_path = 256
group = 16
mega = 1 << 20
curve = math.sqrt(2.0 / math.pi)
cubic = 0.044715
whole = pl.BlockSpec(memory_space=pltpu.VMEM)
scalars = pl.BlockSpec(memory_space=pltpu.SMEM)
outside = pl.BlockSpec(memory_space=pl.ANY)


def mm(a, b):
    return lax.dot_general(a, b, (((1,), (0,)), ((), ())), preferred_element_type=f32)


def mm_nt(a, b):
    return lax.dot_general(a, b, (((1,), (1,)), ((), ())), preferred_element_type=f32)


def mm_tn(a, b):
    return lax.dot_general(a, b, (((0,), (0,)), ((), ())), preferred_element_type=f32)


def as_row(gains, i):
    return gains[i : i + 1, :]


def iota(shape, axis):
    return lax.broadcasted_iota(jnp.int32, shape, axis)


def bucket_of(offsets):
    upper_half = jnp.where(offsets > 0, 16, 0)
    distance = jnp.abs(offsets)
    beyond = jnp.full(offsets.shape, 8, jnp.int32)
    for border in limits:
        beyond = beyond + jnp.where(distance >= border, 1, 0)
    return upper_half + jnp.where(distance < 8, distance, beyond)


def rms_factor(values):
    return lax.rsqrt(jnp.mean(values * values, axis=-1, keepdims=True) + epsilon)


def norm_back(normed, factor, upstream):
    return factor * (upstream - normed * jnp.mean(upstream * normed, axis=-1, keepdims=True))


def half_bent(values, square):
    return 0.5 * jnp.tanh(values * (square * (curve * cubic) + curve)) + 0.5


def gelu(values):
    return values * half_bent(values, values * values)


def gelu_pair(values):
    square = values * values
    half = half_bent(values, square)
    value = half * values
    steep = (value - value * half) * (square * (6.0 * curve * cubic) + 2.0 * curve)
    return value, half + steep


def bias_vector(table, lanes, origin):
    buckets = table.shape[1]
    buckets_at = bucket_of(iota((buckets, lanes), 1) - origin)
    chosen = jnp.where(buckets_at == iota((buckets, lanes), 0), 1.0, 0.0)
    return lax.dot_general(
        table, chosen, (((1,), (0,)), ((), ())), precision=highest, preferred_element_type=f32
    )


def cast_rows(target, source, chunk):
    rows = source.shape[0]

    def step(i, carry):
        at = pl.ds(pl.multiple_of(i * chunk, chunk), chunk)
        target[at, :] = source[at, :].astype(bf16)
        return carry

    lax.fori_loop(0, rows // chunk, step, 0)


def starts_of(lengths, row, count):
    out, at = [], 0
    for i in range(count):
        out.append((at, lengths[row, i]))
        at = at + lengths[row, i]
    return out


def path_kernel(
    dims,
    lengths, known,
    tokens_in, gains,
    wq_in, wk_in, wv_in, wo_in, wi_in, wf_in,
    pay, factors, n1_out, probs_out, dl_out, turned_out, yk_out, yv_out, qf_out, gctx_out, z_out, vz_out,
    ga_out, a2_out, fhat_out, yq_out,
    wq, wk, wv, wo, wi, wf, scores_out,
    tokens, square, padded, first, gather_z, logits, expand, wide_z,
    in_sems, tokens_sem,
):
    rows, length, width, pairs, heads, buckets = dims
    members = known.shape[1] // 2
    count = rows * pairs
    parts = wi.shape[1] // width
    slots = square.shape[0]
    chunks = [(wq_in, wq), (wk_in, wk), (wv_in, wv), (wo_in, wo)]
    for i in range(parts):
        at = pl.ds(i * width, width)
        chunks.append((wi_in.at[:, at], wi.at[:, at]))
    for i in range(parts):
        at = pl.ds(i * width, width)
        chunks.append((wf_in.at[at, :], wf.at[at, :]))

    def load_of(i):
        return pltpu.make_async_copy(chunks[i][0], square.at[i % slots], in_sems.at[i % slots])

    tokens_load = pltpu.make_async_copy(tokens_in, tokens, tokens_sem)
    tokens_load.start()
    order = iter(range(slots))

    def request(count):
        for _ in range(count):
            load_of(next(order)).start()

    request(2)
    tokens_load.wait()
    request(2)

    gain = as_row(gains, 0)
    for r in range(rows):
        padded[r, length:, :] = jnp.zeros((reach, width), bf16)

        def norm_step(i, carry, r=r):
            at = pl.ds(pl.multiple_of(i * 64, 64), 64)
            x = tokens[r, at, :]
            n = (x * rms_factor(x) * gain).astype(bf16)
            n1_out[r, at, :] = n
            padded[r, at, :] = n
            return carry

        lax.fori_loop(0, length // 64, norm_step, 0)
        request(2)
    first[...] = jnp.zeros(first.shape, f32)
    pieces = []
    for r in range(rows):
        for at, size in starts_of(lengths, r, pairs):
            p = len(pieces)
            shift = at & (group - 1)
            pieces.append((r, pl.multiple_of(at - shift, group), shift, size))
            first[p : p + 1, :] = tokens[r, pl.ds(at, 1), :]

    def nearby(p):
        r, base, _, _ = pieces[p]
        return padded[r, pl.ds(base, reach), :]

    spots = [slice(p * group, (p + 1) * group) for p in range(count)]
    head_rows = iota((group, width), 0) == lax.shift_right_logical(
        iota((group, width), 1), int(math.log2(width // heads))
    )

    def widen(values):
        for p in range(count):
            expand[p * group : (p + 1) * group, :] = jnp.where(
                head_rows, values[p : p + 1, :], 0.0
            ).astype(bf16)

    def narrow(target):
        target[...] = jnp.zeros(target.shape, f32)
        for p in range(count):
            block = wide_z[p * group : (p + 1) * group, :]
            target[p : p + 1, :] = jnp.sum(
                jnp.where(head_rows, block, 0.0), axis=0, keepdims=True
            )

    def take(i):
        load_of(i).wait()
        cast_rows(chunks[i][1], square.at[i % slots], 64)
        if i < 4:
            request(1)

    take(0)
    n1_first = (first[...] * rms_factor(first[...]) * gain).astype(bf16)
    q_first = mm(n1_first, wq[...]).astype(bf16)
    qf_out[...] = q_first
    widen(q_first.astype(f32))
    take(1)
    yk_out[...] = mm_nt(expand[...], wk[...]).astype(bf16)
    position = bias_vector(gains[4 : 4 + heads, :buckets], lanes_path, 0)
    position = jnp.concatenate([position, jnp.zeros((group - heads, lanes_path), f32)], axis=0)
    lane = iota((group, lanes_path), 1)
    for p, (_, _, shift, size) in enumerate(pieces):
        logits[spots[p], :reach] = mm_nt(yk_out[spots[p], :], nearby(p))
        block = logits[spots[p], :] + pltpu.roll(position, shift, 1)
        inside = jnp.logical_and(lane >= shift, lane < shift + size)
        logits[spots[p], :] = jnp.where(inside, block, negative)
    take(2)
    take(3)
    scores_in = logits[...]
    peak = jnp.max(scores_in, axis=-1, keepdims=True)
    raised = jnp.exp(scores_in - peak)
    probs = raised / jnp.sum(raised, axis=-1, keepdims=True)
    probs_out[...] = probs.astype(bf16)
    for p in range(count):
        vz_out[spots[p], :] = mm(probs_out[spots[p], :reach], nearby(p)).astype(bf16)
    wide_z[...] = mm(vz_out[...], wv[...])
    narrow(gather_z)
    context = gather_z[...].astype(bf16)
    attended = first[...] + mm(context, wo[...])
    scale_two = rms_factor(attended)
    second = attended * scale_two
    normed_two = (second * as_row(gains, 1)).astype(bf16)
    for i in range(parts):
        take(4 + i)
    value, slope = gelu_pair(mm(normed_two, wi[...]))
    for i in range(parts):
        take(4 + parts + i)
    encoded = attended + mm(value.astype(bf16), wf[...])
    scale_final = rms_factor(encoded)
    final_hat = encoded * scale_final
    fhat_out[...] = final_hat
    unit = as_row(gains, 3) * as_row(gains, 2)
    score_col = jnp.sum(final_hat * unit, axis=-1, keepdims=True)
    square_lane = iota((group, 128), 1)
    row = jnp.sum(
        jnp.where(square_lane == iota((group, 128), 0), score_col, 0.0), axis=0, keepdims=True
    )
    for r in range(rows):
        scores_out[r : r + 1, :] = row[:, r * pairs : (r + 1) * pairs]
    row_lane = iota((1, 128), 1)
    place = lax.axis_index("docs") * count
    for i in range(count):
        row = jnp.where(row_lane == group + i, known[0, place + i].astype(f32), row)
        row = jnp.where(row_lane == 2 * group + i, known[0, members + place + i].astype(f32), row)
    pay[...] = row

    grad_encoded = norm_back(final_hat, scale_final, jnp.broadcast_to(unit, final_hat.shape))
    grad_branch = grad_encoded.astype(bf16)
    grad_preact = (mm_nt(grad_branch, wf[...]) * slope).astype(bf16)
    grad_normed_two = mm_nt(grad_preact, wi[...])
    a2_out[...] = second * grad_normed_two
    grad_attended = grad_encoded + norm_back(second, scale_two, grad_normed_two * as_row(gains, 1))
    ga_out[...] = grad_attended
    grad_attn = grad_attended.astype(bf16)
    grad_context = mm_nt(grad_attn, wo[...])
    gctx_out[...] = grad_context
    widen(grad_context)
    yv_out[...] = mm_nt(expand[...], wv[...]).astype(bf16)
    logits[...] = jnp.zeros(logits.shape, f32)
    for p in range(count):
        logits[spots[p], :reach] = mm_nt(yv_out[spots[p], :], nearby(p))
    grad_probs = logits[...]
    grad_logits = probs * (grad_probs - jnp.sum(probs * grad_probs, axis=-1, keepdims=True))
    dl_out[...] = grad_logits.astype(bf16)
    for p, (_, _, shift, _) in enumerate(pieces):
        rounded = dl_out[spots[p], :]
        z_out[spots[p], :] = mm(rounded[:, :reach], nearby(p))
        turned = pltpu.roll(rounded.astype(f32), (lanes_path - shift) & (lanes_path - 1), 1)
        turned_out[spots[p], :] = turned[:, :window]
    wide_z[...] = mm(z_out[...].astype(bf16), wk[...])
    narrow(gather_z)
    grad_query = gather_z[...].astype(bf16)
    yq_out[...] = mm_nt(grad_query, wq[...])
    span, half = 3 * width // 2, width // 2
    for i, member in enumerate((n1_first, grad_query, context, grad_attn, normed_two, grad_branch)):
        member = member.astype(f32)
        tail = member[8:, :]
        tail = jnp.where(
            iota((8, half), 0) < 4, tail[:, :half], pltpu.roll(tail[:, half:], 4, 0)
        )
        factors[0, :, i * span : i * span + width] = member[:8].astype(bf16)
        factors[0, :, i * span + width : (i + 1) * span] = tail.astype(bf16)


def path_call(tokens, lengths, known, gains, heads, buckets, weights):
    rows, length, width = tokens.shape
    pairs = lengths.shape[1]
    combos = rows * pairs * group
    shape = jax.ShapeDtypeStruct
    outs = [
        shape((1, 128), f32),
        shape((1, 8, 9 * width), bf16),
        shape((rows, length, width), bf16),
        shape((combos, lanes_path), bf16),
        shape((combos, lanes_path), bf16),
        shape((combos, window), f32),
        shape((combos, width), bf16),
        shape((combos, width), bf16),
        shape((group, width), bf16),
        shape((group, width), f32),
        shape((combos, width), f32),
        shape((combos, width), bf16),
        shape((group, width), f32),
        shape((group, width), f32),
        shape((group, width), f32),
        shape((group, width), f32),
    ]
    low = [shape(w.shape, bf16) for w in weights] + [shape((rows, pairs), f32)]
    return pl.pallas_call(
        functools.partial(path_kernel, (rows, length, width, pairs, heads, buckets)),
        out_shape=outs + low,
        in_specs=[scalars] * 2 + [outside, whole] + [outside] * 6,
        out_specs=[whole] * (len(outs) + len(low)),
        scratch_shapes=[
            pltpu.VMEM(tokens.shape, f32),
            pltpu.VMEM((12, width, width), f32),
            pltpu.VMEM((rows, length + reach, width), bf16),
            pltpu.VMEM((group, width), f32),
            pltpu.VMEM((group, width), f32),
            pltpu.VMEM((combos, lanes_path), f32),
            pltpu.VMEM((combos, width), bf16),
            pltpu.VMEM((combos, width), f32),
            pltpu.SemaphoreType.DMA((12,)),
            pltpu.SemaphoreType.DMA,
        ],
        compiler_params=pltpu.CompilerParams(vmem_limit_bytes=45 * mega),
        cost_estimate=pl.CostEstimate(flops=int(9e9), bytes_accessed=int(5e7), transcendentals=0),
        name="path",
    )(lengths, known, tokens, gains, *weights)


def code_of(stages, indices):
    total = len(stages)
    code = 0
    for s, (axis, mask) in enumerate(stages):
        bit = jnp.where((indices[axis] & mask) != 0, 1, 0) if not isinstance(
            indices[axis], int
        ) else (1 if indices[axis] & mask else 0)
        code = code + bit * (1 << (total - 1 - s))
    return code


def cut_stages(stages, width):
    count = 3 + sum(axis == "lists" for axis, _ in stages)
    while (2 * width) % (group << count):
        count -= 1
    return stages[:count]


def own_code(stages):
    return code_of(stages, {axis: lax.axis_index(axis) for axis in ("docs", "lists")})


def terms_kernel(
    dims,
    pay, z, vz, qf, gctx, dl, a2, fhat, gains,
    keep, send, g_all, g_own, smalls,
    term, left, right,
):
    stages, docs, lists, list_count, count, heads, buckets = dims
    width = z.shape[1]
    everything = pay[...]
    lane = iota(everything.shape, 1)
    score = everything
    names = pltpu.roll(everything, 128 - group, 1)
    label = pltpu.roll(everything, 128 - 2 * group, 1)
    used = lane < count
    part = lax.shift_right_logical(iota(everything.shape, 0), int(math.log2(docs)))
    key = jnp.where(used, part * list_count + names.astype(jnp.int32), -1)

    def total_of(values):
        return jnp.sum(jnp.sum(values, axis=1, keepdims=True), axis=0, keepdims=True)

    def top_step(k, top):
        member = key == k
        best = jnp.max(
            jnp.max(jnp.where(member, score, negative), axis=1, keepdims=True),
            axis=0, keepdims=True,
        )
        return jnp.where(member, best, top)

    keys = lists * list_count
    unroll = keys if keys <= 16 else 4
    top = lax.fori_loop(0, keys, top_step, score, unroll=unroll)
    raised = jnp.exp(score - top)

    def sum_step(k, carry):
        total, gain = carry
        member = key == k
        return (
            jnp.where(member, total_of(jnp.where(member, raised, 0.0)), total),
            jnp.where(member, total_of(jnp.where(member, label, 0.0)), gain),
        )

    ones = jnp.ones(everything.shape, f32)
    total, gain = lax.fori_loop(0, keys, sum_step, (ones, ones), unroll=unroll)
    grads = jnp.where(used, raised / total * gain - label, 0.0)
    g_all[...] = grads
    own = grads[0:1, :]
    g_own[...] = jnp.broadcast_to(own, g_own.shape)

    combos = count * group
    pair_of = lax.shift_right_logical(iota((combos, 128), 0), int(math.log2(group)))
    g_combo = jnp.sum(jnp.where(iota((combos, 128), 1) == pair_of, own, 0.0), axis=1, keepdims=True)
    g_pair = jnp.sum(
        jnp.where(iota((group, 128), 1) == iota((group, 128), 0), own, 0.0), axis=1, keepdims=True
    )
    head_rows = iota((group, width), 0) == lax.shift_right_logical(
        iota((group, width), 1), int(math.log2(width // heads))
    )
    queries = qf[...].astype(f32)
    upstream = gctx[...] * g_pair
    for p in range(count):
        at = slice(p * group, (p + 1) * group)
        right[0, at, :] = jnp.where(head_rows, queries[p : p + 1, :], 0.0).astype(bf16)
        right[1, at, :] = jnp.where(head_rows, upstream[p : p + 1, :], 0.0).astype(bf16)
    left[...] = (z[...] * g_combo).astype(bf16)
    term[0:width, :] = mm_tn(left[...], right[0])
    term[width : 2 * width, :] = mm_tn(vz[...], right[1])

    half, piece = keep.shape[0], keep.shape[1]
    blocks = width // piece
    mine = own_code(stages[: half.bit_length()])

    def piece_step(r, carry, target, base):
        owner = mine ^ (base + r)
        side = lax.shift_right_logical(owner, int(math.log2(blocks)))
        at = side * width + (owner & (blocks - 1)) * piece
        target[r] = term[pl.ds(pl.multiple_of(at, group), piece), :].astype(bf16)
        return carry

    lax.fori_loop(0, half, functools.partial(piece_step, target=send, base=half), 0)
    lax.fori_loop(0, half, functools.partial(piece_step, target=keep, base=0), 0)

    smalls[...] = jnp.zeros(smalls.shape, f32)
    smalls[0:1, :] = jnp.sum(a2[...] * g_pair, axis=0, keepdims=True)
    hats = jnp.sum(fhat[...] * g_pair, axis=0, keepdims=True)
    smalls[1:2, :] = hats * as_row(gains, 3)
    smalls[2:3, :] = hats * as_row(gains, 2)
    weighted = dl[...] * g_combo
    summed = weighted[0:group, :]
    for p in range(1, count):
        summed = summed + weighted[p * group : (p + 1) * group, :]
    spots = iota((window, width), 1)
    hot = jnp.where(bucket_of(iota((window, width), 0)) == (spots & (buckets - 1)), 1.0, 0.0)
    spread = lax.dot_general(
        summed, hot, (((1,), (0,)), ((), ())), precision=highest, preferred_element_type=f32
    )
    row_of = lax.shift_right_logical(iota((group, width), 1), int(math.log2(buckets)))
    smalls[3:4, :] = jnp.sum(
        jnp.where(row_of == iota((group, width), 0), spread, 0.0), axis=0, keepdims=True
    )


def terms_call(dims, pay, z, vz, qf, gctx, dl, a2, fhat, gains):
    stages, docs, lists, list_count, count, heads, buckets = dims
    devices = docs * lists
    combos, width = z.shape
    pieces = 1 << len(cut_stages(stages, width))
    piece = 2 * width // pieces
    shape = jax.ShapeDtypeStruct
    half = shape((pieces // 2, piece, width), bf16)
    return pl.pallas_call(
        functools.partial(terms_kernel, dims),
        out_shape=[
            half, half,
            shape((devices, 128), f32),
            shape((8, 128), f32),
            shape((8, width), f32),
        ],
        in_specs=[whole] * 9,
        out_specs=[whole] * 5,
        scratch_shapes=[
            pltpu.VMEM((2 * width, width), f32),
            pltpu.VMEM((combos, width), bf16),
            pltpu.VMEM((2, combos, width), bf16),
        ],
        compiler_params=pltpu.CompilerParams(vmem_limit_bytes=10 * mega),
        cost_estimate=pl.CostEstimate(flops=int(4e9), bytes_accessed=int(1e7), transcendentals=0),
        name="terms",
    )(pay, z, vz, qf, gctx, dl, a2, fhat, gains)


def project_kernel(row, n1, wq, wk, wv, q, k, v):
    for target, low in ((q, wq), (k, wk), (v, wv)):
        target[...] = mm(n1[row], low[...]).astype(bf16)


def project_call(row, n1, wq, wk, wv):
    return pl.pallas_call(
        functools.partial(project_kernel, row),
        out_shape=[jax.ShapeDtypeStruct(n1.shape[1:], bf16)] * 3,
        in_specs=[whole] * 4,
        out_specs=[whole] * 3,
        compiler_params=pltpu.CompilerParams(vmem_limit_bytes=12 * mega),
        cost_estimate=pl.CostEstimate(flops=int(2e9), bytes_accessed=int(4e6), transcendentals=0),
        name=f"project_{row}",
    )(n1, wq, wk, wv)


def bias_kernel(heads, buckets, gains, bias):
    lanes = 4 * window
    vector = bias_vector(gains[4 : 4 + heads, :buckets], lanes, window)
    for h in range(heads):
        bias[h] = pltpu.roll(
            jnp.broadcast_to(vector[h : h + 1, :], (window, lanes)), 0, 1, stride=1, stride_axis=0
        )[:, : 3 * window]


def bias_call(heads, buckets, gains):
    return small_call(
        functools.partial(bias_kernel, heads, buckets), "bias",
        jax.ShapeDtypeStruct((heads, window, 3 * window), f32), gains,
    )


def attention_kernel(
    lengths, tokens_in, bias, wo, *rest
):
    out, tokens, ctx, qseg, kseg, sem = rest[-6:]
    rows, length, width = tokens.shape
    heads = bias.shape[0]
    pairs = lengths.shape[1]
    load = pltpu.make_async_copy(tokens_in, tokens, sem)
    load.start()
    tiles = length // window
    half = iota((2 * window, window), 1) < (width // heads)
    left = half[:window]
    upper = iota((2 * window, window), 0) < window
    chosen = half == upper

    def segment(positions, ends):
        total = jnp.zeros(positions.shape, jnp.int32)
        for end in ends:
            total = total + jnp.where(positions >= end, 1, 0)
        return total

    wide = iota((length, window), 1)
    units = []
    for row in range(rows):
        for j in range(tiles):
            for pair in range(heads // 2):
                units.append((row, j, pair))
    ones = jnp.ones((3 * window, window), bf16)

    def begin(row):
        ends = [at + size for at, size in starts_of(lengths, row, pairs)]
        seg = segment(iota((length, 1), 0), ends)
        qseg[...] = jnp.where(seg == wide, 1.0, 0.0).astype(bf16)
        kseg[...] = jnp.where(jnp.logical_and(seg != wide, wide <= pairs), negative, 0.0).astype(bf16)

    def spans(j):
        t0 = j * window
        k0 = max(j - 1, 0) * window
        k1 = min(j + 2, tiles) * window
        return t0, k0, k1

    def raw_of(row, j, pair):
        t0, k0, k1 = spans(j)
        cols = slice(pair * window, (pair + 1) * window)
        both = rest[3 * row][t0 : t0 + window, cols]
        stacked = jnp.concatenate([both, both], axis=0)
        stacked = jnp.where(chosen, stacked, jnp.zeros_like(stacked))
        mark = qseg[t0 : t0 + window, :]
        return mm_nt(
            jnp.concatenate([stacked, jnp.concatenate([mark, mark], axis=0)], axis=1),
            jnp.concatenate([rest[3 * row + 1][k0:k1, cols], kseg[k0:k1, :]], axis=1),
        )

    def finish(row, j, pair, raw):
        t0, k0, k1 = spans(j)
        off = k0 - (t0 - window)
        cols = slice(pair * window, (pair + 1) * window)
        probs = []
        for side in range(2):
            part = raw[side * window : (side + 1) * window]
            part = part + bias[2 * pair + side, :, off : off + k1 - k0]
            peak = jnp.max(part, axis=-1, keepdims=True)
            probs.append(jnp.exp(part - peak).astype(bf16))
        mixed = mm(
            jnp.concatenate(probs, axis=0),
            jnp.concatenate([rest[3 * row + 2][k0:k1, cols], ones[: k1 - k0]], axis=1),
        )
        ctx[t0 : t0 + window, cols] = jnp.where(
            left,
            mixed[:window, :window] / mixed[:window, window:],
            mixed[window:, :window] / mixed[window:, window:],
        ).astype(bf16)

    def close_row(row):
        if row == 0:
            load.wait()
        out[row] = tokens[row] + mm(ctx[...], wo[...])

    for row in range(rows):
        begin(row)
        last = None
        for unit in units:
            if unit[0] != row:
                continue
            raw = raw_of(*unit)
            if last is not None:
                finish(*last)
            last = unit + (raw,)
        finish(*last)
        close_row(row)


def attention_call(lengths, tokens, bias, wo, projected):
    rows, length, width = tokens.shape
    return pl.pallas_call(
        attention_kernel,
        out_shape=jax.ShapeDtypeStruct(tokens.shape, f32),
        in_specs=[scalars, outside] + [whole] * (2 + len(projected)),
        out_specs=whole,
        scratch_shapes=[
            pltpu.VMEM(tokens.shape, f32),
            pltpu.VMEM((length, width), bf16),
            pltpu.VMEM((length, window), bf16),
            pltpu.VMEM((length, window), bf16),
            pltpu.SemaphoreType.DMA,
        ],
        compiler_params=pltpu.CompilerParams(vmem_limit_bytes=14 * mega),
        cost_estimate=pl.CostEstimate(
            flops=int(1e10), bytes_accessed=int(1e7), transcendentals=int(8e6)
        ),
        name="attention",
    )(lengths, tokens, bias, wo, *projected)


def feed_kernel(row, attended, gains, wi, wf, held, out, normed, total, sem):
    length, width = total.shape
    tile, chunk = 256, 512
    x = attended[row]
    normed[...] = (x * rms_factor(x) * as_row(gains, 1)).astype(bf16)
    total[...] = x

    def finish(t, c, ahead):
        total[t, :] += mm(gelu(ahead).astype(bf16), wf[c, :])

    last = None
    for c in range(wi.shape[1] // chunk):
        for t in range(length // tile):
            t_at, c_at = slice(t * tile, (t + 1) * tile), slice(c * chunk, (c + 1) * chunk)
            ahead = mm(normed[t_at, :], wi[:, c_at])
            if last is not None:
                finish(*last)
            last = (t_at, c_at, ahead)
    finish(*last)
    store = pltpu.make_async_copy(total, out.at[row], sem)
    store.start()
    store.wait()


def feed_call(row, attended, gain, wi, wf, held):
    rows, length, width = attended.shape
    extra = [] if held is None else [held]
    kernel = functools.partial(feed_kernel, row)
    if held is None:
        kernel = lambda a, g, i, f, *rest: feed_kernel(row, a, g, i, f, None, *rest)
    return pl.pallas_call(
        kernel,
        out_shape=jax.ShapeDtypeStruct(attended.shape, f32),
        in_specs=[whole] * 4 + [outside] * len(extra),
        out_specs=outside,
        input_output_aliases={4: 0} if extra else {},
        scratch_shapes=[
            pltpu.VMEM((length, width), bf16),
            pltpu.VMEM((length, width), f32),
            pltpu.SemaphoreType.DMA,
        ],
        compiler_params=pltpu.CompilerParams(vmem_limit_bytes=12 * mega),
        cost_estimate=pl.CostEstimate(
            flops=int(1e10), bytes_accessed=int(1e7), transcendentals=int(3e6)
        ),
        name=f"feed_{row}",
    )(attended, gain, wi, wf, *extra)


def tokens_grad_kernel(
    dims, lengths, tokens_in, g_own, probs, dl, yk, yv, yq, ga, gains,
    out, first_sum, tokens, spread, sems,
):
    rows, length, width, pairs = dims
    loads = [
        pltpu.make_async_copy(tokens_in.at[r], tokens.at[r], sems.at[r]) for r in range(rows)
    ]
    for load in loads:
        load.start()
    own = g_own[0:1, :]
    lane = iota((1, 128), 1)
    total = jnp.zeros((1, width), f32)
    stores = []
    for r in range(rows):
        spread[...] = jnp.zeros(spread.shape, f32)
        starts = starts_of(lengths, r, pairs)
        amounts = []
        for i, (at, size) in enumerate(starts):
            pair = r * pairs + i
            amount = jnp.sum(jnp.where(lane == pair, own, 0.0), axis=1, keepdims=True)
            amounts.append(amount)
            here = slice(pair * group, (pair + 1) * group)
            left = jnp.concatenate([dl[here, :], probs[here, :]], axis=0)
            right = jnp.concatenate([yk[here, :], yv[here, :]], axis=0)
            base = pl.multiple_of(at - (at & (group - 1)), group)
            spread[pl.ds(base, reach), :] += mm_tn(left, right)[:reach] * amount
        for i, (at, size) in enumerate(starts):
            pair = r * pairs + i
            spread[pl.ds(at, 1), :] += yq[pair : pair + 1, :] * amounts[i]
        loads[r].wait()
        gain_row = as_row(gains, 0)

        def step(i, carry, r=r, gain_row=gain_row):
            at = pl.ds(pl.multiple_of(i * 64, 64), 64)
            x = tokens[r, at, :]
            factor = rms_factor(x)
            hat = x * factor
            upstream = spread[at, :]
            tokens[r, at, :] = norm_back(hat, factor, upstream * gain_row)
            return carry + jnp.sum(hat * upstream, axis=0, keepdims=True)

        total = lax.fori_loop(0, length // 64, step, total)
        for i, (at, size) in enumerate(starts):
            pair = r * pairs + i
            tokens[r, pl.ds(at, 1), :] += ga[pair : pair + 1, :] * amounts[i]
        store = pltpu.make_async_copy(tokens.at[r], out.at[r], sems.at[r])
        store.start()
        stores.append(store)
    first_sum[...] = total
    for store in stores:
        store.wait()


def tokens_grad_call(lengths, tokens, g_own, probs, dl, yk, yv, yq, ga, gain):
    rows, length, width = tokens.shape
    pairs = lengths.shape[1]
    return pl.pallas_call(
        functools.partial(tokens_grad_kernel, (rows, length, width, pairs)),
        out_shape=[
            jax.ShapeDtypeStruct(tokens.shape, f32),
            jax.ShapeDtypeStruct((1, width), f32),
        ],
        in_specs=[scalars, outside] + [whole] * 8,
        out_specs=[outside, whole],
        scratch_shapes=[
            pltpu.VMEM(tokens.shape, f32),
            pltpu.VMEM((length + reach, width), f32),
            pltpu.SemaphoreType.DMA((rows,)),
        ],
        compiler_params=pltpu.CompilerParams(vmem_limit_bytes=12 * mega),
        cost_estimate=pl.CostEstimate(flops=int(2e9), bytes_accessed=int(1e7), transcendentals=0),
        name="tokens_grad",
    )(lengths, tokens, g_own, probs, dl, yk, yv, yq, ga, gain)


def outer_kernel(dims, *rest):
    part, chunk, blocks = dims
    halves = rest[:2], rest[2:4]
    g_all, wi, wf = rest[4:7]
    rest = rest[9:] if part == 2 else rest[7:]
    factors, g, branch, inner, outer, flat, out_sems = rest[2:9]
    width, hidden = wi.shape
    steps = hidden // chunk
    mine = range((part - 1) * steps // 2, part * steps // 2) if part else ()
    needed = (4, 5) if part else (0, 1, 2, 3)
    members = factors.shape[1] // 12
    main = members * 8
    span, half = 3 * width // 2, width // 2

    def scaled(i):
        return (factors[i].astype(f32) * g[...]).astype(bf16)

    def unpack(sources, b):
        near = iota((8, half), 0) < 4
        for i in needed:
            side, at = i // 3, slice((i % 3) * span, (i % 3 + 1) * span)
            held = []
            for d in range(members):
                if side:
                    d = (d & ~12) | ((d & 4) << 1) | ((d & 8) >> 1)
                source = sources[side][d // sources[side][0].shape[0]]
                held.append(source[d % source.shape[0], :, at].astype(f32))
            for k in range(0, members, 2):
                even, odd = held[k], held[k + 1]
                factors[i, k * 8 : (k + 2) * 8, :] = jnp.concatenate(
                    [even[:, :width], odd[:, :width]], axis=0
                ).astype(bf16)
            for k in range(0, members, 4):
                tiles = []
                for j in (k, k + 2):
                    even, odd = held[j][:, width:], held[j + 1][:, width:]
                    tiles.append(
                        jnp.concatenate(
                            [
                                jnp.where(near, even, pltpu.roll(odd, 4, 0)),
                                jnp.where(near, pltpu.roll(even, 4, 0), odd),
                            ],
                            axis=1,
                        )
                    )
                at = main + k * 4
                factors[i, at : at + 16, :] = jnp.concatenate(tiles, axis=0).astype(bf16)
        same = iota((8, 128), 1) == iota((8, 128), 0)
        more = iota((8, 128), 1) == 8 + (iota((8, 128), 0) & 3)
        for d in range(members):
            here = g_all[pl.ds(b * members + d, 1), :]
            g[d * 8 : (d + 1) * 8, :] = jnp.sum(jnp.where(same, here, 0.0), axis=1, keepdims=True)
        for d in range(0, members, 2):
            both = jnp.where(
                iota((8, 128), 0) < 4,
                g_all[pl.ds(b * members + d, 1), :],
                g_all[pl.ds(b * members + d + 1, 1), :],
            )
            at = main + d * 4
            g[at : at + 8, :] = jnp.sum(jnp.where(more, both, 0.0), axis=1, keepdims=True)
        if part:
            branch[...] = scaled(5)

    def put(target, values, b):
        if blocks == 1:
            target[...] = values
        else:
            target[...] = jnp.where(b == 0, values, target[...] + values)

    def each_block(one):
        if blocks == 1:
            one(0, 0)
        else:
            arrived, sem = rest[-2], rest[-1]

            def step(b, carry):
                for side in range(2):
                    for i in range(2):

                        @pl.when((b < blocks // 2) == (i == 0))
                        def _(side=side, i=i):
                            at = b - i * (blocks // 2)
                            load = pltpu.make_async_copy(
                                halves[side][i].at[pl.ds(at * members, members)],
                                arrived.at[side], sem,
                            )
                            load.start()
                            load.wait()

                unpack([[arrived.at[0]], [arrived.at[1]]], b)
                return one(b, carry)

            lax.fori_loop(0, blocks, step, 0)

    stores = {}

    def save(source, target, sem):
        store = pltpu.make_async_copy(source, target, out_sems.at[sem])
        store.start()
        stores[sem] = store

    if blocks == 1:
        unpack(halves, 0)
    if not part:
        for i, j, slot, target in ((0, 1, 0, rest[0]), (2, 3, 1, rest[1])):

            def square(b, carry, i=i, j=j, slot=slot):
                put(flat.at[slot], mm_tn(factors[i], scaled(j)), b)
                return carry

            each_block(square)
            save(flat.at[slot], target, 4 + slot)
    for c in mine:
        slot = c % 2
        at = slice(c * chunk, (c + 1) * chunk)

        def one(b, carry, slot=slot, at=at):
            value, slope = gelu_pair(mm(factors[4], wi[:, at]))
            grad = (mm_nt(branch[...], wf[at, :]) * slope).astype(bf16)
            put(inner.at[slot], mm_tn(factors[4], grad), b)
            put(outer.at[slot], mm_tn(value.astype(bf16), branch[...]), b)
            return carry

        each_block(one)
        save(inner.at[slot], rest[0].at[:, pl.ds(c * chunk, chunk)], slot)
        save(outer.at[slot], rest[1].at[pl.ds(c * chunk, chunk), :], 2 + slot)
    for store in stores.values():
        store.wait()


def outer_call(part, held_rows, g_all, wi, wf, held):
    low = held_rows[0]
    devices = 2 * low.shape[0]
    width, hidden = wi.shape
    chunk = hidden // 4
    members = min(devices, 32)
    blocks = devices // members
    block = members * 12
    shape = jax.ShapeDtypeStruct
    wide = [shape((width, hidden), f32), shape((hidden, width), f32)]
    flat = [shape((width, width), f32)] * 2
    place = whole if blocks == 1 else outside
    more = [] if blocks == 1 else [
        pltpu.VMEM((2, members) + low.shape[1:], bf16), pltpu.SemaphoreType.DMA
    ]
    return pl.pallas_call(
        functools.partial(outer_kernel, (part, chunk, blocks)),
        out_shape=wide if part else flat,
        in_specs=[place] * 4 + [whole] * 3 + [outside] * len(held),
        out_specs=[outside] * 2,
        input_output_aliases={7: 0, 8: 1} if held else {},
        scratch_shapes=[
            pltpu.VMEM((6, block, width), bf16),
            pltpu.VMEM((block, 1), f32),
            pltpu.VMEM((block, width), bf16),
            pltpu.VMEM((2, width, chunk), f32),
            pltpu.VMEM((2, chunk, width), f32),
            pltpu.VMEM((2, width, width), f32),
            pltpu.SemaphoreType.DMA((6,)),
        ] + more,
        compiler_params=pltpu.CompilerParams(vmem_limit_bytes=28 * mega),
        cost_estimate=pl.CostEstimate(
            flops=int(1e10), bytes_accessed=int(2e7), transcendentals=int(1e6)
        ),
        name=f"outer_{part}",
    )(*held_rows, g_all, wi, wf, *held)


def small_call(kernel, name, outs, *args):
    return pl.pallas_call(
        kernel,
        out_shape=outs,
        in_specs=[whole] * len(args),
        out_specs=[whole] * len(outs) if isinstance(outs, (list, tuple)) else whole,
        compiler_params=pltpu.CompilerParams(vmem_limit_bytes=8 * mega),
        cost_estimate=pl.CostEstimate(flops=1000, bytes_accessed=int(1e6), transcendentals=0),
        name=name,
    )(*args)


def join(mine, come):
    if mine.size > 1 << 21:
        return jnp.concatenate([mine, come], axis=0)

    def kernel(a, b, out):
        out[: a.shape[0]] = a[...]
        out[a.shape[0] :] = b[...]

    shape = (2 * mine.shape[0],) + mine.shape[1:]
    return small_call(kernel, "join", jax.ShapeDtypeStruct(shape, mine.dtype), mine, come)


def fold(keep, come):
    half = keep.shape[0] // 2

    def kernel(a, b, first, second):
        for i in range(half):
            first[i] = a[i] + b[i]
            second[i] = a[half + i] + b[half + i]

    out = jax.ShapeDtypeStruct((half,) + keep.shape[1:], keep.dtype)
    return small_call(kernel, "fold", [out, out], keep, come)


def split(mine, come):
    half = mine.shape[2] // 2

    def kernel(a, b, left, right):
        for i, part in enumerate((a, b)):
            at = slice(i * count, (i + 1) * count)
            left[at] = part[:, :, :half]
            right[at] = part[:, :, half:]

    count = mine.shape[0]
    out = jax.ShapeDtypeStruct((2 * count, mine.shape[1], half), mine.dtype)
    return small_call(kernel, "split", [out, out], mine, come)


def weave(left, come_left, right, come_right):
    half = left.shape[2]

    def kernel(a, b, c, d, out):
        for i in range(8):
            first, second, third = i >> 2, (i >> 1) & 1, i & 1
            out[i, :, :half] = (b if first else a)[2 * second + third]
            out[i, :, half:] = (d if second else c)[2 * first + third]

    out = jax.ShapeDtypeStruct((8,) + left.shape[1:2] + (2 * half,), left.dtype)
    return small_call(kernel, "weave", out, left, come_left, right, come_right)


def close(keep, come, smalls, first_sum):
    rows = keep.shape[1]

    def kernel(a, b, c, d, out):
        out[0, :rows, :] = a[0] + b[0]
        low = jnp.where(iota(c.shape, 0) == 4, d[...], c[...])
        tail = jnp.concatenate([low, jnp.zeros_like(low)], axis=0)
        out[0, rows:, :] = tail.astype(bf16)

    out = jax.ShapeDtypeStruct((1, rows + group, keep.shape[2]), keep.dtype)
    return small_call(kernel, "close", out, keep, come, smalls, first_sum)


def add(mine, come):
    def kernel(a, b, out):
        out[...] = a[...] + b[...]

    return small_call(kernel, "add", jax.ShapeDtypeStruct(mine.shape, mine.dtype), mine, come)


def last_kernel(dims, held, *rest):
    stages, part, piece, heads, buckets = dims
    half, _, width = held.shape
    if part:
        earlier, rest = rest[0], rest[3:]
    sides = rest[:2]
    values, sems = rest[-2:]
    me = own_code(stages)
    blocks = width // piece
    for i in range(half):
        owner = me ^ (part * half + i)
        at = pl.multiple_of((owner & (blocks - 1)) * piece, group)
        side_of = lax.shift_right_logical(owner, int(math.log2(blocks)))
        values[i] = held[i, :piece, :].astype(f32)
        for side in range(2):

            @pl.when(side_of == side)
            def _(side=side, at=at, i=i):
                pltpu.make_async_copy(
                    values.at[i], sides[side].at[pl.ds(at, piece), :], sems.at[i]
                ).start()

    total = sum(held[i, piece:, :].astype(f32)[:8] for i in range(half))
    if part:
        total = total + earlier[...]
        for i, out in zip((4, 0, 1, 2), rest[2:6]):
            out[...] = total[i : i + 1, :].reshape(width)
        spots = iota((width, 128), 0)
        by_bucket = jnp.where((spots & (buckets - 1)) == iota((width, 128), 1), 1.0, 0.0)
        by_head = jnp.where(
            lax.shift_right_logical(iota((group, width), 1), int(math.log2(buckets)))
            == iota((group, width), 0),
            total[3:4, :], 0.0,
        )
        table = lax.dot_general(
            by_head, by_bucket, (((1,), (0,)), ((), ())),
            precision=highest, preferred_element_type=f32,
        )
        rest[6][...] = table[:heads, :buckets]
    else:
        rest[2][...] = total
    for i in range(half):
        pltpu.make_async_copy(values.at[i], sides[0].at[pl.ds(0, piece), :], sems.at[i]).wait()


def last_call(stages, part, held, piece, buckets, heads, earlier):
    half, _, width = held.shape
    shape = jax.ShapeDtypeStruct
    squares = [shape((width, width), f32)] * 2
    more = (
        [shape((width,), f32)] * 4 + [shape((heads, buckets), f32)] if part else [shape((8, width), f32)]
    )
    return pl.pallas_call(
        functools.partial(last_kernel, (stages, part, piece, heads, buckets)),
        out_shape=squares + more,
        in_specs=[whole] * (2 if part else 1) + [outside] * (2 if part else 0),
        out_specs=[outside] * 2 + [whole] * len(more),
        input_output_aliases={2: 0, 3: 1} if part else {},
        scratch_shapes=[pltpu.VMEM((half, piece, width), f32), pltpu.SemaphoreType.DMA((half,))],
        compiler_params=pltpu.CompilerParams(vmem_limit_bytes=12 * mega),
        cost_estimate=pl.CostEstimate(flops=int(1e7), bytes_accessed=int(5e6), transcendentals=0),
        name=f"last_{part}",
    )(held, *earlier)


def shards(
    docs, lists,
    tokens, pair_lengths, list_ids, relevance,
    first_gain, query_weight, key_weight, value_weight, output_weight, bias_table,
    second_gain, inner_weight, outer_weight, final_gain, score_vector,
):
    row_count, length, width = tokens.shape[1:]
    pairs = pair_lengths.shape[2]
    buckets, heads = bias_table.shape
    devices = docs * lists
    sizes = {"docs": docs, "lists": lists}
    stages = tuple(("lists", 1 << b) for b in range(lists.bit_length() - 1)) + tuple(
        ("docs", 1 << b) for b in range(docs.bit_length() - 1)
    )

    def swap(values, stage):
        axis, mask = stage
        return lax.ppermute(values, axis, [(i, i ^ mask) for i in range(sizes[axis])])

    rows = tokens.reshape(row_count, length, width)
    lengths = pair_lengths.reshape(row_count, pairs)
    spot = lax.broadcasted_iota(jnp.int32, (group, width), 0)
    gains = jnp.pad(bias_table.T, ((4, group - 4 - heads), (0, width - buckets)))
    for i, vector in enumerate((first_gain, second_gain, final_gain, score_vector)):
        gains = jnp.where(spot == i, vector[None, :], gains)
    members = list_ids.shape[1]
    known = jnp.pad(list_ids, ((0, 0), (0, members))) + jnp.pad(relevance, ((0, 0), (members, 0)))
    outs = path_call(
        rows, lengths, known, gains, heads, buckets,
        (query_weight, key_weight, value_weight, output_weight, inner_weight, outer_weight),
    )
    pay, factors, n1, probs, dl, turned, yk, yv, qf, gctx, z, vz, ga, a2, fhat, yq = outs[:16]
    wq, wk, wv, wo, wi, wf, scores = outs[16:]

    tie = lax.optimization_barrier
    gather_order = tuple(reversed(stages))

    rows_left = list(gather_order)
    come = None
    projected, bias = [], None
    for i, stage in enumerate(gather_order):
        if i < row_count:
            n1, pay = tie((n1, pay))
            come_pay = swap(pay, stage)
            made = project_call(i, n1, wq, wk, wv)
            come_pay, made = tie((come_pay, tuple(made)))
            projected += made
        elif i == row_count:
            gains, pay = tie((gains, pay))
            come_pay = swap(pay, stage)
            bias = bias_call(heads, buckets, gains)
            come_pay, bias = tie((come_pay, bias))
        else:
            come_pay = swap(pay, stage)
        pay = join(pay, come_pay)
        if i == 0:
            factors, pay = tie((factors, pay))
            come = swap(factors, rows_left.pop(0))
        elif i == 2:
            come, pay = tie((come, pay))
            factors = join(factors, come)
            come = swap(factors, rows_left.pop(0))
    come, pay = tie((come, pay))
    left, right = split(factors, come)
    count = row_count * pairs
    dims = (stages, docs, lists, docs // 2, count, heads, buckets)
    keep, send, g_all, g_own, smalls = terms_call(
        dims, pay, z, vz, qf, gctx, turned, a2, fhat, gains
    )
    piece = keep.shape[1]
    cut = cut_stages(stages, width)
    rest = stages[len(cut) :]
    for stage in cut[:-3]:
        keep, send = fold(keep, swap(send, stage))

    third, fourth = rows_left[:2]
    bias, probs, send, left, right = tie((bias, probs, send, left, right))
    arrived = swap(send, cut[-3])
    come = swap(left, third), swap(right, fourth)
    attended = attention_call(lengths, rows, bias, wo, projected)
    grads, first_sum = tokens_grad_call(
        lengths, rows, g_own, probs, dl, yk, yv, yq, ga, gains
    )
    grads, first_sum, attended = tie((grads, first_sum, attended))
    arrived, come, attended = tie((arrived, come, attended))
    keep, send = fold(keep, arrived)
    left, right = join(left, come[0]), join(right, come[1])

    attended, send, left, right = tie((attended, send, left, right))
    arrived = swap(send, cut[-2])
    come = swap(left, fourth), swap(right, third)
    encoded = feed_call(0, attended, gains, wi, wf, None)
    arrived, encoded = tie((arrived, encoded))
    keep, send = fold(keep, arrived)

    arrived = swap(send, cut[-1])
    held = close(keep, arrived, smalls, first_sum)

    for stage in rest[:-1]:
        held = add(held, swap(held, stage))
    attended, held = tie((attended, held))
    arrived = swap(held, rest[-1])
    held, come = tie((held, come))
    left, right = join(left, come[0]), join(right, come[1])
    for stage in rows_left[2:-1]:
        left, right = join(left, swap(left, stage)), join(right, swap(right, stage))
    come = swap(left, rows_left[-1]), swap(right, rows_left[-1])
    attended, left = tie((attended, left))
    encoded = feed_call(1, attended, gains, wi, wf, encoded)
    arrived, encoded, come = tie((arrived, encoded, come))
    held = add(held, arrived)
    held_rows = (left, come[0], right, come[1])

    held, held_rows = tie((held, held_rows))
    arrived = swap(held, cut[-1])
    products = tuple(outer_call(0, held_rows, g_all, wi, wf, ()))
    products, arrived = tie((products, arrived))
    query_grad, output_grad = products
    left, right = split(held, arrived)

    left, right, held_rows = tie((left, right, held_rows))
    come = swap(left, cut[-2]), swap(right, cut[-3])
    wide = tuple(outer_call(1, held_rows, g_all, wi, wf, ()))
    wide, come = tie((wide, come))
    left, right = join(left, come[0]), join(right, come[1])

    left, right, wide = tie((left, right, wide))
    come = swap(left, cut[-3]), swap(right, cut[-2])
    wide = outer_call(2, held_rows, g_all, wi, wf, wide)
    wide, come = tie((tuple(wide), come))
    held = weave(left, come[0], right, come[1])

    for stage in reversed(cut[1:-3]):
        held = join(held, swap(held, stage))
    come = swap(held, cut[0])
    key_grad, value_grad, small_sums = last_call(cut, 0, held, piece, buckets, heads, ())
    (
        key_grad, value_grad, first_grad, second_grad, final_grad, vector_grad, table_grad
    ) = last_call(cut, 1, come, piece, buckets, heads, (small_sums, key_grad, value_grad))
    inner_grad, outer_grad = wide
    return (
        encoded.reshape(tokens.shape),
        scores.reshape(1, row_count, pairs),
        grads.reshape(tokens.shape),
        first_grad,
        query_grad,
        key_grad,
        value_grad,
        output_grad,
        table_grad.T,
        second_grad,
        inner_grad,
        outer_grad,
        final_grad,
        vector_grad,
    )


def solution(mesh):
    placed = P("lists", "docs", None, None)
    return jax.shard_map(
        functools.partial(shards, mesh.shape["docs"], mesh.shape["lists"]),
        mesh=mesh,
        in_specs=(placed, P("lists", "docs", None), P("lists", None), P("lists", None)) + (P(),) * 11,
        out_specs=(placed, P("lists", "docs", None), placed) + (P(),) * 11,
        check_vma=False,
    )
```

```python
import functools
import math

import jax
import jax.numpy as jnp
from jax import lax
from jax.experimental import pallas as pl
from jax.experimental.pallas import tpu as pltpu
from jax.sharding import PartitionSpec as P

epsilon = 1e-06
negative = -1000000000.0
highest = lax.Precision.HIGHEST
limits = (12, 16, 23, 32, 46, 64, 91)
f32 = jnp.float32
bf16 = jnp.bfloat16
window = 128
reach = 144
lanes_path = 256
group = 16
mega = 1 << 20
curve = math.sqrt(2.0 / math.pi)
cubic = 0.044715
whole = pl.BlockSpec(memory_space=pltpu.VMEM)
scalars = pl.BlockSpec(memory_space=pltpu.SMEM)
outside = pl.BlockSpec(memory_space=pl.ANY)


def mm(a, b):
    return lax.dot_general(a, b, (((1,), (0,)), ((), ())), preferred_element_type=f32)


def mm_nt(a, b):
    return lax.dot_general(a, b, (((1,), (1,)), ((), ())), preferred_element_type=f32)


def mm_tn(a, b):
    return lax.dot_general(a, b, (((0,), (0,)), ((), ())), preferred_element_type=f32)


def as_row(gains, i):
    return gains[i : i + 1, :]


def iota(shape, axis):
    return lax.broadcasted_iota(jnp.int32, shape, axis)


def bucket_of(offsets):
    upper_half = jnp.where(offsets > 0, 16, 0)
    distance = jnp.abs(offsets)
    beyond = jnp.full(offsets.shape, 8, jnp.int32)
    for border in limits:
        beyond = beyond + jnp.where(distance >= border, 1, 0)
    return upper_half + jnp.where(distance < 8, distance, beyond)


def rms_factor(values):
    return lax.rsqrt(jnp.mean(values * values, axis=-1, keepdims=True) + epsilon)


def norm_back(normed, factor, upstream):
    return factor * (upstream - normed * jnp.mean(upstream * normed, axis=-1, keepdims=True))


def half_bent(values, square):
    return 0.5 * jnp.tanh(values * (square * (curve * cubic) + curve)) + 0.5


def gelu(values):
    return values * half_bent(values, values * values)


def gelu_pair(values):
    square = values * values
    half = half_bent(values, square)
    value = half * values
    steep = (value - value * half) * (square * (6.0 * curve * cubic) + 2.0 * curve)
    return value, half + steep


def bias_vector(table, lanes, origin):
    buckets = table.shape[1]
    buckets_at = bucket_of(iota((buckets, lanes), 1) - origin)
    chosen = jnp.where(buckets_at == iota((buckets, lanes), 0), 1.0, 0.0)
    return lax.dot_general(
        table, chosen, (((1,), (0,)), ((), ())), precision=highest, preferred_element_type=f32
    )


def cast_rows(target, source, chunk):
    rows = source.shape[0]

    def step(i, carry):
        at = pl.ds(pl.multiple_of(i * chunk, chunk), chunk)
        target[at, :] = source[at, :].astype(bf16)
        return carry

    lax.fori_loop(0, rows // chunk, step, 0)


def starts_of(lengths, row, count):
    out, at = [], 0
    for i in range(count):
        out.append((at, lengths[row, i]))
        at = at + lengths[row, i]
    return out


def path_kernel(
    dims,
    lengths, known,
    tokens_in, gains,
    wq_in, wk_in, wv_in, wo_in, wi_in, wf_in,
    pay, factors, n1_out, probs_out, dl_out, turned_out, yk_out, yv_out, qf_out, gctx_out, z_out, vz_out,
    ga_out, a2_out, fhat_out, yq_out,
    wq, wk, wv, wo, wi, wf, scores_out,
    tokens, square, padded, first, gather_z, logits, expand, wide_z,
    in_sems, tokens_sem,
):
    rows, length, width, pairs, heads, buckets = dims
    members = known.shape[1] // 2
    count = rows * pairs
    parts = wi.shape[1] // width
    slots = square.shape[0]
    chunks = [(wq_in, wq), (wk_in, wk), (wv_in, wv), (wo_in, wo)]
    for i in range(parts):
        at = pl.ds(i * width, width)
        chunks.append((wi_in.at[:, at], wi.at[:, at]))
    for i in range(parts):
        at = pl.ds(i * width, width)
        chunks.append((wf_in.at[at, :], wf.at[at, :]))

    def load_of(i):
        return pltpu.make_async_copy(chunks[i][0], square.at[i % slots], in_sems.at[i % slots])

    tokens_load = pltpu.make_async_copy(tokens_in, tokens, tokens_sem)
    tokens_load.start()
    order = iter(range(slots))

    def request(count):
        for _ in range(count):
            load_of(next(order)).start()

    request(2)
    tokens_load.wait()
    request(2)

    gain = as_row(gains, 0)
    for r in range(rows):
        padded[r, length:, :] = jnp.zeros((reach, width), bf16)

        def norm_step(i, carry, r=r):
            at = pl.ds(pl.multiple_of(i * 64, 64), 64)
            x = tokens[r, at, :]
            n = (x * rms_factor(x) * gain).astype(bf16)
            n1_out[r, at, :] = n
            padded[r, at, :] = n
            return carry

        lax.fori_loop(0, length // 64, norm_step, 0)
        request(2)
    first[...] = jnp.zeros(first.shape, f32)
    pieces = []
    for r in range(rows):
        for at, size in starts_of(lengths, r, pairs):
            p = len(pieces)
            shift = at & (group - 1)
            pieces.append((r, pl.multiple_of(at - shift, group), shift, size))
            first[p : p + 1, :] = tokens[r, pl.ds(at, 1), :]

    def nearby(p):
        r, base, _, _ = pieces[p]
        return padded[r, pl.ds(base, reach), :]

    spots = [slice(p * group, (p + 1) * group) for p in range(count)]
    head_rows = iota((group, width), 0) == lax.shift_right_logical(
        iota((group, width), 1), int(math.log2(width // heads))
    )

    def widen(values):
        for p in range(count):
            expand[p * group : (p + 1) * group, :] = jnp.where(
                head_rows, values[p : p + 1, :], 0.0
            ).astype(bf16)

    def narrow(target):
        target[...] = jnp.zeros(target.shape, f32)
        for p in range(count):
            block = wide_z[p * group : (p + 1) * group, :]
            target[p : p + 1, :] = jnp.sum(
                jnp.where(head_rows, block, 0.0), axis=0, keepdims=True
            )

    def take(i):
        load_of(i).wait()
        cast_rows(chunks[i][1], square.at[i % slots], 64)
        if i < 4:
            request(1)

    take(0)
    n1_first = (first[...] * rms_factor(first[...]) * gain).astype(bf16)
    q_first = mm(n1_first, wq[...]).astype(bf16)
    qf_out[...] = q_first
    widen(q_first.astype(f32))
    take(1)
    yk_out[...] = mm_nt(expand[...], wk[...]).astype(bf16)
    position = bias_vector(gains[4 : 4 + heads, :buckets], lanes_path, 0)
    position = jnp.concatenate([position, jnp.zeros((group - heads, lanes_path), f32)], axis=0)
    lane = iota((group, lanes_path), 1)
    for p, (_, _, shift, size) in enumerate(pieces):
        logits[spots[p], :reach] = mm_nt(yk_out[spots[p], :], nearby(p))
        block = logits[spots[p], :] + pltpu.roll(position, shift, 1)
        inside = jnp.logical_and(lane >= shift, lane < shift + size)
        logits[spots[p], :] = jnp.where(inside, block, negative)
    take(2)
    take(3)
    scores_in = logits[...]
    peak = jnp.max(scores_in, axis=-1, keepdims=True)
    raised = jnp.exp(scores_in - peak)
    probs = raised / jnp.sum(raised, axis=-1, keepdims=True)
    probs_out[...] = probs.astype(bf16)
    for p in range(count):
        vz_out[spots[p], :] = mm(probs_out[spots[p], :reach], nearby(p)).astype(bf16)
    wide_z[...] = mm(vz_out[...], wv[...])
    narrow(gather_z)
    context = gather_z[...].astype(bf16)
    attended = first[...] + mm(context, wo[...])
    scale_two = rms_factor(attended)
    second = attended * scale_two
    normed_two = (second * as_row(gains, 1)).astype(bf16)
    for i in range(parts):
        take(4 + i)
    value, slope = gelu_pair(mm(normed_two, wi[...]))
    for i in range(parts):
        take(4 + parts + i)
    encoded = attended + mm(value.astype(bf16), wf[...])
    scale_final = rms_factor(encoded)
    final_hat = encoded * scale_final
    fhat_out[...] = final_hat
    unit = as_row(gains, 3) * as_row(gains, 2)
    score_col = jnp.sum(final_hat * unit, axis=-1, keepdims=True)
    square_lane = iota((group, 128), 1)
    row = jnp.sum(
        jnp.where(square_lane == iota((group, 128), 0), score_col, 0.0), axis=0, keepdims=True
    )
    for r in range(rows):
        scores_out[r : r + 1, :] = row[:, r * pairs : (r + 1) * pairs]
    row_lane = iota((1, 128), 1)
    place = lax.axis_index("docs") * count
    for i in range(count):
        row = jnp.where(row_lane == group + i, known[0, place + i].astype(f32), row)
        row = jnp.where(row_lane == 2 * group + i, known[0, members + place + i].astype(f32), row)
    pay[...] = row

    grad_encoded = norm_back(final_hat, scale_final, jnp.broadcast_to(unit, final_hat.shape))
    grad_branch = grad_encoded.astype(bf16)
    grad_preact = (mm_nt(grad_branch, wf[...]) * slope).astype(bf16)
    grad_normed_two = mm_nt(grad_preact, wi[...])
    a2_out[...] = second * grad_normed_two
    grad_attended = grad_encoded + norm_back(second, scale_two, grad_normed_two * as_row(gains, 1))
    ga_out[...] = grad_attended
    grad_attn = grad_attended.astype(bf16)
    grad_context = mm_nt(grad_attn, wo[...])
    gctx_out[...] = grad_context
    widen(grad_context)
    yv_out[...] = mm_nt(expand[...], wv[...]).astype(bf16)
    logits[...] = jnp.zeros(logits.shape, f32)
    for p in range(count):
        logits[spots[p], :reach] = mm_nt(yv_out[spots[p], :], nearby(p))
    grad_probs = logits[...]
    grad_logits = probs * (grad_probs - jnp.sum(probs * grad_probs, axis=-1, keepdims=True))
    dl_out[...] = grad_logits.astype(bf16)
    for p, (_, _, shift, _) in enumerate(pieces):
        rounded = dl_out[spots[p], :]
        z_out[spots[p], :] = mm(rounded[:, :reach], nearby(p))
        turned = pltpu.roll(rounded.astype(f32), (lanes_path - shift) & (lanes_path - 1), 1)
        turned_out[spots[p], :] = turned[:, :window]
    wide_z[...] = mm(z_out[...].astype(bf16), wk[...])
    narrow(gather_z)
    grad_query = gather_z[...].astype(bf16)
    yq_out[...] = mm_nt(grad_query, wq[...])
    span, half = 3 * width // 2, width // 2
    for i, member in enumerate((n1_first, grad_query, context, grad_attn, normed_two, grad_branch)):
        member = member.astype(f32)
        tail = member[8:, :]
        tail = jnp.where(
            iota((8, half), 0) < 4, tail[:, :half], pltpu.roll(tail[:, half:], 4, 0)
        )
        factors[0, :, i * span : i * span + width] = member[:8].astype(bf16)
        factors[0, :, i * span + width : (i + 1) * span] = tail.astype(bf16)


def path_call(tokens, lengths, known, gains, heads, buckets, weights):
    rows, length, width = tokens.shape
    pairs = lengths.shape[1]
    combos = rows * pairs * group
    shape = jax.ShapeDtypeStruct
    outs = [
        shape((1, 128), f32),
        shape((1, 8, 9 * width), bf16),
        shape((rows, length, width), bf16),
        shape((combos, lanes_path), bf16),
        shape((combos, lanes_path), bf16),
        shape((combos, window), f32),
        shape((combos, width), bf16),
        shape((combos, width), bf16),
        shape((group, width), bf16),
        shape((group, width), f32),
        shape((combos, width), f32),
        shape((combos, width), bf16),
        shape((group, width), f32),
        shape((group, width), f32),
        shape((group, width), f32),
        shape((group, width), f32),
    ]
    low = [shape(w.shape, bf16) for w in weights] + [shape((rows, pairs), f32)]
    return pl.pallas_call(
        functools.partial(path_kernel, (rows, length, width, pairs, heads, buckets)),
        out_shape=outs + low,
        in_specs=[scalars] * 2 + [outside, whole] + [outside] * 6,
        out_specs=[whole] * (len(outs) + len(low)),
        scratch_shapes=[
            pltpu.VMEM(tokens.shape, f32),
            pltpu.VMEM((12, width, width), f32),
            pltpu.VMEM((rows, length + reach, width), bf16),
            pltpu.VMEM((group, width), f32),
            pltpu.VMEM((group, width), f32),
            pltpu.VMEM((combos, lanes_path), f32),
            pltpu.VMEM((combos, width), bf16),
            pltpu.VMEM((combos, width), f32),
            pltpu.SemaphoreType.DMA((12,)),
            pltpu.SemaphoreType.DMA,
        ],
        compiler_params=pltpu.CompilerParams(vmem_limit_bytes=45 * mega),
        cost_estimate=pl.CostEstimate(flops=int(9e9), bytes_accessed=int(5e7), transcendentals=0),
        name="path",
    )(lengths, known, tokens, gains, *weights)


def code_of(stages, indices):
    total = len(stages)
    code = 0
    for s, (axis, mask) in enumerate(stages):
        bit = jnp.where((indices[axis] & mask) != 0, 1, 0) if not isinstance(
            indices[axis], int
        ) else (1 if indices[axis] & mask else 0)
        code = code + bit * (1 << (total - 1 - s))
    return code


def cut_stages(stages, width):
    count = 3 + sum(axis == "lists" for axis, _ in stages)
    while (2 * width) % (group << count):
        count -= 1
    return stages[:count]


def own_code(stages):
    return code_of(stages, {axis: lax.axis_index(axis) for axis in ("docs", "lists")})


def terms_kernel(
    dims,
    pay, z, vz, qf, gctx, dl, a2, fhat, gains,
    keep, send, g_all, g_own, smalls,
    term, left, right,
):
    stages, docs, lists, list_count, count, heads, buckets = dims
    width = z.shape[1]
    everything = pay[...]
    lane = iota(everything.shape, 1)
    score = everything
    names = pltpu.roll(everything, 128 - group, 1)
    label = pltpu.roll(everything, 128 - 2 * group, 1)
    used = lane < count
    part = lax.shift_right_logical(iota(everything.shape, 0), int(math.log2(docs)))
    key = jnp.where(used, part * list_count + names.astype(jnp.int32), -1)

    def total_of(values):
        return jnp.sum(jnp.sum(values, axis=1, keepdims=True), axis=0, keepdims=True)

    def top_step(k, top):
        member = key == k
        best = jnp.max(
            jnp.max(jnp.where(member, score, negative), axis=1, keepdims=True),
            axis=0, keepdims=True,
        )
        return jnp.where(member, best, top)

    keys = lists * list_count
    unroll = keys if keys <= 16 else 4
    top = lax.fori_loop(0, keys, top_step, score, unroll=unroll)
    raised = jnp.exp(score - top)

    def sum_step(k, carry):
        total, gain = carry
        member = key == k
        return (
            jnp.where(member, total_of(jnp.where(member, raised, 0.0)), total),
            jnp.where(member, total_of(jnp.where(member, label, 0.0)), gain),
        )

    ones = jnp.ones(everything.shape, f32)
    total, gain = lax.fori_loop(0, keys, sum_step, (ones, ones), unroll=unroll)
    grads = jnp.where(used, raised / total * gain - label, 0.0)
    g_all[...] = grads
    own = grads[0:1, :]
    g_own[...] = jnp.broadcast_to(own, g_own.shape)

    combos = count * group
    pair_of = lax.shift_right_logical(iota((combos, 128), 0), int(math.log2(group)))
    g_combo = jnp.sum(jnp.where(iota((combos, 128), 1) == pair_of, own, 0.0), axis=1, keepdims=True)
    g_pair = jnp.sum(
        jnp.where(iota((group, 128), 1) == iota((group, 128), 0), own, 0.0), axis=1, keepdims=True
    )
    head_rows = iota((group, width), 0) == lax.shift_right_logical(
        iota((group, width), 1), int(math.log2(width // heads))
    )
    queries = qf[...].astype(f32)
    upstream = gctx[...] * g_pair
    for p in range(count):
        at = slice(p * group, (p + 1) * group)
        right[0, at, :] = jnp.where(head_rows, queries[p : p + 1, :], 0.0).astype(bf16)
        right[1, at, :] = jnp.where(head_rows, upstream[p : p + 1, :], 0.0).astype(bf16)
    left[...] = (z[...] * g_combo).astype(bf16)
    term[0:width, :] = mm_tn(left[...], right[0])
    term[width : 2 * width, :] = mm_tn(vz[...], right[1])

    half, piece = keep.shape[0], keep.shape[1]
    blocks = width // piece
    mine = own_code(stages[: half.bit_length()])

    def piece_step(r, carry, target, base):
        owner = mine ^ (base + r)
        side = lax.shift_right_logical(owner, int(math.log2(blocks)))
        at = side * width + (owner & (blocks - 1)) * piece
        target[r] = term[pl.ds(pl.multiple_of(at, group), piece), :].astype(bf16)
        return carry

    lax.fori_loop(0, half, functools.partial(piece_step, target=send, base=half), 0)
    lax.fori_loop(0, half, functools.partial(piece_step, target=keep, base=0), 0)

    smalls[...] = jnp.zeros(smalls.shape, f32)
    smalls[0:1, :] = jnp.sum(a2[...] * g_pair, axis=0, keepdims=True)
    hats = jnp.sum(fhat[...] * g_pair, axis=0, keepdims=True)
    smalls[1:2, :] = hats * as_row(gains, 3)
    smalls[2:3, :] = hats * as_row(gains, 2)
    weighted = dl[...] * g_combo
    summed = weighted[0:group, :]
    for p in range(1, count):
        summed = summed + weighted[p * group : (p + 1) * group, :]
    spots = iota((window, width), 1)
    hot = jnp.where(bucket_of(iota((window, width), 0)) == (spots & (buckets - 1)), 1.0, 0.0)
    spread = lax.dot_general(
        summed, hot, (((1,), (0,)), ((), ())), precision=highest, preferred_element_type=f32
    )
    row_of = lax.shift_right_logical(iota((group, width), 1), int(math.log2(buckets)))
    smalls[3:4, :] = jnp.sum(
        jnp.where(row_of == iota((group, width), 0), spread, 0.0), axis=0, keepdims=True
    )


def terms_call(dims, pay, z, vz, qf, gctx, dl, a2, fhat, gains):
    stages, docs, lists, list_count, count, heads, buckets = dims
    devices = docs * lists
    combos, width = z.shape
    pieces = 1 << len(cut_stages(stages, width))
    piece = 2 * width // pieces
    shape = jax.ShapeDtypeStruct
    half = shape((pieces // 2, piece, width), bf16)
    return pl.pallas_call(
        functools.partial(terms_kernel, dims),
        out_shape=[
            half, half,
            shape((devices, 128), f32),
            shape((8, 128), f32),
            shape((8, width), f32),
        ],
        in_specs=[whole] * 9,
        out_specs=[whole] * 5,
        scratch_shapes=[
            pltpu.VMEM((2 * width, width), f32),
            pltpu.VMEM((combos, width), bf16),
            pltpu.VMEM((2, combos, width), bf16),
        ],
        compiler_params=pltpu.CompilerParams(vmem_limit_bytes=10 * mega),
        cost_estimate=pl.CostEstimate(flops=int(4e9), bytes_accessed=int(1e7), transcendentals=0),
        name="terms",
    )(pay, z, vz, qf, gctx, dl, a2, fhat, gains)


def project_kernel(row, n1, wq, wk, wv, q, k, v):
    for target, low in ((q, wq), (k, wk), (v, wv)):
        target[...] = mm(n1[row], low[...]).astype(bf16)


def project_call(row, n1, wq, wk, wv):
    return pl.pallas_call(
        functools.partial(project_kernel, row),
        out_shape=[jax.ShapeDtypeStruct(n1.shape[1:], bf16)] * 3,
        in_specs=[whole] * 4,
        out_specs=[whole] * 3,
        compiler_params=pltpu.CompilerParams(vmem_limit_bytes=12 * mega),
        cost_estimate=pl.CostEstimate(flops=int(2e9), bytes_accessed=int(4e6), transcendentals=0),
        name=f"project_{row}",
    )(n1, wq, wk, wv)


def bias_kernel(heads, buckets, gains, bias):
    lanes = 4 * window
    vector = bias_vector(gains[4 : 4 + heads, :buckets], lanes, window)
    for h in range(heads):
        bias[h] = pltpu.roll(
            jnp.broadcast_to(vector[h : h + 1, :], (window, lanes)), 0, 1, stride=1, stride_axis=0
        )[:, : 3 * window]


def bias_call(heads, buckets, gains):
    return small_call(
        functools.partial(bias_kernel, heads, buckets), "bias",
        jax.ShapeDtypeStruct((heads, window, 3 * window), f32), gains,
    )


def attention_kernel(
    lengths, tokens_in, bias, wo, *rest
):
    out, tokens, ctx, qseg, kseg, sem = rest[-6:]
    rows, length, width = tokens.shape
    heads = bias.shape[0]
    pairs = lengths.shape[1]
    load = pltpu.make_async_copy(tokens_in, tokens, sem)
    load.start()
    tiles = length // window
    half = iota((2 * window, window), 1) < (width // heads)
    left = half[:window]
    upper = iota((2 * window, window), 0) < window
    chosen = half == upper

    def segment(positions, ends):
        total = jnp.zeros(positions.shape, jnp.int32)
        for end in ends:
            total = total + jnp.where(positions >= end, 1, 0)
        return total

    wide = iota((length, window), 1)
    units = []
    for row in range(rows):
        for j in range(tiles):
            for pair in range(heads // 2):
                units.append((row, j, pair))
    ones = jnp.ones((3 * window, window), bf16)

    def begin(row):
        ends = [at + size for at, size in starts_of(lengths, row, pairs)]
        seg = segment(iota((length, 1), 0), ends)
        qseg[...] = jnp.where(seg == wide, 1.0, 0.0).astype(bf16)
        kseg[...] = jnp.where(jnp.logical_and(seg != wide, wide <= pairs), negative, 0.0).astype(bf16)

    def spans(j):
        t0 = j * window
        k0 = max(j - 1, 0) * window
        k1 = min(j + 2, tiles) * window
        return t0, k0, k1

    def raw_of(row, j, pair):
        t0, k0, k1 = spans(j)
        cols = slice(pair * window, (pair + 1) * window)
        both = rest[3 * row][t0 : t0 + window, cols]
        stacked = jnp.concatenate([both, both], axis=0)
        stacked = jnp.where(chosen, stacked, jnp.zeros_like(stacked))
        mark = qseg[t0 : t0 + window, :]
        return mm_nt(
            jnp.concatenate([stacked, jnp.concatenate([mark, mark], axis=0)], axis=1),
            jnp.concatenate([rest[3 * row + 1][k0:k1, cols], kseg[k0:k1, :]], axis=1),
        )

    def finish(row, j, pair, raw):
        t0, k0, k1 = spans(j)
        off = k0 - (t0 - window)
        cols = slice(pair * window, (pair + 1) * window)
        probs = []
        for side in range(2):
            part = raw[side * window : (side + 1) * window]
            part = part + bias[2 * pair + side, :, off : off + k1 - k0]
            peak = jnp.max(part, axis=-1, keepdims=True)
            probs.append(jnp.exp(part - peak).astype(bf16))
        mixed = mm(
            jnp.concatenate(probs, axis=0),
            jnp.concatenate([rest[3 * row + 2][k0:k1, cols], ones[: k1 - k0]], axis=1),
        )
        ctx[t0 : t0 + window, cols] = jnp.where(
            left,
            mixed[:window, :window] / mixed[:window, window:],
            mixed[window:, :window] / mixed[window:, window:],
        ).astype(bf16)

    def close_row(row):
        if row == 0:
            load.wait()
        out[row] = tokens[row] + mm(ctx[...], wo[...])

    for row in range(rows):
        begin(row)
        last = None
        for unit in units:
            if unit[0] != row:
                continue
            raw = raw_of(*unit)
            if last is not None:
                finish(*last)
            last = unit + (raw,)
        finish(*last)
        close_row(row)


def attention_call(lengths, tokens, bias, wo, projected):
    rows, length, width = tokens.shape
    return pl.pallas_call(
        attention_kernel,
        out_shape=jax.ShapeDtypeStruct(tokens.shape, f32),
        in_specs=[scalars, outside] + [whole] * (2 + len(projected)),
        out_specs=whole,
        scratch_shapes=[
            pltpu.VMEM(tokens.shape, f32),
            pltpu.VMEM((length, width), bf16),
            pltpu.VMEM((length, window), bf16),
            pltpu.VMEM((length, window), bf16),
            pltpu.SemaphoreType.DMA,
        ],
        compiler_params=pltpu.CompilerParams(vmem_limit_bytes=14 * mega),
        cost_estimate=pl.CostEstimate(
            flops=int(1e10), bytes_accessed=int(1e7), transcendentals=int(8e6)
        ),
        name="attention",
    )(lengths, tokens, bias, wo, *projected)


def feed_kernel(row, attended, gains, wi, wf, held, out, normed, total, sem):
    length, width = total.shape
    tile, chunk = 256, 512
    x = attended[row]
    normed[...] = (x * rms_factor(x) * as_row(gains, 1)).astype(bf16)
    total[...] = x

    def finish(t, c, ahead):
        total[t, :] += mm(gelu(ahead).astype(bf16), wf[c, :])

    last = None
    for c in range(wi.shape[1] // chunk):
        for t in range(length // tile):
            t_at, c_at = slice(t * tile, (t + 1) * tile), slice(c * chunk, (c + 1) * chunk)
            ahead = mm(normed[t_at, :], wi[:, c_at])
            if last is not None:
                finish(*last)
            last = (t_at, c_at, ahead)
    finish(*last)
    store = pltpu.make_async_copy(total, out.at[row], sem)
    store.start()
    store.wait()


def feed_call(row, attended, gain, wi, wf, held):
    rows, length, width = attended.shape
    extra = [] if held is None else [held]
    kernel = functools.partial(feed_kernel, row)
    if held is None:
        kernel = lambda a, g, i, f, *rest: feed_kernel(row, a, g, i, f, None, *rest)
    return pl.pallas_call(
        kernel,
        out_shape=jax.ShapeDtypeStruct(attended.shape, f32),
        in_specs=[whole] * 4 + [outside] * len(extra),
        out_specs=outside,
        input_output_aliases={4: 0} if extra else {},
        scratch_shapes=[
            pltpu.VMEM((length, width), bf16),
            pltpu.VMEM((length, width), f32),
            pltpu.SemaphoreType.DMA,
        ],
        compiler_params=pltpu.CompilerParams(vmem_limit_bytes=12 * mega),
        cost_estimate=pl.CostEstimate(
            flops=int(1e10), bytes_accessed=int(1e7), transcendentals=int(3e6)
        ),
        name=f"feed_{row}",
    )(attended, gain, wi, wf, *extra)


def tokens_grad_kernel(
    dims, lengths, tokens_in, g_own, probs, dl, yk, yv, yq, ga, gains,
    out, first_sum, tokens, spread, sems,
):
    rows, length, width, pairs = dims
    loads = [
        pltpu.make_async_copy(tokens_in.at[r], tokens.at[r], sems.at[r]) for r in range(rows)
    ]
    for load in loads:
        load.start()
    own = g_own[0:1, :]
    lane = iota((1, 128), 1)
    total = jnp.zeros((1, width), f32)
    stores = []
    for r in range(rows):
        spread[...] = jnp.zeros(spread.shape, f32)
        starts = starts_of(lengths, r, pairs)
        amounts = []
        for i, (at, size) in enumerate(starts):
            pair = r * pairs + i
            amount = jnp.sum(jnp.where(lane == pair, own, 0.0), axis=1, keepdims=True)
            amounts.append(amount)
            here = slice(pair * group, (pair + 1) * group)
            left = jnp.concatenate([dl[here, :], probs[here, :]], axis=0)
            right = jnp.concatenate([yk[here, :], yv[here, :]], axis=0)
            base = pl.multiple_of(at - (at & (group - 1)), group)
            spread[pl.ds(base, reach), :] += mm_tn(left, right)[:reach] * amount
        for i, (at, size) in enumerate(starts):
            pair = r * pairs + i
            spread[pl.ds(at, 1), :] += yq[pair : pair + 1, :] * amounts[i]
        loads[r].wait()
        gain_row = as_row(gains, 0)

        def step(i, carry, r=r, gain_row=gain_row):
            at = pl.ds(pl.multiple_of(i * 64, 64), 64)
            x = tokens[r, at, :]
            factor = rms_factor(x)
            hat = x * factor
            upstream = spread[at, :]
            tokens[r, at, :] = norm_back(hat, factor, upstream * gain_row)
            return carry + jnp.sum(hat * upstream, axis=0, keepdims=True)

        total = lax.fori_loop(0, length // 64, step, total)
        for i, (at, size) in enumerate(starts):
            pair = r * pairs + i
            tokens[r, pl.ds(at, 1), :] += ga[pair : pair + 1, :] * amounts[i]
        store = pltpu.make_async_copy(tokens.at[r], out.at[r], sems.at[r])
        store.start()
        stores.append(store)
    first_sum[...] = total
    for store in stores:
        store.wait()


def tokens_grad_call(lengths, tokens, g_own, probs, dl, yk, yv, yq, ga, gain):
    rows, length, width = tokens.shape
    pairs = lengths.shape[1]
    return pl.pallas_call(
        functools.partial(tokens_grad_kernel, (rows, length, width, pairs)),
        out_shape=[
            jax.ShapeDtypeStruct(tokens.shape, f32),
            jax.ShapeDtypeStruct((1, width), f32),
        ],
        in_specs=[scalars, outside] + [whole] * 8,
        out_specs=[outside, whole],
        scratch_shapes=[
            pltpu.VMEM(tokens.shape, f32),
            pltpu.VMEM((length + reach, width), f32),
            pltpu.SemaphoreType.DMA((rows,)),
        ],
        compiler_params=pltpu.CompilerParams(vmem_limit_bytes=12 * mega),
        cost_estimate=pl.CostEstimate(flops=int(2e9), bytes_accessed=int(1e7), transcendentals=0),
        name="tokens_grad",
    )(lengths, tokens, g_own, probs, dl, yk, yv, yq, ga, gain)


def outer_kernel(dims, *rest):
    part, chunk, blocks = dims
    halves = rest[:2], rest[2:4]
    g_all, wi, wf = rest[4:7]
    rest = rest[9:] if part == 2 else rest[7:]
    factors, g, branch, inner, outer, flat, out_sems = rest[2:9]
    width, hidden = wi.shape
    steps = hidden // chunk
    mine = range((part - 1) * steps // 2, part * steps // 2) if part else ()
    needed = (4, 5) if part else (0, 1, 2, 3)
    members = factors.shape[1] // 12
    main = members * 8
    span, half = 3 * width // 2, width // 2

    def scaled(i):
        return (factors[i].astype(f32) * g[...]).astype(bf16)

    def unpack(sources, b):
        near = iota((8, half), 0) < 4
        for i in needed:
            side, at = i // 3, slice((i % 3) * span, (i % 3 + 1) * span)
            held = []
            for d in range(members):
                if side:
                    d = (d & ~12) | ((d & 4) << 1) | ((d & 8) >> 1)
                source = sources[side][d // sources[side][0].shape[0]]
                held.append(source[d % source.shape[0], :, at].astype(f32))
            for k in range(0, members, 2):
                even, odd = held[k], held[k + 1]
                factors[i, k * 8 : (k + 2) * 8, :] = jnp.concatenate(
                    [even[:, :width], odd[:, :width]], axis=0
                ).astype(bf16)
            for k in range(0, members, 4):
                tiles = []
                for j in (k, k + 2):
                    even, odd = held[j][:, width:], held[j + 1][:, width:]
                    tiles.append(
                        jnp.concatenate(
                            [
                                jnp.where(near, even, pltpu.roll(odd, 4, 0)),
                                jnp.where(near, pltpu.roll(even, 4, 0), odd),
                            ],
                            axis=1,
                        )
                    )
                at = main + k * 4
                factors[i, at : at + 16, :] = jnp.concatenate(tiles, axis=0).astype(bf16)
        same = iota((8, 128), 1) == iota((8, 128), 0)
        more = iota((8, 128), 1) == 8 + (iota((8, 128), 0) & 3)
        for d in range(members):
            here = g_all[pl.ds(b * members + d, 1), :]
            g[d * 8 : (d + 1) * 8, :] = jnp.sum(jnp.where(same, here, 0.0), axis=1, keepdims=True)
        for d in range(0, members, 2):
            both = jnp.where(
                iota((8, 128), 0) < 4,
                g_all[pl.ds(b * members + d, 1), :],
                g_all[pl.ds(b * members + d + 1, 1), :],
            )
            at = main + d * 4
            g[at : at + 8, :] = jnp.sum(jnp.where(more, both, 0.0), axis=1, keepdims=True)
        if part:
            branch[...] = scaled(5)

    def put(target, values, b):
        if blocks == 1:
            target[...] = values
        else:
            target[...] = jnp.where(b == 0, values, target[...] + values)

    def each_block(one):
        if blocks == 1:
            one(0, 0)
        else:
            arrived, sem = rest[-2], rest[-1]

            def step(b, carry):
                for side in range(2):
                    for i in range(2):

                        @pl.when((b < blocks // 2) == (i == 0))
                        def _(side=side, i=i):
                            at = b - i * (blocks // 2)
                            load = pltpu.make_async_copy(
                                halves[side][i].at[pl.ds(at * members, members)],
                                arrived.at[side], sem,
                            )
                            load.start()
                            load.wait()

                unpack([[arrived.at[0]], [arrived.at[1]]], b)
                return one(b, carry)

            lax.fori_loop(0, blocks, step, 0)

    stores = {}

    def save(source, target, sem):
        store = pltpu.make_async_copy(source, target, out_sems.at[sem])
        store.start()
        stores[sem] = store

    if blocks == 1:
        unpack(halves, 0)
    if not part:
        for i, j, slot, target in ((0, 1, 0, rest[0]), (2, 3, 1, rest[1])):

            def square(b, carry, i=i, j=j, slot=slot):
                put(flat.at[slot], mm_tn(factors[i], scaled(j)), b)
                return carry

            each_block(square)
            save(flat.at[slot], target, 4 + slot)
    for c in mine:
        slot = c % 2
        at = slice(c * chunk, (c + 1) * chunk)

        def one(b, carry, slot=slot, at=at):
            value, slope = gelu_pair(mm(factors[4], wi[:, at]))
            grad = (mm_nt(branch[...], wf[at, :]) * slope).astype(bf16)
            put(inner.at[slot], mm_tn(factors[4], grad), b)
            put(outer.at[slot], mm_tn(value.astype(bf16), branch[...]), b)
            return carry

        each_block(one)
        save(inner.at[slot], rest[0].at[:, pl.ds(c * chunk, chunk)], slot)
        save(outer.at[slot], rest[1].at[pl.ds(c * chunk, chunk), :], 2 + slot)
    for store in stores.values():
        store.wait()


def outer_call(part, held_rows, g_all, wi, wf, held):
    low = held_rows[0]
    devices = 2 * low.shape[0]
    width, hidden = wi.shape
    chunk = hidden // 4
    members = min(devices, 32)
    blocks = devices // members
    block = members * 12
    shape = jax.ShapeDtypeStruct
    wide = [shape((width, hidden), f32), shape((hidden, width), f32)]
    flat = [shape((width, width), f32)] * 2
    place = whole if blocks == 1 else outside
    more = [] if blocks == 1 else [
        pltpu.VMEM((2, members) + low.shape[1:], bf16), pltpu.SemaphoreType.DMA
    ]
    return pl.pallas_call(
        functools.partial(outer_kernel, (part, chunk, blocks)),
        out_shape=wide if part else flat,
        in_specs=[place] * 4 + [whole] * 3 + [outside] * len(held),
        out_specs=[outside] * 2,
        input_output_aliases={7: 0, 8: 1} if held else {},
        scratch_shapes=[
            pltpu.VMEM((6, block, width), bf16),
            pltpu.VMEM((block, 1), f32),
            pltpu.VMEM((block, width), bf16),
            pltpu.VMEM((2, width, chunk), f32),
            pltpu.VMEM((2, chunk, width), f32),
            pltpu.VMEM((2, width, width), f32),
            pltpu.SemaphoreType.DMA((6,)),
        ] + more,
        compiler_params=pltpu.CompilerParams(vmem_limit_bytes=28 * mega),
        cost_estimate=pl.CostEstimate(
            flops=int(1e10), bytes_accessed=int(2e7), transcendentals=int(1e6)
        ),
        name=f"outer_{part}",
    )(*held_rows, g_all, wi, wf, *held)


def small_call(kernel, name, outs, *args):
    return pl.pallas_call(
        kernel,
        out_shape=outs,
        in_specs=[whole] * len(args),
        out_specs=[whole] * len(outs) if isinstance(outs, (list, tuple)) else whole,
        compiler_params=pltpu.CompilerParams(vmem_limit_bytes=8 * mega),
        cost_estimate=pl.CostEstimate(flops=1000, bytes_accessed=int(1e6), transcendentals=0),
        name=name,
    )(*args)


def join(mine, come):
    if mine.size > 1 << 21:
        return jnp.concatenate([mine, come], axis=0)

    def kernel(a, b, out):
        out[: a.shape[0]] = a[...]
        out[a.shape[0] :] = b[...]

    shape = (2 * mine.shape[0],) + mine.shape[1:]
    return small_call(kernel, "join", jax.ShapeDtypeStruct(shape, mine.dtype), mine, come)


def fold(keep, come):
    half = keep.shape[0] // 2

    def kernel(a, b, first, second):
        for i in range(half):
            first[i] = a[i] + b[i]
            second[i] = a[half + i] + b[half + i]

    out = jax.ShapeDtypeStruct((half,) + keep.shape[1:], keep.dtype)
    return small_call(kernel, "fold", [out, out], keep, come)


def fold_columns(keep, come):
    half = keep.shape[2] // 2

    def kernel(a, b, keep_left, send_left, keep_right, send_right):
        for i in range(8):
            first, second, third = i >> 2, (i >> 1) & 1, i & 1
            total = a[i] + b[i]
            (send_left if first else keep_left)[2 * second + third] = total[:, :half]
            (send_right if second else keep_right)[2 * first + third] = total[:, half:]

    out = jax.ShapeDtypeStruct((4, keep.shape[1], half), keep.dtype)
    return tuple(small_call(kernel, "fold_columns", [out] * 4, keep, come))


def fold_pair(left, come_left, right, come_right):
    half = left.shape[2]

    def kernel(a, b, c, d, first, second):
        for i, out in enumerate((first, second)):
            out[0, :, :half] = a[i] + b[i]
            out[0, :, half:] = c[i] + d[i]

    out = jax.ShapeDtypeStruct((1, left.shape[1], 2 * half), left.dtype)
    return small_call(kernel, "fold_pair", [out, out], left, come_left, right, come_right)


def split(mine, come):
    half = mine.shape[2] // 2

    def kernel(a, b, left, right):
        for i, part in enumerate((a, b)):
            at = slice(i * count, (i + 1) * count)
            left[at] = part[:, :, :half]
            right[at] = part[:, :, half:]

    count = mine.shape[0]
    out = jax.ShapeDtypeStruct((2 * count, mine.shape[1], half), mine.dtype)
    return small_call(kernel, "split", [out, out], mine, come)


def weave(left, come_left, right, come_right):
    half = left.shape[2]

    def kernel(a, b, c, d, out):
        for i in range(8):
            first, second, third = i >> 2, (i >> 1) & 1, i & 1
            out[i, :, :half] = (b if first else a)[2 * second + third]
            out[i, :, half:] = (d if second else c)[2 * first + third]

    out = jax.ShapeDtypeStruct((8,) + left.shape[1:2] + (2 * half,), left.dtype)
    return small_call(kernel, "weave", out, left, come_left, right, come_right)


def close(keep, come, smalls, first_sum):
    rows = keep.shape[1]

    def kernel(a, b, c, d, out):
        out[0, :rows, :] = a[0] + b[0]
        low = jnp.where(iota(c.shape, 0) == 4, d[...], c[...])
        tail = jnp.concatenate([low, jnp.zeros_like(low)], axis=0)
        out[0, rows:, :] = tail.astype(bf16)

    out = jax.ShapeDtypeStruct((1, rows + group, keep.shape[2]), keep.dtype)
    return small_call(kernel, "close", out, keep, come, smalls, first_sum)


def add(mine, come):
    def kernel(a, b, out):
        out[...] = a[...] + b[...]

    return small_call(kernel, "add", jax.ShapeDtypeStruct(mine.shape, mine.dtype), mine, come)


def last_kernel(dims, held, *rest):
    stages, part, piece, heads, buckets = dims
    half, _, width = held.shape
    if part:
        earlier, rest = rest[0], rest[3:]
    sides = rest[:2]
    values, sems = rest[-2:]
    me = own_code(stages)
    blocks = width // piece
    for i in range(half):
        owner = me ^ (part * half + i)
        at = pl.multiple_of((owner & (blocks - 1)) * piece, group)
        side_of = lax.shift_right_logical(owner, int(math.log2(blocks)))
        values[i] = held[i, :piece, :].astype(f32)
        for side in range(2):

            @pl.when(side_of == side)
            def _(side=side, at=at, i=i):
                pltpu.make_async_copy(
                    values.at[i], sides[side].at[pl.ds(at, piece), :], sems.at[i]
                ).start()

    total = sum(held[i, piece:, :].astype(f32)[:8] for i in range(half))
    if part:
        total = total + earlier[...]
        for i, out in zip((4, 0, 1, 2), rest[2:6]):
            out[...] = total[i : i + 1, :].reshape(width)
        spots = iota((width, 128), 0)
        by_bucket = jnp.where((spots & (buckets - 1)) == iota((width, 128), 1), 1.0, 0.0)
        by_head = jnp.where(
            lax.shift_right_logical(iota((group, width), 1), int(math.log2(buckets)))
            == iota((group, width), 0),
            total[3:4, :], 0.0,
        )
        table = lax.dot_general(
            by_head, by_bucket, (((1,), (0,)), ((), ())),
            precision=highest, preferred_element_type=f32,
        )
        rest[6][...] = table[:heads, :buckets]
    else:
        rest[2][...] = total
    for i in range(half):
        pltpu.make_async_copy(values.at[i], sides[0].at[pl.ds(0, piece), :], sems.at[i]).wait()


def last_call(stages, part, held, piece, buckets, heads, earlier):
    half, _, width = held.shape
    shape = jax.ShapeDtypeStruct
    squares = [shape((width, width), f32)] * 2
    more = (
        [shape((width,), f32)] * 4 + [shape((heads, buckets), f32)] if part else [shape((8, width), f32)]
    )
    return pl.pallas_call(
        functools.partial(last_kernel, (stages, part, piece, heads, buckets)),
        out_shape=squares + more,
        in_specs=[whole] * (2 if part else 1) + [outside] * (2 if part else 0),
        out_specs=[outside] * 2 + [whole] * len(more),
        input_output_aliases={2: 0, 3: 1} if part else {},
        scratch_shapes=[pltpu.VMEM((half, piece, width), f32), pltpu.SemaphoreType.DMA((half,))],
        compiler_params=pltpu.CompilerParams(vmem_limit_bytes=12 * mega),
        cost_estimate=pl.CostEstimate(flops=int(1e7), bytes_accessed=int(5e6), transcendentals=0),
        name=f"last_{part}",
    )(held, *earlier)


def shards(
    docs, lists,
    tokens, pair_lengths, list_ids, relevance,
    first_gain, query_weight, key_weight, value_weight, output_weight, bias_table,
    second_gain, inner_weight, outer_weight, final_gain, score_vector,
):
    row_count, length, width = tokens.shape[1:]
    pairs = pair_lengths.shape[2]
    buckets, heads = bias_table.shape
    devices = docs * lists
    sizes = {"docs": docs, "lists": lists}
    stages = tuple(("lists", 1 << b) for b in range(lists.bit_length() - 1)) + tuple(
        ("docs", 1 << b) for b in range(docs.bit_length() - 1)
    )

    def swap(values, stage):
        axis, mask = stage
        return lax.ppermute(values, axis, [(i, i ^ mask) for i in range(sizes[axis])])

    rows = tokens.reshape(row_count, length, width)
    lengths = pair_lengths.reshape(row_count, pairs)
    spot = lax.broadcasted_iota(jnp.int32, (group, width), 0)
    gains = jnp.pad(bias_table.T, ((4, group - 4 - heads), (0, width - buckets)))
    for i, vector in enumerate((first_gain, second_gain, final_gain, score_vector)):
        gains = jnp.where(spot == i, vector[None, :], gains)
    members = list_ids.shape[1]
    known = jnp.pad(list_ids, ((0, 0), (0, members))) + jnp.pad(relevance, ((0, 0), (members, 0)))
    outs = path_call(
        rows, lengths, known, gains, heads, buckets,
        (query_weight, key_weight, value_weight, output_weight, inner_weight, outer_weight),
    )
    pay, factors, n1, probs, dl, turned, yk, yv, qf, gctx, z, vz, ga, a2, fhat, yq = outs[:16]
    wq, wk, wv, wo, wi, wf, scores = outs[16:]

    tie = lax.optimization_barrier
    gather_order = tuple(reversed(stages))

    rows_left = list(gather_order)
    come = None
    projected, bias = [], None
    for i, stage in enumerate(gather_order):
        if i < row_count:
            n1, pay = tie((n1, pay))
            come_pay = swap(pay, stage)
            made = project_call(i, n1, wq, wk, wv)
            come_pay, made = tie((come_pay, tuple(made)))
            projected += made
        elif i == row_count:
            gains, pay = tie((gains, pay))
            come_pay = swap(pay, stage)
            bias = bias_call(heads, buckets, gains)
            come_pay, bias = tie((come_pay, bias))
        else:
            come_pay = swap(pay, stage)
        pay = join(pay, come_pay)
        if i == 0:
            factors, pay = tie((factors, pay))
            come = swap(factors, rows_left.pop(0))
        elif i == 2:
            come, pay = tie((come, pay))
            factors = join(factors, come)
            come = swap(factors, rows_left.pop(0))
    come, pay = tie((come, pay))
    left, right = split(factors, come)
    count = row_count * pairs
    dims = (stages, docs, lists, docs // 2, count, heads, buckets)
    keep, send, g_all, g_own, smalls = terms_call(
        dims, pay, z, vz, qf, gctx, turned, a2, fhat, gains
    )
    piece = keep.shape[1]
    cut = cut_stages(stages, width)
    rest = stages[len(cut) :]
    for stage in cut[:-4]:
        keep, send = fold(keep, swap(send, stage))
    sums = fold_columns(keep, swap(send, cut[-4]))

    third, fourth = rows_left[:2]
    bias, sums, left, right = tie((bias, sums, left, right))
    arrived = swap(sums[1], cut[-3]), swap(sums[3], cut[-2])
    come = swap(left, third), swap(right, fourth)
    attended = attention_call(lengths, rows, bias, wo, projected)
    arrived, come, attended = tie((arrived, come, attended))
    keep_left, send_left = fold(sums[0], arrived[0])
    keep_right, send_right = fold(sums[2], arrived[1])
    left, right = join(left, come[0]), join(right, come[1])

    attended, send_left, send_right, left, right = tie(
        (attended, send_left, send_right, left, right)
    )
    arrived = swap(send_left, cut[-2]), swap(send_right, cut[-3])
    come = swap(left, fourth), swap(right, third)
    encoded = feed_call(0, attended, gains, wi, wf, None)
    arrived, encoded = tie((arrived, encoded))
    keep, send = fold_pair(keep_left, arrived[0], keep_right, arrived[1])

    probs, send, encoded = tie((probs, send, encoded))
    arrived = swap(send, cut[-1])
    grads, first_sum = tokens_grad_call(
        lengths, rows, g_own, probs, dl, yk, yv, yq, ga, gains
    )
    arrived, grads, first_sum = tie((arrived, grads, first_sum))
    held = close(keep, arrived, smalls, first_sum)

    for stage in rest[:-1]:
        held = add(held, swap(held, stage))
    attended, held = tie((attended, held))
    arrived = swap(held, rest[-1])
    held, come = tie((held, come))
    left, right = join(left, come[0]), join(right, come[1])
    for stage in rows_left[2:-1]:
        left, right = join(left, swap(left, stage)), join(right, swap(right, stage))
    come = swap(left, rows_left[-1]), swap(right, rows_left[-1])
    attended, left = tie((attended, left))
    encoded = feed_call(1, attended, gains, wi, wf, encoded)
    arrived, encoded, come = tie((arrived, encoded, come))
    held = add(held, arrived)
    held_rows = (left, come[0], right, come[1])

    held, held_rows = tie((held, held_rows))
    arrived = swap(held, cut[-1])
    products = tuple(outer_call(0, held_rows, g_all, wi, wf, ()))
    products, arrived = tie((products, arrived))
    query_grad, output_grad = products
    left, right = split(held, arrived)

    left, right, held_rows = tie((left, right, held_rows))
    come = swap(left, cut[-2]), swap(right, cut[-3])
    wide = tuple(outer_call(1, held_rows, g_all, wi, wf, ()))
    wide, come = tie((wide, come))
    left, right = join(left, come[0]), join(right, come[1])

    left, right, wide = tie((left, right, wide))
    come = swap(left, cut[-3]), swap(right, cut[-2])
    wide = outer_call(2, held_rows, g_all, wi, wf, wide)
    wide, come = tie((tuple(wide), come))
    held = weave(left, come[0], right, come[1])

    for stage in reversed(cut[1:-3]):
        held = join(held, swap(held, stage))
    come = swap(held, cut[0])
    key_grad, value_grad, small_sums = last_call(cut, 0, held, piece, buckets, heads, ())
    (
        key_grad, value_grad, first_grad, second_grad, final_grad, vector_grad, table_grad
    ) = last_call(cut, 1, come, piece, buckets, heads, (small_sums, key_grad, value_grad))
    inner_grad, outer_grad = wide
    return (
        encoded.reshape(tokens.shape),
        scores.reshape(1, row_count, pairs),
        grads.reshape(tokens.shape),
        first_grad,
        query_grad,
        key_grad,
        value_grad,
        output_grad,
        table_grad.T,
        second_grad,
        inner_grad,
        outer_grad,
        final_grad,
        vector_grad,
    )


def solution(mesh):
    placed = P("lists", "docs", None, None)
    return jax.shard_map(
        functools.partial(shards, mesh.shape["docs"], mesh.shape["lists"]),
        mesh=mesh,
        in_specs=(placed, P("lists", "docs", None), P("lists", None), P("lists", None)) + (P(),) * 11,
        out_specs=(placed, P("lists", "docs", None), placed) + (P(),) * 11,
        check_vma=False,
    )
```

```python
import functools
import math

import jax
import jax.numpy as jnp
from jax import lax
from jax.experimental import pallas as pl
from jax.experimental.pallas import tpu as pltpu
from jax.sharding import PartitionSpec as P

epsilon = 1e-06
negative = -1000000000.0
highest = lax.Precision.HIGHEST
limits = (12, 16, 23, 32, 46, 64, 91)
f32 = jnp.float32
bf16 = jnp.bfloat16
window = 128
reach = 144
lanes_path = 256
group = 16
mega = 1 << 20
curve = math.sqrt(2.0 / math.pi)
cubic = 0.044715
whole = pl.BlockSpec(memory_space=pltpu.VMEM)
scalars = pl.BlockSpec(memory_space=pltpu.SMEM)
outside = pl.BlockSpec(memory_space=pl.ANY)


def mm(a, b):
    return lax.dot_general(a, b, (((1,), (0,)), ((), ())), preferred_element_type=f32)


def mm_nt(a, b):
    return lax.dot_general(a, b, (((1,), (1,)), ((), ())), preferred_element_type=f32)


def mm_tn(a, b):
    return lax.dot_general(a, b, (((0,), (0,)), ((), ())), preferred_element_type=f32)


def as_row(gains, i):
    return gains[i : i + 1, :]


def iota(shape, axis):
    return lax.broadcasted_iota(jnp.int32, shape, axis)


def bucket_of(offsets):
    upper_half = jnp.where(offsets > 0, 16, 0)
    distance = jnp.abs(offsets)
    beyond = jnp.full(offsets.shape, 8, jnp.int32)
    for border in limits:
        beyond = beyond + jnp.where(distance >= border, 1, 0)
    return upper_half + jnp.where(distance < 8, distance, beyond)


def rms_factor(values):
    return lax.rsqrt(jnp.mean(values * values, axis=-1, keepdims=True) + epsilon)


def norm_back(normed, factor, upstream):
    return factor * (upstream - normed * jnp.mean(upstream * normed, axis=-1, keepdims=True))


def half_bent(values, square):
    return 0.5 * jnp.tanh(values * (square * (curve * cubic) + curve)) + 0.5


def gelu(values):
    return values * half_bent(values, values * values)


def gelu_pair(values):
    square = values * values
    half = half_bent(values, square)
    value = half * values
    steep = (value - value * half) * (square * (6.0 * curve * cubic) + 2.0 * curve)
    return value, half + steep


def bias_vector(table, lanes, origin):
    buckets = table.shape[1]
    buckets_at = bucket_of(iota((buckets, lanes), 1) - origin)
    chosen = jnp.where(buckets_at == iota((buckets, lanes), 0), 1.0, 0.0)
    return lax.dot_general(
        table, chosen, (((1,), (0,)), ((), ())), precision=highest, preferred_element_type=f32
    )


def cast_rows(target, source, chunk):
    rows = source.shape[0]

    def step(i, carry):
        at = pl.ds(pl.multiple_of(i * chunk, chunk), chunk)
        target[at, :] = source[at, :].astype(bf16)
        return carry

    lax.fori_loop(0, rows // chunk, step, 0)


def starts_of(lengths, row, count):
    out, at = [], 0
    for i in range(count):
        out.append((at, lengths[row, i]))
        at = at + lengths[row, i]
    return out


def path_kernel(
    dims,
    lengths, known,
    tokens_in, gains,
    wq_in, wk_in, wv_in, wo_in, wi_in, wf_in,
    pay, factors, n1_out, probs_out, dl_out, turned_out, yk_out, yv_out, qf_out, gctx_out, z_out, vz_out,
    ga_out, a2_out, fhat_out, yq_out,
    wq, wk, wv, wo, wi, wf, scores_out,
    tokens, square, padded, first, gather_z, logits, expand, wide_z,
    in_sems, tokens_sem,
):
    rows, length, width, pairs, heads, buckets = dims
    members = known.shape[1] // 2
    count = rows * pairs
    parts = wi.shape[1] // width
    slots = square.shape[0]
    chunks = [(wq_in, wq), (wk_in, wk), (wv_in, wv), (wo_in, wo)]
    for i in range(parts):
        at = pl.ds(i * width, width)
        chunks.append((wi_in.at[:, at], wi.at[:, at]))
    for i in range(parts):
        at = pl.ds(i * width, width)
        chunks.append((wf_in.at[at, :], wf.at[at, :]))

    def load_of(i):
        return pltpu.make_async_copy(chunks[i][0], square.at[i % slots], in_sems.at[i % slots])

    tokens_load = pltpu.make_async_copy(tokens_in, tokens, tokens_sem)
    tokens_load.start()
    order = iter(range(slots))

    def request(count):
        for _ in range(count):
            load_of(next(order)).start()

    request(2)
    tokens_load.wait()
    request(2)

    gain = as_row(gains, 0)
    for r in range(rows):
        padded[r, length:, :] = jnp.zeros((reach, width), bf16)

        def norm_step(i, carry, r=r):
            at = pl.ds(pl.multiple_of(i * 64, 64), 64)
            x = tokens[r, at, :]
            n = (x * rms_factor(x) * gain).astype(bf16)
            n1_out[r, at, :] = n
            padded[r, at, :] = n
            return carry

        lax.fori_loop(0, length // 64, norm_step, 0)
        request(2)
    first[...] = jnp.zeros(first.shape, f32)
    pieces = []
    for r in range(rows):
        for at, size in starts_of(lengths, r, pairs):
            p = len(pieces)
            shift = at & (group - 1)
            pieces.append((r, pl.multiple_of(at - shift, group), shift, size))
            first[p : p + 1, :] = tokens[r, pl.ds(at, 1), :]

    def nearby(p):
        r, base, _, _ = pieces[p]
        return padded[r, pl.ds(base, reach), :]

    spots = [slice(p * group, (p + 1) * group) for p in range(count)]
    head_rows = iota((group, width), 0) == lax.shift_right_logical(
        iota((group, width), 1), int(math.log2(width // heads))
    )

    def widen(values):
        for p in range(count):
            expand[p * group : (p + 1) * group, :] = jnp.where(
                head_rows, values[p : p + 1, :], 0.0
            ).astype(bf16)

    def narrow(target):
        target[...] = jnp.zeros(target.shape, f32)
        for p in range(count):
            block = wide_z[p * group : (p + 1) * group, :]
            target[p : p + 1, :] = jnp.sum(
                jnp.where(head_rows, block, 0.0), axis=0, keepdims=True
            )

    def take(i):
        load_of(i).wait()
        cast_rows(chunks[i][1], square.at[i % slots], 64)
        if i < 4:
            request(1)

    take(0)
    n1_first = (first[...] * rms_factor(first[...]) * gain).astype(bf16)
    q_first = mm(n1_first, wq[...]).astype(bf16)
    qf_out[...] = q_first
    widen(q_first.astype(f32))
    take(1)
    yk_out[...] = mm_nt(expand[...], wk[...]).astype(bf16)
    position = bias_vector(gains[4 : 4 + heads, :buckets], lanes_path, 0)
    position = jnp.concatenate([position, jnp.zeros((group - heads, lanes_path), f32)], axis=0)
    lane = iota((group, lanes_path), 1)
    for p, (_, _, shift, size) in enumerate(pieces):
        logits[spots[p], :reach] = mm_nt(yk_out[spots[p], :], nearby(p))
        block = logits[spots[p], :] + pltpu.roll(position, shift, 1)
        inside = jnp.logical_and(lane >= shift, lane < shift + size)
        logits[spots[p], :] = jnp.where(inside, block, negative)
    take(2)
    take(3)
    scores_in = logits[...]
    peak = jnp.max(scores_in, axis=-1, keepdims=True)
    raised = jnp.exp(scores_in - peak)
    probs = raised / jnp.sum(raised, axis=-1, keepdims=True)
    probs_out[...] = probs.astype(bf16)
    for p in range(count):
        vz_out[spots[p], :] = mm(probs_out[spots[p], :reach], nearby(p)).astype(bf16)
    wide_z[...] = mm(vz_out[...], wv[...])
    narrow(gather_z)
    context = gather_z[...].astype(bf16)
    attended = first[...] + mm(context, wo[...])
    scale_two = rms_factor(attended)
    second = attended * scale_two
    normed_two = (second * as_row(gains, 1)).astype(bf16)
    for i in range(parts):
        take(4 + i)
    value, slope = gelu_pair(mm(normed_two, wi[...]))
    for i in range(parts):
        take(4 + parts + i)
    encoded = attended + mm(value.astype(bf16), wf[...])
    scale_final = rms_factor(encoded)
    final_hat = encoded * scale_final
    fhat_out[...] = final_hat
    unit = as_row(gains, 3) * as_row(gains, 2)
    score_col = jnp.sum(final_hat * unit, axis=-1, keepdims=True)
    square_lane = iota((group, 128), 1)
    row = jnp.sum(
        jnp.where(square_lane == iota((group, 128), 0), score_col, 0.0), axis=0, keepdims=True
    )
    for r in range(rows):
        scores_out[r : r + 1, :] = row[:, r * pairs : (r + 1) * pairs]
    row_lane = iota((1, 128), 1)
    place = lax.axis_index("docs") * count
    for i in range(count):
        row = jnp.where(row_lane == group + i, known[0, place + i].astype(f32), row)
        row = jnp.where(row_lane == 2 * group + i, known[0, members + place + i].astype(f32), row)
    pay[...] = row

    grad_encoded = norm_back(final_hat, scale_final, jnp.broadcast_to(unit, final_hat.shape))
    grad_branch = grad_encoded.astype(bf16)
    grad_preact = (mm_nt(grad_branch, wf[...]) * slope).astype(bf16)
    grad_normed_two = mm_nt(grad_preact, wi[...])
    a2_out[...] = second * grad_normed_two
    grad_attended = grad_encoded + norm_back(second, scale_two, grad_normed_two * as_row(gains, 1))
    ga_out[...] = grad_attended
    grad_attn = grad_attended.astype(bf16)
    grad_context = mm_nt(grad_attn, wo[...])
    gctx_out[...] = grad_context
    widen(grad_context)
    yv_out[...] = mm_nt(expand[...], wv[...]).astype(bf16)
    logits[...] = jnp.zeros(logits.shape, f32)
    for p in range(count):
        logits[spots[p], :reach] = mm_nt(yv_out[spots[p], :], nearby(p))
    grad_probs = logits[...]
    grad_logits = probs * (grad_probs - jnp.sum(probs * grad_probs, axis=-1, keepdims=True))
    dl_out[...] = grad_logits.astype(bf16)
    for p, (_, _, shift, _) in enumerate(pieces):
        rounded = dl_out[spots[p], :]
        z_out[spots[p], :] = mm(rounded[:, :reach], nearby(p))
        turned = pltpu.roll(rounded.astype(f32), (lanes_path - shift) & (lanes_path - 1), 1)
        turned_out[spots[p], :] = turned[:, :window]
    wide_z[...] = mm(z_out[...].astype(bf16), wk[...])
    narrow(gather_z)
    grad_query = gather_z[...].astype(bf16)
    yq_out[...] = mm_nt(grad_query, wq[...])
    span, half = 3 * width // 2, width // 2
    for i, member in enumerate((n1_first, grad_query, context, grad_attn, normed_two, grad_branch)):
        member = member.astype(f32)
        tail = member[8:, :]
        tail = jnp.where(
            iota((8, half), 0) < 4, tail[:, :half], pltpu.roll(tail[:, half:], 4, 0)
        )
        factors[0, :, i * span : i * span + width] = member[:8].astype(bf16)
        factors[0, :, i * span + width : (i + 1) * span] = tail.astype(bf16)


def path_call(tokens, lengths, known, gains, heads, buckets, weights):
    rows, length, width = tokens.shape
    pairs = lengths.shape[1]
    combos = rows * pairs * group
    shape = jax.ShapeDtypeStruct
    outs = [
        shape((1, 128), f32),
        shape((1, 8, 9 * width), bf16),
        shape((rows, length, width), bf16),
        shape((combos, lanes_path), bf16),
        shape((combos, lanes_path), bf16),
        shape((combos, window), f32),
        shape((combos, width), bf16),
        shape((combos, width), bf16),
        shape((group, width), bf16),
        shape((group, width), f32),
        shape((combos, width), f32),
        shape((combos, width), bf16),
        shape((group, width), f32),
        shape((group, width), f32),
        shape((group, width), f32),
        shape((group, width), f32),
    ]
    low = [shape(w.shape, bf16) for w in weights] + [shape((rows, pairs), f32)]
    return pl.pallas_call(
        functools.partial(path_kernel, (rows, length, width, pairs, heads, buckets)),
        out_shape=outs + low,
        in_specs=[scalars] * 2 + [outside, whole] + [outside] * 6,
        out_specs=[whole] * (len(outs) + len(low)),
        scratch_shapes=[
            pltpu.VMEM(tokens.shape, f32),
            pltpu.VMEM((12, width, width), f32),
            pltpu.VMEM((rows, length + reach, width), bf16),
            pltpu.VMEM((group, width), f32),
            pltpu.VMEM((group, width), f32),
            pltpu.VMEM((combos, lanes_path), f32),
            pltpu.VMEM((combos, width), bf16),
            pltpu.VMEM((combos, width), f32),
            pltpu.SemaphoreType.DMA((12,)),
            pltpu.SemaphoreType.DMA,
        ],
        compiler_params=pltpu.CompilerParams(vmem_limit_bytes=45 * mega),
        cost_estimate=pl.CostEstimate(flops=int(9e9), bytes_accessed=int(5e7), transcendentals=0),
        name="path",
    )(lengths, known, tokens, gains, *weights)


def code_of(stages, indices):
    total = len(stages)
    code = 0
    for s, (axis, mask) in enumerate(stages):
        bit = jnp.where((indices[axis] & mask) != 0, 1, 0) if not isinstance(
            indices[axis], int
        ) else (1 if indices[axis] & mask else 0)
        code = code + bit * (1 << (total - 1 - s))
    return code


def cut_stages(stages, width):
    count = 3 + sum(axis == "lists" for axis, _ in stages)
    while (2 * width) % (group << count):
        count -= 1
    return stages[:count]


def own_code(stages):
    return code_of(stages, {axis: lax.axis_index(axis) for axis in ("docs", "lists")})


def terms_kernel(
    dims,
    pay, z, vz, qf, gctx, dl, a2, fhat, gains,
    keep, send, g_all, g_own, smalls,
    term, left, right,
):
    stages, docs, lists, list_count, count, heads, buckets = dims
    width = z.shape[1]
    everything = pay[...]
    lane = iota(everything.shape, 1)
    score = everything
    names = pltpu.roll(everything, 128 - group, 1)
    label = pltpu.roll(everything, 128 - 2 * group, 1)
    used = lane < count
    part = lax.shift_right_logical(iota(everything.shape, 0), int(math.log2(docs)))
    key = jnp.where(used, part * list_count + names.astype(jnp.int32), -1)

    def total_of(values):
        return jnp.sum(jnp.sum(values, axis=1, keepdims=True), axis=0, keepdims=True)

    def top_step(k, top):
        member = key == k
        best = jnp.max(
            jnp.max(jnp.where(member, score, negative), axis=1, keepdims=True),
            axis=0, keepdims=True,
        )
        return jnp.where(member, best, top)

    keys = lists * list_count
    unroll = keys if keys <= 16 else 4
    top = lax.fori_loop(0, keys, top_step, score, unroll=unroll)
    raised = jnp.exp(score - top)

    def sum_step(k, carry):
        total, gain = carry
        member = key == k
        return (
            jnp.where(member, total_of(jnp.where(member, raised, 0.0)), total),
            jnp.where(member, total_of(jnp.where(member, label, 0.0)), gain),
        )

    ones = jnp.ones(everything.shape, f32)
    total, gain = lax.fori_loop(0, keys, sum_step, (ones, ones), unroll=unroll)
    grads = jnp.where(used, raised / total * gain - label, 0.0)
    g_all[...] = grads
    own = grads[0:1, :]
    g_own[...] = jnp.broadcast_to(own, g_own.shape)

    combos = count * group
    pair_of = lax.shift_right_logical(iota((combos, 128), 0), int(math.log2(group)))
    g_combo = jnp.sum(jnp.where(iota((combos, 128), 1) == pair_of, own, 0.0), axis=1, keepdims=True)
    g_pair = jnp.sum(
        jnp.where(iota((group, 128), 1) == iota((group, 128), 0), own, 0.0), axis=1, keepdims=True
    )
    head_rows = iota((group, width), 0) == lax.shift_right_logical(
        iota((group, width), 1), int(math.log2(width // heads))
    )
    queries = qf[...].astype(f32)
    upstream = gctx[...] * g_pair
    for p in range(count):
        at = slice(p * group, (p + 1) * group)
        right[0, at, :] = jnp.where(head_rows, queries[p : p + 1, :], 0.0).astype(bf16)
        right[1, at, :] = jnp.where(head_rows, upstream[p : p + 1, :], 0.0).astype(bf16)
    left[...] = (z[...] * g_combo).astype(bf16)
    term[0:width, :] = mm_tn(left[...], right[0])
    term[width : 2 * width, :] = mm_tn(vz[...], right[1])

    half, piece = keep.shape[0], keep.shape[1]
    blocks = width // piece
    mine = own_code(stages[: half.bit_length()])

    def piece_step(r, carry, target, base):
        owner = mine ^ (base + r)
        side = lax.shift_right_logical(owner, int(math.log2(blocks)))
        at = side * width + (owner & (blocks - 1)) * piece
        target[r] = term[pl.ds(pl.multiple_of(at, group), piece), :].astype(bf16)
        return carry

    lax.fori_loop(0, half, functools.partial(piece_step, target=send, base=half), 0)
    lax.fori_loop(0, half, functools.partial(piece_step, target=keep, base=0), 0)

    smalls[...] = jnp.zeros(smalls.shape, f32)
    smalls[0:1, :] = jnp.sum(a2[...] * g_pair, axis=0, keepdims=True)
    hats = jnp.sum(fhat[...] * g_pair, axis=0, keepdims=True)
    smalls[1:2, :] = hats * as_row(gains, 3)
    smalls[2:3, :] = hats * as_row(gains, 2)
    weighted = dl[...] * g_combo
    summed = weighted[0:group, :]
    for p in range(1, count):
        summed = summed + weighted[p * group : (p + 1) * group, :]
    spots = iota((window, width), 1)
    hot = jnp.where(bucket_of(iota((window, width), 0)) == (spots & (buckets - 1)), 1.0, 0.0)
    spread = lax.dot_general(
        summed, hot, (((1,), (0,)), ((), ())), precision=highest, preferred_element_type=f32
    )
    row_of = lax.shift_right_logical(iota((group, width), 1), int(math.log2(buckets)))
    smalls[3:4, :] = jnp.sum(
        jnp.where(row_of == iota((group, width), 0), spread, 0.0), axis=0, keepdims=True
    )


def terms_call(dims, pay, z, vz, qf, gctx, dl, a2, fhat, gains):
    stages, docs, lists, list_count, count, heads, buckets = dims
    devices = docs * lists
    combos, width = z.shape
    pieces = 1 << len(cut_stages(stages, width))
    piece = 2 * width // pieces
    shape = jax.ShapeDtypeStruct
    half = shape((pieces // 2, piece, width), bf16)
    return pl.pallas_call(
        functools.partial(terms_kernel, dims),
        out_shape=[
            half, half,
            shape((devices, 128), f32),
            shape((8, 128), f32),
            shape((8, width), f32),
        ],
        in_specs=[whole] * 9,
        out_specs=[whole] * 5,
        scratch_shapes=[
            pltpu.VMEM((2 * width, width), f32),
            pltpu.VMEM((combos, width), bf16),
            pltpu.VMEM((2, combos, width), bf16),
        ],
        compiler_params=pltpu.CompilerParams(vmem_limit_bytes=10 * mega),
        cost_estimate=pl.CostEstimate(flops=int(4e9), bytes_accessed=int(1e7), transcendentals=0),
        name="terms",
    )(pay, z, vz, qf, gctx, dl, a2, fhat, gains)


def project_kernel(row, n1, wq, wk, wv, q, k, v):
    for target, low in ((q, wq), (k, wk), (v, wv)):
        target[...] = mm(n1[row], low[...]).astype(bf16)


def project_call(row, n1, wq, wk, wv):
    return pl.pallas_call(
        functools.partial(project_kernel, row),
        out_shape=[jax.ShapeDtypeStruct(n1.shape[1:], bf16)] * 3,
        in_specs=[whole] * 4,
        out_specs=[whole] * 3,
        compiler_params=pltpu.CompilerParams(vmem_limit_bytes=12 * mega),
        cost_estimate=pl.CostEstimate(flops=int(2e9), bytes_accessed=int(4e6), transcendentals=0),
        name=f"project_{row}",
    )(n1, wq, wk, wv)


def bias_kernel(heads, buckets, gains, bias):
    lanes = 4 * window
    vector = bias_vector(gains[4 : 4 + heads, :buckets], lanes, window)
    for h in range(heads):
        bias[h] = pltpu.roll(
            jnp.broadcast_to(vector[h : h + 1, :], (window, lanes)), 0, 1, stride=1, stride_axis=0
        )[:, : 3 * window]


def bias_call(heads, buckets, gains):
    return small_call(
        functools.partial(bias_kernel, heads, buckets), "bias",
        jax.ShapeDtypeStruct((heads, window, 3 * window), f32), gains,
    )


def attention_kernel(
    lengths, tokens_in, bias, wo, *rest
):
    out, tokens, ctx, qseg, kseg, sem = rest[-6:]
    rows, length, width = tokens.shape
    heads = bias.shape[0]
    pairs = lengths.shape[1]
    load = pltpu.make_async_copy(tokens_in, tokens, sem)
    load.start()
    tiles = length // window
    half = iota((2 * window, window), 1) < (width // heads)
    left = half[:window]
    upper = iota((2 * window, window), 0) < window
    chosen = half == upper

    def segment(positions, ends):
        total = jnp.zeros(positions.shape, jnp.int32)
        for end in ends:
            total = total + jnp.where(positions >= end, 1, 0)
        return total

    wide = iota((length, window), 1)
    units = []
    for row in range(rows):
        for j in range(tiles):
            for pair in range(heads // 2):
                units.append((row, j, pair))
    ones = jnp.ones((3 * window, window), bf16)

    def begin(row):
        ends = [at + size for at, size in starts_of(lengths, row, pairs)]
        seg = segment(iota((length, 1), 0), ends)
        qseg[...] = jnp.where(seg == wide, 1.0, 0.0).astype(bf16)
        kseg[...] = jnp.where(jnp.logical_and(seg != wide, wide <= pairs), negative, 0.0).astype(bf16)

    def spans(j):
        t0 = j * window
        k0 = max(j - 1, 0) * window
        k1 = min(j + 2, tiles) * window
        return t0, k0, k1

    def raw_of(row, j, pair):
        t0, k0, k1 = spans(j)
        cols = slice(pair * window, (pair + 1) * window)
        both = rest[3 * row][t0 : t0 + window, cols]
        stacked = jnp.concatenate([both, both], axis=0)
        stacked = jnp.where(chosen, stacked, jnp.zeros_like(stacked))
        mark = qseg[t0 : t0 + window, :]
        return mm_nt(
            jnp.concatenate([stacked, jnp.concatenate([mark, mark], axis=0)], axis=1),
            jnp.concatenate([rest[3 * row + 1][k0:k1, cols], kseg[k0:k1, :]], axis=1),
        )

    def finish(row, j, pair, raw):
        t0, k0, k1 = spans(j)
        off = k0 - (t0 - window)
        cols = slice(pair * window, (pair + 1) * window)
        probs = []
        for side in range(2):
            part = raw[side * window : (side + 1) * window]
            part = part + bias[2 * pair + side, :, off : off + k1 - k0]
            peak = jnp.max(part, axis=-1, keepdims=True)
            probs.append(jnp.exp(part - peak).astype(bf16))
        mixed = mm(
            jnp.concatenate(probs, axis=0),
            jnp.concatenate([rest[3 * row + 2][k0:k1, cols], ones[: k1 - k0]], axis=1),
        )
        ctx[t0 : t0 + window, cols] = jnp.where(
            left,
            mixed[:window, :window] / mixed[:window, window:],
            mixed[window:, :window] / mixed[window:, window:],
        ).astype(bf16)

    def close_row(row):
        if row == 0:
            load.wait()
        out[row] = tokens[row] + mm(ctx[...], wo[...])

    for row in range(rows):
        begin(row)
        last = None
        for unit in units:
            if unit[0] != row:
                continue
            raw = raw_of(*unit)
            if last is not None:
                finish(*last)
            last = unit + (raw,)
        finish(*last)
        close_row(row)


def attention_call(lengths, tokens, bias, wo, projected):
    rows, length, width = tokens.shape
    return pl.pallas_call(
        attention_kernel,
        out_shape=jax.ShapeDtypeStruct(tokens.shape, f32),
        in_specs=[scalars, outside] + [whole] * (2 + len(projected)),
        out_specs=whole,
        scratch_shapes=[
            pltpu.VMEM(tokens.shape, f32),
            pltpu.VMEM((length, width), bf16),
            pltpu.VMEM((length, window), bf16),
            pltpu.VMEM((length, window), bf16),
            pltpu.SemaphoreType.DMA,
        ],
        compiler_params=pltpu.CompilerParams(vmem_limit_bytes=14 * mega),
        cost_estimate=pl.CostEstimate(
            flops=int(1e10), bytes_accessed=int(1e7), transcendentals=int(8e6)
        ),
        name="attention",
    )(lengths, tokens, bias, wo, *projected)


def feed_kernel(row, attended, gains, wi, wf, held, out, normed, total, sem):
    length, width = total.shape
    tile, chunk = 256, 512
    x = attended[row]
    normed[...] = (x * rms_factor(x) * as_row(gains, 1)).astype(bf16)
    total[...] = x

    def finish(t, c, ahead):
        total[t, :] += mm(gelu(ahead).astype(bf16), wf[c, :])

    last = None
    for c in range(wi.shape[1] // chunk):
        for t in range(length // tile):
            t_at, c_at = slice(t * tile, (t + 1) * tile), slice(c * chunk, (c + 1) * chunk)
            ahead = mm(normed[t_at, :], wi[:, c_at])
            if last is not None:
                finish(*last)
            last = (t_at, c_at, ahead)
    finish(*last)
    store = pltpu.make_async_copy(total, out.at[row], sem)
    store.start()
    store.wait()


def feed_call(row, attended, gain, wi, wf, held):
    rows, length, width = attended.shape
    extra = [] if held is None else [held]
    kernel = functools.partial(feed_kernel, row)
    if held is None:
        kernel = lambda a, g, i, f, *rest: feed_kernel(row, a, g, i, f, None, *rest)
    return pl.pallas_call(
        kernel,
        out_shape=jax.ShapeDtypeStruct(attended.shape, f32),
        in_specs=[whole] * 4 + [outside] * len(extra),
        out_specs=outside,
        input_output_aliases={4: 0} if extra else {},
        scratch_shapes=[
            pltpu.VMEM((length, width), bf16),
            pltpu.VMEM((length, width), f32),
            pltpu.SemaphoreType.DMA,
        ],
        compiler_params=pltpu.CompilerParams(vmem_limit_bytes=12 * mega),
        cost_estimate=pl.CostEstimate(
            flops=int(1e10), bytes_accessed=int(1e7), transcendentals=int(3e6)
        ),
        name=f"feed_{row}",
    )(attended, gain, wi, wf, *extra)


def spread_kernel(row, lengths, probs, dl, yk, yv, yq, out):
    pairs = lengths.shape[1]
    out[...] = jnp.zeros(out.shape, f32)
    starts = starts_of(lengths, row, pairs)
    for i, (at, size) in enumerate(starts):
        pair = row * pairs + i
        here = slice(pair * group, (pair + 1) * group)
        left = jnp.concatenate([dl[here, :], probs[here, :]], axis=0)
        right = jnp.concatenate([yk[here, :], yv[here, :]], axis=0)
        base = pl.multiple_of(at - (at & (group - 1)), group)
        out[pl.ds(base, reach), :] += mm_tn(left, right)[:reach]
    for i, (at, size) in enumerate(starts):
        pair = row * pairs + i
        out[pl.ds(at, 1), :] += yq[pair : pair + 1, :]


def spread_call(row, length, lengths, probs, dl, yk, yv, yq):
    return pl.pallas_call(
        functools.partial(spread_kernel, row),
        out_shape=jax.ShapeDtypeStruct((length + reach, yq.shape[1]), f32),
        in_specs=[scalars] + [whole] * 5,
        out_specs=whole,
        compiler_params=pltpu.CompilerParams(vmem_limit_bytes=8 * mega),
        cost_estimate=pl.CostEstimate(flops=int(1e9), bytes_accessed=int(2e6), transcendentals=0),
        name=f"spread_{row}",
    )(lengths, probs, dl, yk, yv, yq)


def tokens_grad_kernel(dims, lengths, tokens_in, g_own, ga, gains, *rest):
    rows, length, width, pairs = dims
    spreads = rest[:rows]
    out, first_sum, tokens, sems = rest[rows:]
    loads = [
        pltpu.make_async_copy(tokens_in.at[r], tokens.at[r], sems.at[r]) for r in range(rows)
    ]
    for load in loads:
        load.start()
    own = g_own[0:1, :]
    lane = iota((1, 128), 1)
    total = jnp.zeros((1, width), f32)
    gain_row = as_row(gains, 0)
    stores = []
    for r in range(rows):
        starts = starts_of(lengths, r, pairs)
        amounts = [
            jnp.sum(jnp.where(lane == r * pairs + i, own, 0.0), axis=1, keepdims=True)
            for i in range(pairs)
        ]
        loads[r].wait()

        def step(i, carry, r=r, starts=starts, amounts=amounts):
            at = pl.ds(pl.multiple_of(i * 64, 64), 64)
            spot = i * 64 + iota((64, 1), 0)
            amount = jnp.zeros((64, 1), f32)
            for (start, size), value in zip(starts, amounts):
                inside = jnp.logical_and(spot >= start, spot < start + size)
                amount = jnp.where(inside, value, amount)
            x = tokens[r, at, :]
            factor = rms_factor(x)
            hat = x * factor
            upstream = spreads[r][at, :] * amount
            tokens[r, at, :] = norm_back(hat, factor, upstream * gain_row)
            return carry + jnp.sum(hat * upstream, axis=0, keepdims=True)

        total = lax.fori_loop(0, length // 64, step, total)
        for i, (at, size) in enumerate(starts):
            pair = r * pairs + i
            tokens[r, pl.ds(at, 1), :] += ga[pair : pair + 1, :] * amounts[i]
        store = pltpu.make_async_copy(tokens.at[r], out.at[r], sems.at[r])
        store.start()
        stores.append(store)
    first_sum[...] = total
    for store in stores:
        store.wait()


def tokens_grad_call(lengths, tokens, g_own, ga, gains, spreads):
    rows, length, width = tokens.shape
    pairs = lengths.shape[1]
    return pl.pallas_call(
        functools.partial(tokens_grad_kernel, (rows, length, width, pairs)),
        out_shape=[
            jax.ShapeDtypeStruct(tokens.shape, f32),
            jax.ShapeDtypeStruct((1, width), f32),
        ],
        in_specs=[scalars, outside] + [whole] * (3 + rows),
        out_specs=[outside, whole],
        scratch_shapes=[
            pltpu.VMEM(tokens.shape, f32),
            pltpu.SemaphoreType.DMA((rows,)),
        ],
        compiler_params=pltpu.CompilerParams(vmem_limit_bytes=12 * mega),
        cost_estimate=pl.CostEstimate(flops=int(2e9), bytes_accessed=int(1e7), transcendentals=0),
        name="tokens_grad",
    )(lengths, tokens, g_own, ga, gains, *spreads)


def outer_kernel(dims, *rest):
    part, chunk, blocks = dims
    halves = rest[:2], rest[2:4]
    g_all, wi, wf = rest[4:7]
    rest = rest[9:] if part == 2 else rest[7:]
    factors, g, branch, inner, outer, flat, out_sems = rest[2:9]
    width, hidden = wi.shape
    steps = hidden // chunk
    mine = range((part - 1) * steps // 2, part * steps // 2) if part else ()
    needed = (4, 5) if part else (0, 1, 2, 3)
    members = factors.shape[1] // 12
    main = members * 8
    span, half = 3 * width // 2, width // 2

    def scaled(i):
        return (factors[i].astype(f32) * g[...]).astype(bf16)

    def unpack(sources, b):
        near = iota((8, half), 0) < 4
        for i in needed:
            side, at = i // 3, slice((i % 3) * span, (i % 3 + 1) * span)
            held = []
            for d in range(members):
                if side:
                    d = (d & ~12) | ((d & 4) << 1) | ((d & 8) >> 1)
                source = sources[side][d // sources[side][0].shape[0]]
                held.append(source[d % source.shape[0], :, at].astype(f32))
            for k in range(0, members, 2):
                even, odd = held[k], held[k + 1]
                factors[i, k * 8 : (k + 2) * 8, :] = jnp.concatenate(
                    [even[:, :width], odd[:, :width]], axis=0
                ).astype(bf16)
            for k in range(0, members, 4):
                tiles = []
                for j in (k, k + 2):
                    even, odd = held[j][:, width:], held[j + 1][:, width:]
                    tiles.append(
                        jnp.concatenate(
                            [
                                jnp.where(near, even, pltpu.roll(odd, 4, 0)),
                                jnp.where(near, pltpu.roll(even, 4, 0), odd),
                            ],
                            axis=1,
                        )
                    )
                at = main + k * 4
                factors[i, at : at + 16, :] = jnp.concatenate(tiles, axis=0).astype(bf16)
        same = iota((8, 128), 1) == iota((8, 128), 0)
        more = iota((8, 128), 1) == 8 + (iota((8, 128), 0) & 3)
        for d in range(members):
            here = g_all[pl.ds(b * members + d, 1), :]
            g[d * 8 : (d + 1) * 8, :] = jnp.sum(jnp.where(same, here, 0.0), axis=1, keepdims=True)
        for d in range(0, members, 2):
            both = jnp.where(
                iota((8, 128), 0) < 4,
                g_all[pl.ds(b * members + d, 1), :],
                g_all[pl.ds(b * members + d + 1, 1), :],
            )
            at = main + d * 4
            g[at : at + 8, :] = jnp.sum(jnp.where(more, both, 0.0), axis=1, keepdims=True)
        if part:
            branch[...] = scaled(5)

    def put(target, values, b):
        if blocks == 1:
            target[...] = values
        else:
            target[...] = jnp.where(b == 0, values, target[...] + values)

    def each_block(one):
        if blocks == 1:
            one(0, 0)
        else:
            arrived, sem = rest[-2], rest[-1]

            def step(b, carry):
                for side in range(2):
                    for i in range(2):

                        @pl.when((b < blocks // 2) == (i == 0))
                        def _(side=side, i=i):
                            at = b - i * (blocks // 2)
                            load = pltpu.make_async_copy(
                                halves[side][i].at[pl.ds(at * members, members)],
                                arrived.at[side], sem,
                            )
                            load.start()
                            load.wait()

                unpack([[arrived.at[0]], [arrived.at[1]]], b)
                return one(b, carry)

            lax.fori_loop(0, blocks, step, 0)

    stores = {}

    def save(source, target, sem):
        store = pltpu.make_async_copy(source, target, out_sems.at[sem])
        store.start()
        stores[sem] = store

    if blocks == 1:
        unpack(halves, 0)
    if not part:
        for i, j, slot, target in ((0, 1, 0, rest[0]), (2, 3, 1, rest[1])):

            def square(b, carry, i=i, j=j, slot=slot):
                put(flat.at[slot], mm_tn(factors[i], scaled(j)), b)
                return carry

            each_block(square)
            save(flat.at[slot], target, 4 + slot)
    for c in mine:
        slot = c % 2
        at = slice(c * chunk, (c + 1) * chunk)

        def one(b, carry, slot=slot, at=at):
            value, slope = gelu_pair(mm(factors[4], wi[:, at]))
            grad = (mm_nt(branch[...], wf[at, :]) * slope).astype(bf16)
            put(inner.at[slot], mm_tn(factors[4], grad), b)
            put(outer.at[slot], mm_tn(value.astype(bf16), branch[...]), b)
            return carry

        each_block(one)
        save(inner.at[slot], rest[0].at[:, pl.ds(c * chunk, chunk)], slot)
        save(outer.at[slot], rest[1].at[pl.ds(c * chunk, chunk), :], 2 + slot)
    for store in stores.values():
        store.wait()


def outer_call(part, held_rows, g_all, wi, wf, held):
    low = held_rows[0]
    devices = 2 * low.shape[0]
    width, hidden = wi.shape
    chunk = hidden // 4
    members = min(devices, 32)
    blocks = devices // members
    block = members * 12
    shape = jax.ShapeDtypeStruct
    wide = [shape((width, hidden), f32), shape((hidden, width), f32)]
    flat = [shape((width, width), f32)] * 2
    place = whole if blocks == 1 else outside
    more = [] if blocks == 1 else [
        pltpu.VMEM((2, members) + low.shape[1:], bf16), pltpu.SemaphoreType.DMA
    ]
    return pl.pallas_call(
        functools.partial(outer_kernel, (part, chunk, blocks)),
        out_shape=wide if part else flat,
        in_specs=[place] * 4 + [whole] * 3 + [outside] * len(held),
        out_specs=[outside] * 2,
        input_output_aliases={7: 0, 8: 1} if held else {},
        scratch_shapes=[
            pltpu.VMEM((6, block, width), bf16),
            pltpu.VMEM((block, 1), f32),
            pltpu.VMEM((block, width), bf16),
            pltpu.VMEM((2, width, chunk), f32),
            pltpu.VMEM((2, chunk, width), f32),
            pltpu.VMEM((2, width, width), f32),
            pltpu.SemaphoreType.DMA((6,)),
        ] + more,
        compiler_params=pltpu.CompilerParams(vmem_limit_bytes=28 * mega),
        cost_estimate=pl.CostEstimate(
            flops=int(1e10), bytes_accessed=int(2e7), transcendentals=int(1e6)
        ),
        name=f"outer_{part}",
    )(*held_rows, g_all, wi, wf, *held)


def small_call(kernel, name, outs, *args):
    return pl.pallas_call(
        kernel,
        out_shape=outs,
        in_specs=[whole] * len(args),
        out_specs=[whole] * len(outs) if isinstance(outs, (list, tuple)) else whole,
        compiler_params=pltpu.CompilerParams(vmem_limit_bytes=8 * mega),
        cost_estimate=pl.CostEstimate(flops=1000, bytes_accessed=int(1e6), transcendentals=0),
        name=name,
    )(*args)


def join(mine, come):
    if mine.size > 1 << 21:
        return jnp.concatenate([mine, come], axis=0)

    def kernel(a, b, out):
        out[: a.shape[0]] = a[...]
        out[a.shape[0] :] = b[...]

    shape = (2 * mine.shape[0],) + mine.shape[1:]
    return small_call(kernel, "join", jax.ShapeDtypeStruct(shape, mine.dtype), mine, come)


def fold(keep, come):
    half = keep.shape[0] // 2

    def kernel(a, b, first, second):
        for i in range(half):
            first[i] = a[i] + b[i]
            second[i] = a[half + i] + b[half + i]

    out = jax.ShapeDtypeStruct((half,) + keep.shape[1:], keep.dtype)
    return small_call(kernel, "fold", [out, out], keep, come)


def fold_columns(keep, come):
    half = keep.shape[2] // 2

    def kernel(a, b, keep_left, send_left, keep_right, send_right):
        for i in range(8):
            first, second, third = i >> 2, (i >> 1) & 1, i & 1
            total = a[i] + b[i]
            (send_left if first else keep_left)[2 * second + third] = total[:, :half]
            (send_right if second else keep_right)[2 * first + third] = total[:, half:]

    out = jax.ShapeDtypeStruct((4, keep.shape[1], half), keep.dtype)
    return tuple(small_call(kernel, "fold_columns", [out] * 4, keep, come))


def fold_pair(left, come_left, right, come_right):
    half = left.shape[2]

    def kernel(a, b, c, d, first, second):
        for i, out in enumerate((first, second)):
            out[0, :, :half] = a[i] + b[i]
            out[0, :, half:] = c[i] + d[i]

    out = jax.ShapeDtypeStruct((1, left.shape[1], 2 * half), left.dtype)
    return small_call(kernel, "fold_pair", [out, out], left, come_left, right, come_right)


def split(mine, come):
    half = mine.shape[2] // 2

    def kernel(a, b, left, right):
        for i, part in enumerate((a, b)):
            at = slice(i * count, (i + 1) * count)
            left[at] = part[:, :, :half]
            right[at] = part[:, :, half:]

    count = mine.shape[0]
    out = jax.ShapeDtypeStruct((2 * count, mine.shape[1], half), mine.dtype)
    return small_call(kernel, "split", [out, out], mine, come)


def weave(left, come_left, right, come_right):
    half = left.shape[2]

    def kernel(a, b, c, d, out):
        for i in range(8):
            first, second, third = i >> 2, (i >> 1) & 1, i & 1
            out[i, :, :half] = (b if first else a)[2 * second + third]
            out[i, :, half:] = (d if second else c)[2 * first + third]

    out = jax.ShapeDtypeStruct((8,) + left.shape[1:2] + (2 * half,), left.dtype)
    return small_call(kernel, "weave", out, left, come_left, right, come_right)


def close(keep, come, smalls, first_sum):
    rows = keep.shape[1]

    def kernel(a, b, c, d, out):
        out[0, :rows, :] = a[0] + b[0]
        low = jnp.where(iota(c.shape, 0) == 4, d[...], c[...])
        tail = jnp.concatenate([low, jnp.zeros_like(low)], axis=0)
        out[0, rows:, :] = tail.astype(bf16)

    out = jax.ShapeDtypeStruct((1, rows + group, keep.shape[2]), keep.dtype)
    return small_call(kernel, "close", out, keep, come, smalls, first_sum)


def add(mine, come):
    def kernel(a, b, out):
        out[...] = a[...] + b[...]

    return small_call(kernel, "add", jax.ShapeDtypeStruct(mine.shape, mine.dtype), mine, come)


def last_kernel(dims, held, *rest):
    stages, part, piece, heads, buckets = dims
    half, _, width = held.shape
    if part:
        earlier, rest = rest[0], rest[3:]
    sides = rest[:2]
    values, sems = rest[-2:]
    me = own_code(stages)
    blocks = width // piece
    for i in range(half):
        owner = me ^ (part * half + i)
        at = pl.multiple_of((owner & (blocks - 1)) * piece, group)
        side_of = lax.shift_right_logical(owner, int(math.log2(blocks)))
        values[i] = held[i, :piece, :].astype(f32)
        for side in range(2):

            @pl.when(side_of == side)
            def _(side=side, at=at, i=i):
                pltpu.make_async_copy(
                    values.at[i], sides[side].at[pl.ds(at, piece), :], sems.at[i]
                ).start()

    total = sum(held[i, piece:, :].astype(f32)[:8] for i in range(half))
    if part:
        total = total + earlier[...]
        for i, out in zip((4, 0, 1, 2), rest[2:6]):
            out[...] = total[i : i + 1, :].reshape(width)
        spots = iota((width, 128), 0)
        by_bucket = jnp.where((spots & (buckets - 1)) == iota((width, 128), 1), 1.0, 0.0)
        by_head = jnp.where(
            lax.shift_right_logical(iota((group, width), 1), int(math.log2(buckets)))
            == iota((group, width), 0),
            total[3:4, :], 0.0,
        )
        table = lax.dot_general(
            by_head, by_bucket, (((1,), (0,)), ((), ())),
            precision=highest, preferred_element_type=f32,
        )
        rest[6][...] = table[:heads, :buckets]
    else:
        rest[2][...] = total
    for i in range(half):
        pltpu.make_async_copy(values.at[i], sides[0].at[pl.ds(0, piece), :], sems.at[i]).wait()


def last_call(stages, part, held, piece, buckets, heads, earlier):
    half, _, width = held.shape
    shape = jax.ShapeDtypeStruct
    squares = [shape((width, width), f32)] * 2
    more = (
        [shape((width,), f32)] * 4 + [shape((heads, buckets), f32)] if part else [shape((8, width), f32)]
    )
    return pl.pallas_call(
        functools.partial(last_kernel, (stages, part, piece, heads, buckets)),
        out_shape=squares + more,
        in_specs=[whole] * (2 if part else 1) + [outside] * (2 if part else 0),
        out_specs=[outside] * 2 + [whole] * len(more),
        input_output_aliases={2: 0, 3: 1} if part else {},
        scratch_shapes=[pltpu.VMEM((half, piece, width), f32), pltpu.SemaphoreType.DMA((half,))],
        compiler_params=pltpu.CompilerParams(vmem_limit_bytes=12 * mega),
        cost_estimate=pl.CostEstimate(flops=int(1e7), bytes_accessed=int(5e6), transcendentals=0),
        name=f"last_{part}",
    )(held, *earlier)


def shards(
    docs, lists,
    tokens, pair_lengths, list_ids, relevance,
    first_gain, query_weight, key_weight, value_weight, output_weight, bias_table,
    second_gain, inner_weight, outer_weight, final_gain, score_vector,
):
    row_count, length, width = tokens.shape[1:]
    pairs = pair_lengths.shape[2]
    buckets, heads = bias_table.shape
    devices = docs * lists
    sizes = {"docs": docs, "lists": lists}
    stages = tuple(("lists", 1 << b) for b in range(lists.bit_length() - 1)) + tuple(
        ("docs", 1 << b) for b in range(docs.bit_length() - 1)
    )

    def swap(values, stage):
        axis, mask = stage
        return lax.ppermute(values, axis, [(i, i ^ mask) for i in range(sizes[axis])])

    rows = tokens.reshape(row_count, length, width)
    lengths = pair_lengths.reshape(row_count, pairs)
    spot = lax.broadcasted_iota(jnp.int32, (group, width), 0)
    gains = jnp.pad(bias_table.T, ((4, group - 4 - heads), (0, width - buckets)))
    for i, vector in enumerate((first_gain, second_gain, final_gain, score_vector)):
        gains = jnp.where(spot == i, vector[None, :], gains)
    members = list_ids.shape[1]
    known = jnp.pad(list_ids, ((0, 0), (0, members))) + jnp.pad(relevance, ((0, 0), (members, 0)))
    outs = path_call(
        rows, lengths, known, gains, heads, buckets,
        (query_weight, key_weight, value_weight, output_weight, inner_weight, outer_weight),
    )
    pay, factors, n1, probs, dl, turned, yk, yv, qf, gctx, z, vz, ga, a2, fhat, yq = outs[:16]
    wq, wk, wv, wo, wi, wf, scores = outs[16:]

    tie = lax.optimization_barrier
    gather_order = tuple(reversed(stages))

    rows_left = list(gather_order)
    come = None
    projected, bias, spreads = [], None, []
    for i, stage in enumerate(gather_order):
        if i < row_count:
            n1, pay = tie((n1, pay))
            come_pay = swap(pay, stage)
            made = project_call(i, n1, wq, wk, wv)
            come_pay, made = tie((come_pay, tuple(made)))
            projected += made
        elif i == row_count:
            gains, pay = tie((gains, pay))
            come_pay = swap(pay, stage)
            bias = bias_call(heads, buckets, gains)
            come_pay, bias = tie((come_pay, bias))
        elif i == row_count + 1:
            probs, pay = tie((probs, pay))
            come_pay = swap(pay, stage)
            spreads.append(spread_call(0, length, lengths, probs, dl, yk, yv, yq))
            come_pay, spreads = tie((come_pay, spreads))
        else:
            come_pay = swap(pay, stage)
        pay = join(pay, come_pay)
        if i == 0:
            factors, pay = tie((factors, pay))
            come = swap(factors, rows_left.pop(0))
        elif i == 2:
            come, pay = tie((come, pay))
            factors = join(factors, come)
            come = swap(factors, rows_left.pop(0))
    come, pay = tie((come, pay))
    left, right = split(factors, come)
    count = row_count * pairs
    dims = (stages, docs, lists, docs // 2, count, heads, buckets)
    keep, send, g_all, g_own, smalls = terms_call(
        dims, pay, z, vz, qf, gctx, turned, a2, fhat, gains
    )
    piece = keep.shape[1]
    cut = cut_stages(stages, width)
    rest = stages[len(cut) :]
    for stage in cut[:-4]:
        keep, send = fold(keep, swap(send, stage))
    probs, send = tie((probs, send))
    arrived = swap(send, cut[-4])
    for r in range(1, row_count):
        spreads.append(spread_call(r, length, lengths, probs, dl, yk, yv, yq))
    arrived, spreads = tie((arrived, spreads))
    sums = fold_columns(keep, arrived)

    third, fourth = rows_left[:2]
    bias, sums, left, right = tie((bias, sums, left, right))
    arrived = swap(sums[1], cut[-3]), swap(sums[3], cut[-2])
    come = swap(left, third), swap(right, fourth)
    attended = attention_call(lengths, rows, bias, wo, projected)
    arrived, come, attended = tie((arrived, come, attended))
    keep_left, send_left = fold(sums[0], arrived[0])
    keep_right, send_right = fold(sums[2], arrived[1])
    left, right = join(left, come[0]), join(right, come[1])

    attended, send_left, send_right, left, right = tie(
        (attended, send_left, send_right, left, right)
    )
    arrived = swap(send_left, cut[-2]), swap(send_right, cut[-3])
    come = swap(left, fourth), swap(right, third)
    encoded = feed_call(0, attended, gains, wi, wf, None)
    arrived, encoded = tie((arrived, encoded))
    keep, send = fold_pair(keep_left, arrived[0], keep_right, arrived[1])

    spreads, send, encoded = tie((spreads, send, encoded))
    arrived = swap(send, cut[-1])
    grads, first_sum = tokens_grad_call(
        lengths, rows, g_own, ga, gains, spreads
    )
    arrived, grads, first_sum = tie((arrived, grads, first_sum))
    held = close(keep, arrived, smalls, first_sum)

    for stage in rest[:-1]:
        held = add(held, swap(held, stage))
    attended, held = tie((attended, held))
    arrived = swap(held, rest[-1])
    held, come = tie((held, come))
    left, right = join(left, come[0]), join(right, come[1])
    for stage in rows_left[2:-1]:
        left, right = join(left, swap(left, stage)), join(right, swap(right, stage))
    come = swap(left, rows_left[-1]), swap(right, rows_left[-1])
    attended, left = tie((attended, left))
    encoded = feed_call(1, attended, gains, wi, wf, encoded)
    arrived, encoded, come = tie((arrived, encoded, come))
    held = add(held, arrived)
    held_rows = (left, come[0], right, come[1])

    held, held_rows = tie((held, held_rows))
    arrived = swap(held, cut[-1])
    products = tuple(outer_call(0, held_rows, g_all, wi, wf, ()))
    products, arrived = tie((products, arrived))
    query_grad, output_grad = products
    left, right = split(held, arrived)

    left, right, held_rows = tie((left, right, held_rows))
    come = swap(left, cut[-2]), swap(right, cut[-3])
    wide = tuple(outer_call(1, held_rows, g_all, wi, wf, ()))
    wide, come = tie((wide, come))
    left, right = join(left, come[0]), join(right, come[1])

    left, right, wide = tie((left, right, wide))
    come = swap(left, cut[-3]), swap(right, cut[-2])
    wide = outer_call(2, held_rows, g_all, wi, wf, wide)
    wide, come = tie((tuple(wide), come))
    held = weave(left, come[0], right, come[1])

    for stage in reversed(cut[1:-3]):
        held = join(held, swap(held, stage))
    come = swap(held, cut[0])
    key_grad, value_grad, small_sums = last_call(cut, 0, held, piece, buckets, heads, ())
    (
        key_grad, value_grad, first_grad, second_grad, final_grad, vector_grad, table_grad
    ) = last_call(cut, 1, come, piece, buckets, heads, (small_sums, key_grad, value_grad))
    inner_grad, outer_grad = wide
    return (
        encoded.reshape(tokens.shape),
        scores.reshape(1, row_count, pairs),
        grads.reshape(tokens.shape),
        first_grad,
        query_grad,
        key_grad,
        value_grad,
        output_grad,
        table_grad.T,
        second_grad,
        inner_grad,
        outer_grad,
        final_grad,
        vector_grad,
    )


def solution(mesh):
    placed = P("lists", "docs", None, None)
    return jax.shard_map(
        functools.partial(shards, mesh.shape["docs"], mesh.shape["lists"]),
        mesh=mesh,
        in_specs=(placed, P("lists", "docs", None), P("lists", None), P("lists", None)) + (P(),) * 11,
        out_specs=(placed, P("lists", "docs", None), placed) + (P(),) * 11,
        check_vma=False,
    )
```

```python
import functools
import math

import jax
import jax.numpy as jnp
from jax import lax
from jax.experimental import pallas as pl
from jax.experimental.pallas import tpu as pltpu
from jax.sharding import PartitionSpec as P

epsilon = 1e-06
negative = -1000000000.0
highest = lax.Precision.HIGHEST
limits = (12, 16, 23, 32, 46, 64, 91)
f32 = jnp.float32
bf16 = jnp.bfloat16
window = 128
reach = 144
lanes_path = 256
group = 16
mega = 1 << 20
curve = math.sqrt(2.0 / math.pi)
cubic = 0.044715
whole = pl.BlockSpec(memory_space=pltpu.VMEM)
scalars = pl.BlockSpec(memory_space=pltpu.SMEM)
outside = pl.BlockSpec(memory_space=pl.ANY)


def mm(a, b):
    return lax.dot_general(a, b, (((1,), (0,)), ((), ())), preferred_element_type=f32)


def mm_nt(a, b):
    return lax.dot_general(a, b, (((1,), (1,)), ((), ())), preferred_element_type=f32)


def mm_tn(a, b):
    return lax.dot_general(a, b, (((0,), (0,)), ((), ())), preferred_element_type=f32)


def as_row(gains, i):
    return gains[i : i + 1, :]


def iota(shape, axis):
    return lax.broadcasted_iota(jnp.int32, shape, axis)


def bucket_of(offsets):
    upper_half = jnp.where(offsets > 0, 16, 0)
    distance = jnp.abs(offsets)
    beyond = jnp.full(offsets.shape, 8, jnp.int32)
    for border in limits:
        beyond = beyond + jnp.where(distance >= border, 1, 0)
    return upper_half + jnp.where(distance < 8, distance, beyond)


def rms_factor(values):
    return lax.rsqrt(jnp.mean(values * values, axis=-1, keepdims=True) + epsilon)


def norm_back(normed, factor, upstream):
    return factor * (upstream - normed * jnp.mean(upstream * normed, axis=-1, keepdims=True))


def half_bent(values, square):
    return 0.5 * jnp.tanh(values * (square * (curve * cubic) + curve)) + 0.5


def gelu(values):
    return values * half_bent(values, values * values)


def gelu_pair(values):
    square = values * values
    half = half_bent(values, square)
    value = half * values
    steep = (value - value * half) * (square * (6.0 * curve * cubic) + 2.0 * curve)
    return value, half + steep


def bias_vector(table, lanes, origin):
    buckets = table.shape[1]
    buckets_at = bucket_of(iota((buckets, lanes), 1) - origin)
    chosen = jnp.where(buckets_at == iota((buckets, lanes), 0), 1.0, 0.0)
    return lax.dot_general(
        table, chosen, (((1,), (0,)), ((), ())), precision=highest, preferred_element_type=f32
    )


def cast_rows(target, source, chunk):
    rows = source.shape[0]

    def step(i, carry):
        at = pl.ds(pl.multiple_of(i * chunk, chunk), chunk)
        target[at, :] = source[at, :].astype(bf16)
        return carry

    lax.fori_loop(0, rows // chunk, step, 0)


def starts_of(lengths, row, count):
    out, at = [], 0
    for i in range(count):
        out.append((at, lengths[row, i]))
        at = at + lengths[row, i]
    return out


def path_kernel(
    dims,
    lengths, known,
    tokens_in, gains,
    wq_in, wk_in, wv_in, wo_in, wi_in, wf_in,
    pay, factors, n1_out, probs_out, dl_out, turned_out, yk_out, yv_out, qf_out, gctx_out, z_out, vz_out,
    ga_out, a2_out, fhat_out, yq_out,
    wq, wk, wv, wo, wi, wf, scores_out,
    tokens, square, padded, first, gather_z, logits, expand, wide_z,
    in_sems, tokens_sem,
):
    rows, length, width, pairs, heads, buckets = dims
    members = known.shape[1] // 2
    count = rows * pairs
    parts = wi.shape[1] // width
    slots = square.shape[0]
    chunks = [(wq_in, wq), (wk_in, wk), (wv_in, wv), (wo_in, wo)]
    for i in range(parts):
        at = pl.ds(i * width, width)
        chunks.append((wi_in.at[:, at], wi.at[:, at]))
    for i in range(parts):
        at = pl.ds(i * width, width)
        chunks.append((wf_in.at[at, :], wf.at[at, :]))

    def load_of(i):
        return pltpu.make_async_copy(chunks[i][0], square.at[i % slots], in_sems.at[i % slots])

    tokens_load = pltpu.make_async_copy(tokens_in, tokens, tokens_sem)
    tokens_load.start()
    order = iter(range(slots))

    def request(count):
        for _ in range(count):
            load_of(next(order)).start()

    request(2)
    tokens_load.wait()
    request(2)

    gain = as_row(gains, 0)
    for r in range(rows):
        padded[r, length:, :] = jnp.zeros((reach, width), bf16)

        def norm_step(i, carry, r=r):
            at = pl.ds(pl.multiple_of(i * 64, 64), 64)
            x = tokens[r, at, :]
            n = (x * rms_factor(x) * gain).astype(bf16)
            n1_out[r, at, :] = n
            padded[r, at, :] = n
            return carry

        lax.fori_loop(0, length // 64, norm_step, 0)
        request(2)
    first[...] = jnp.zeros(first.shape, f32)
    pieces = []
    for r in range(rows):
        for at, size in starts_of(lengths, r, pairs):
            p = len(pieces)
            shift = at & (group - 1)
            pieces.append((r, pl.multiple_of(at - shift, group), shift, size))
            first[p : p + 1, :] = tokens[r, pl.ds(at, 1), :]

    def nearby(p):
        r, base, _, _ = pieces[p]
        return padded[r, pl.ds(base, reach), :]

    spots = [slice(p * group, (p + 1) * group) for p in range(count)]
    head_rows = iota((group, width), 0) == lax.shift_right_logical(
        iota((group, width), 1), int(math.log2(width // heads))
    )

    def widen(values):
        for p in range(count):
            expand[p * group : (p + 1) * group, :] = jnp.where(
                head_rows, values[p : p + 1, :], 0.0
            ).astype(bf16)

    def narrow(target):
        target[...] = jnp.zeros(target.shape, f32)
        for p in range(count):
            block = wide_z[p * group : (p + 1) * group, :]
            target[p : p + 1, :] = jnp.sum(
                jnp.where(head_rows, block, 0.0), axis=0, keepdims=True
            )

    def take(i):
        load_of(i).wait()
        cast_rows(chunks[i][1], square.at[i % slots], 64)
        if i < 4:
            request(1)

    take(0)
    n1_first = (first[...] * rms_factor(first[...]) * gain).astype(bf16)
    q_first = mm(n1_first, wq[...]).astype(bf16)
    qf_out[...] = q_first
    widen(q_first.astype(f32))
    take(1)
    yk_out[...] = mm_nt(expand[...], wk[...]).astype(bf16)
    position = bias_vector(gains[4 : 4 + heads, :buckets], lanes_path, 0)
    position = jnp.concatenate([position, jnp.zeros((group - heads, lanes_path), f32)], axis=0)
    lane = iota((group, lanes_path), 1)
    for p, (_, _, shift, size) in enumerate(pieces):
        logits[spots[p], :reach] = mm_nt(yk_out[spots[p], :], nearby(p))
        block = logits[spots[p], :] + pltpu.roll(position, shift, 1)
        inside = jnp.logical_and(lane >= shift, lane < shift + size)
        logits[spots[p], :] = jnp.where(inside, block, negative)
    take(2)
    take(3)
    scores_in = logits[...]
    peak = jnp.max(scores_in, axis=-1, keepdims=True)
    raised = jnp.exp(scores_in - peak)
    probs = raised / jnp.sum(raised, axis=-1, keepdims=True)
    probs_out[...] = probs.astype(bf16)
    for p in range(count):
        vz_out[spots[p], :] = mm(probs_out[spots[p], :reach], nearby(p)).astype(bf16)
    wide_z[...] = mm(vz_out[...], wv[...])
    narrow(gather_z)
    context = gather_z[...].astype(bf16)
    attended = first[...] + mm(context, wo[...])
    scale_two = rms_factor(attended)
    second = attended * scale_two
    normed_two = (second * as_row(gains, 1)).astype(bf16)
    for i in range(parts):
        take(4 + i)
    value, slope = gelu_pair(mm(normed_two, wi[...]))
    for i in range(parts):
        take(4 + parts + i)
    encoded = attended + mm(value.astype(bf16), wf[...])
    scale_final = rms_factor(encoded)
    final_hat = encoded * scale_final
    fhat_out[...] = final_hat
    unit = as_row(gains, 3) * as_row(gains, 2)
    score_col = jnp.sum(final_hat * unit, axis=-1, keepdims=True)
    square_lane = iota((group, 128), 1)
    row = jnp.sum(
        jnp.where(square_lane == iota((group, 128), 0), score_col, 0.0), axis=0, keepdims=True
    )
    for r in range(rows):
        scores_out[r : r + 1, :] = row[:, r * pairs : (r + 1) * pairs]
    row_lane = iota((1, 128), 1)
    place = lax.axis_index("docs") * count
    for i in range(count):
        row = jnp.where(row_lane == group + i, known[0, place + i].astype(f32), row)
        row = jnp.where(row_lane == 2 * group + i, known[0, members + place + i].astype(f32), row)
    pay[...] = row

    grad_encoded = norm_back(final_hat, scale_final, jnp.broadcast_to(unit, final_hat.shape))
    grad_branch = grad_encoded.astype(bf16)
    grad_preact = (mm_nt(grad_branch, wf[...]) * slope).astype(bf16)
    grad_normed_two = mm_nt(grad_preact, wi[...])
    a2_out[...] = second * grad_normed_two
    grad_attended = grad_encoded + norm_back(second, scale_two, grad_normed_two * as_row(gains, 1))
    ga_out[...] = grad_attended
    grad_attn = grad_attended.astype(bf16)
    grad_context = mm_nt(grad_attn, wo[...])
    gctx_out[...] = grad_context
    widen(grad_context)
    yv_out[...] = mm_nt(expand[...], wv[...]).astype(bf16)
    logits[...] = jnp.zeros(logits.shape, f32)
    for p in range(count):
        logits[spots[p], :reach] = mm_nt(yv_out[spots[p], :], nearby(p))
    grad_probs = logits[...]
    grad_logits = probs * (grad_probs - jnp.sum(probs * grad_probs, axis=-1, keepdims=True))
    dl_out[...] = grad_logits.astype(bf16)
    for p, (_, _, shift, _) in enumerate(pieces):
        rounded = dl_out[spots[p], :]
        z_out[spots[p], :] = mm(rounded[:, :reach], nearby(p))
        turned = pltpu.roll(rounded.astype(f32), (lanes_path - shift) & (lanes_path - 1), 1)
        turned_out[spots[p], :] = turned[:, :window]
    wide_z[...] = mm(z_out[...].astype(bf16), wk[...])
    narrow(gather_z)
    grad_query = gather_z[...].astype(bf16)
    yq_out[...] = mm_nt(grad_query, wq[...])
    span, half = 3 * width // 2, width // 2
    for i, member in enumerate((n1_first, grad_query, context, grad_attn, normed_two, grad_branch)):
        member = member.astype(f32)
        tail = member[8:, :]
        tail = jnp.where(
            iota((8, half), 0) < 4, tail[:, :half], pltpu.roll(tail[:, half:], 4, 0)
        )
        factors[0, :, i * span : i * span + width] = member[:8].astype(bf16)
        factors[0, :, i * span + width : (i + 1) * span] = tail.astype(bf16)


def path_call(tokens, lengths, known, gains, heads, buckets, weights):
    rows, length, width = tokens.shape
    pairs = lengths.shape[1]
    combos = rows * pairs * group
    shape = jax.ShapeDtypeStruct
    outs = [
        shape((1, 128), f32),
        shape((1, 8, 9 * width), bf16),
        shape((rows, length, width), bf16),
        shape((combos, lanes_path), bf16),
        shape((combos, lanes_path), bf16),
        shape((combos, window), f32),
        shape((combos, width), bf16),
        shape((combos, width), bf16),
        shape((group, width), bf16),
        shape((group, width), f32),
        shape((combos, width), f32),
        shape((combos, width), bf16),
        shape((group, width), f32),
        shape((group, width), f32),
        shape((group, width), f32),
        shape((group, width), f32),
    ]
    low = [shape(w.shape, bf16) for w in weights] + [shape((rows, pairs), f32)]
    return pl.pallas_call(
        functools.partial(path_kernel, (rows, length, width, pairs, heads, buckets)),
        out_shape=outs + low,
        in_specs=[scalars] * 2 + [outside, whole] + [outside] * 6,
        out_specs=[whole] * (len(outs) + len(low)),
        scratch_shapes=[
            pltpu.VMEM(tokens.shape, f32),
            pltpu.VMEM((12, width, width), f32),
            pltpu.VMEM((rows, length + reach, width), bf16),
            pltpu.VMEM((group, width), f32),
            pltpu.VMEM((group, width), f32),
            pltpu.VMEM((combos, lanes_path), f32),
            pltpu.VMEM((combos, width), bf16),
            pltpu.VMEM((combos, width), f32),
            pltpu.SemaphoreType.DMA((12,)),
            pltpu.SemaphoreType.DMA,
        ],
        compiler_params=pltpu.CompilerParams(vmem_limit_bytes=45 * mega),
        cost_estimate=pl.CostEstimate(flops=int(9e9), bytes_accessed=int(5e7), transcendentals=0),
        name="path",
    )(lengths, known, tokens, gains, *weights)


def code_of(stages, indices):
    total = len(stages)
    code = 0
    for s, (axis, mask) in enumerate(stages):
        bit = jnp.where((indices[axis] & mask) != 0, 1, 0) if not isinstance(
            indices[axis], int
        ) else (1 if indices[axis] & mask else 0)
        code = code + bit * (1 << (total - 1 - s))
    return code


def cut_stages(stages, width):
    count = 3 + sum(axis == "lists" for axis, _ in stages)
    while (2 * width) % (group << count):
        count -= 1
    return stages[:count]


def own_code(stages):
    return code_of(stages, {axis: lax.axis_index(axis) for axis in ("docs", "lists")})


def terms_kernel(
    dims,
    pay, z, vz, qf, gctx, dl, a2, fhat, gains,
    keep, send, g_all, g_own, smalls,
    term, left, right,
):
    stages, docs, lists, list_count, count, heads, buckets = dims
    width = z.shape[1]
    everything = pay[...]
    lane = iota(everything.shape, 1)
    score = everything
    names = pltpu.roll(everything, 128 - group, 1)
    label = pltpu.roll(everything, 128 - 2 * group, 1)
    used = lane < count
    part = lax.shift_right_logical(iota(everything.shape, 0), int(math.log2(docs)))
    key = jnp.where(used, part * list_count + names.astype(jnp.int32), -1)

    def total_of(values):
        return jnp.sum(jnp.sum(values, axis=1, keepdims=True), axis=0, keepdims=True)

    def top_step(k, top):
        member = key == k
        best = jnp.max(
            jnp.max(jnp.where(member, score, negative), axis=1, keepdims=True),
            axis=0, keepdims=True,
        )
        return jnp.where(member, best, top)

    keys = lists * list_count
    unroll = keys if keys <= 16 else 4
    top = lax.fori_loop(0, keys, top_step, score, unroll=unroll)
    raised = jnp.exp(score - top)

    def sum_step(k, carry):
        total, gain = carry
        member = key == k
        return (
            jnp.where(member, total_of(jnp.where(member, raised, 0.0)), total),
            jnp.where(member, total_of(jnp.where(member, label, 0.0)), gain),
        )

    ones = jnp.ones(everything.shape, f32)
    total, gain = lax.fori_loop(0, keys, sum_step, (ones, ones), unroll=unroll)
    grads = jnp.where(used, raised / total * gain - label, 0.0)
    g_all[...] = grads
    own = grads[0:1, :]
    g_own[...] = jnp.broadcast_to(own, g_own.shape)

    combos = count * group
    pair_of = lax.shift_right_logical(iota((combos, 128), 0), int(math.log2(group)))
    g_combo = jnp.sum(jnp.where(iota((combos, 128), 1) == pair_of, own, 0.0), axis=1, keepdims=True)
    g_pair = jnp.sum(
        jnp.where(iota((group, 128), 1) == iota((group, 128), 0), own, 0.0), axis=1, keepdims=True
    )
    head_rows = iota((group, width), 0) == lax.shift_right_logical(
        iota((group, width), 1), int(math.log2(width // heads))
    )
    queries = qf[...].astype(f32)
    upstream = gctx[...] * g_pair
    for p in range(count):
        at = slice(p * group, (p + 1) * group)
        right[0, at, :] = jnp.where(head_rows, queries[p : p + 1, :], 0.0).astype(bf16)
        right[1, at, :] = jnp.where(head_rows, upstream[p : p + 1, :], 0.0).astype(bf16)
    left[...] = (z[...] * g_combo).astype(bf16)
    term[0:width, :] = mm_tn(left[...], right[0])
    term[width : 2 * width, :] = mm_tn(vz[...], right[1])

    half, piece = keep.shape[0], keep.shape[1]
    blocks = width // piece
    mine = own_code(stages[: half.bit_length()])

    def piece_step(r, carry, target, base):
        owner = mine ^ (base + r)
        side = lax.shift_right_logical(owner, int(math.log2(blocks)))
        at = side * width + (owner & (blocks - 1)) * piece
        target[r] = term[pl.ds(pl.multiple_of(at, group), piece), :].astype(bf16)
        return carry

    lax.fori_loop(0, half, functools.partial(piece_step, target=send, base=half), 0)
    lax.fori_loop(0, half, functools.partial(piece_step, target=keep, base=0), 0)

    smalls[...] = jnp.zeros(smalls.shape, f32)
    smalls[0:1, :] = jnp.sum(a2[...] * g_pair, axis=0, keepdims=True)
    hats = jnp.sum(fhat[...] * g_pair, axis=0, keepdims=True)
    smalls[1:2, :] = hats * as_row(gains, 3)
    smalls[2:3, :] = hats * as_row(gains, 2)
    weighted = dl[...] * g_combo
    summed = weighted[0:group, :]
    for p in range(1, count):
        summed = summed + weighted[p * group : (p + 1) * group, :]
    spots = iota((window, width), 1)
    hot = jnp.where(bucket_of(iota((window, width), 0)) == (spots & (buckets - 1)), 1.0, 0.0)
    spread = lax.dot_general(
        summed, hot, (((1,), (0,)), ((), ())), precision=highest, preferred_element_type=f32
    )
    row_of = lax.shift_right_logical(iota((group, width), 1), int(math.log2(buckets)))
    smalls[3:4, :] = jnp.sum(
        jnp.where(row_of == iota((group, width), 0), spread, 0.0), axis=0, keepdims=True
    )


def terms_call(dims, pay, z, vz, qf, gctx, dl, a2, fhat, gains):
    stages, docs, lists, list_count, count, heads, buckets = dims
    devices = docs * lists
    combos, width = z.shape
    pieces = 1 << len(cut_stages(stages, width))
    piece = 2 * width // pieces
    shape = jax.ShapeDtypeStruct
    half = shape((pieces // 2, piece, width), bf16)
    return pl.pallas_call(
        functools.partial(terms_kernel, dims),
        out_shape=[
            half, half,
            shape((devices, 128), f32),
            shape((8, 128), f32),
            shape((8, width), f32),
        ],
        in_specs=[whole] * 9,
        out_specs=[whole] * 5,
        scratch_shapes=[
            pltpu.VMEM((2 * width, width), f32),
            pltpu.VMEM((combos, width), bf16),
            pltpu.VMEM((2, combos, width), bf16),
        ],
        compiler_params=pltpu.CompilerParams(vmem_limit_bytes=10 * mega),
        cost_estimate=pl.CostEstimate(flops=int(4e9), bytes_accessed=int(1e7), transcendentals=0),
        name="terms",
    )(pay, z, vz, qf, gctx, dl, a2, fhat, gains)


def project_kernel(row, n1, wq, wk, wv, q, k, v):
    for target, low in ((q, wq), (k, wk), (v, wv)):
        target[...] = mm(n1[row], low[...]).astype(bf16)


def project_call(row, n1, wq, wk, wv):
    return pl.pallas_call(
        functools.partial(project_kernel, row),
        out_shape=[jax.ShapeDtypeStruct(n1.shape[1:], bf16)] * 3,
        in_specs=[whole] * 4,
        out_specs=[whole] * 3,
        compiler_params=pltpu.CompilerParams(vmem_limit_bytes=12 * mega),
        cost_estimate=pl.CostEstimate(flops=int(2e9), bytes_accessed=int(4e6), transcendentals=0),
        name=f"project_{row}",
    )(n1, wq, wk, wv)


def bias_kernel(heads, buckets, gains, bias):
    lanes = 4 * window
    vector = bias_vector(gains[4 : 4 + heads, :buckets], lanes, window)
    for h in range(heads):
        bias[h] = pltpu.roll(
            jnp.broadcast_to(vector[h : h + 1, :], (window, lanes)), 0, 1, stride=1, stride_axis=0
        )[:, : 3 * window]


def bias_call(heads, buckets, gains):
    return small_call(
        functools.partial(bias_kernel, heads, buckets), "bias",
        jax.ShapeDtypeStruct((heads, window, 3 * window), f32), gains,
    )


def attention_kernel(
    lengths, tokens_in, bias, wo, *rest
):
    out, tokens, ctx, qseg, kseg, sem = rest[-6:]
    rows, length, width = tokens.shape
    heads = bias.shape[0]
    pairs = lengths.shape[1]
    load = pltpu.make_async_copy(tokens_in, tokens, sem)
    load.start()
    tiles = length // window
    half = iota((2 * window, window), 1) < (width // heads)
    left = half[:window]
    upper = iota((2 * window, window), 0) < window
    chosen = half == upper

    def segment(positions, ends):
        total = jnp.zeros(positions.shape, jnp.int32)
        for end in ends:
            total = total + jnp.where(positions >= end, 1, 0)
        return total

    wide = iota((length, window), 1)
    units = []
    for row in range(rows):
        for j in range(tiles):
            for pair in range(heads // 2):
                units.append((row, j, pair))
    ones = jnp.ones((3 * window, window), bf16)

    def begin(row):
        ends = [at + size for at, size in starts_of(lengths, row, pairs)]
        seg = segment(iota((length, 1), 0), ends)
        qseg[...] = jnp.where(seg == wide, 1.0, 0.0).astype(bf16)
        kseg[...] = jnp.where(jnp.logical_and(seg != wide, wide <= pairs), negative, 0.0).astype(bf16)

    def spans(j):
        t0 = j * window
        k0 = max(j - 1, 0) * window
        k1 = min(j + 2, tiles) * window
        return t0, k0, k1

    def raw_of(row, j, pair):
        t0, k0, k1 = spans(j)
        cols = slice(pair * window, (pair + 1) * window)
        both = rest[3 * row][t0 : t0 + window, cols]
        stacked = jnp.concatenate([both, both], axis=0)
        stacked = jnp.where(chosen, stacked, jnp.zeros_like(stacked))
        mark = qseg[t0 : t0 + window, :]
        return mm_nt(
            jnp.concatenate([stacked, jnp.concatenate([mark, mark], axis=0)], axis=1),
            jnp.concatenate([rest[3 * row + 1][k0:k1, cols], kseg[k0:k1, :]], axis=1),
        )

    def finish(row, j, pair, raw):
        t0, k0, k1 = spans(j)
        off = k0 - (t0 - window)
        cols = slice(pair * window, (pair + 1) * window)
        probs = []
        for side in range(2):
            part = raw[side * window : (side + 1) * window]
            part = part + bias[2 * pair + side, :, off : off + k1 - k0]
            peak = jnp.max(part, axis=-1, keepdims=True)
            probs.append(jnp.exp(part - peak).astype(bf16))
        mixed = mm(
            jnp.concatenate(probs, axis=0),
            jnp.concatenate([rest[3 * row + 2][k0:k1, cols], ones[: k1 - k0]], axis=1),
        )
        ctx[t0 : t0 + window, cols] = jnp.where(
            left,
            mixed[:window, :window] / mixed[:window, window:],
            mixed[window:, :window] / mixed[window:, window:],
        ).astype(bf16)

    def close_row(row):
        if row == 0:
            load.wait()
        out[row] = tokens[row] + mm(ctx[...], wo[...])

    for row in range(rows):
        begin(row)
        last = None
        for unit in units:
            if unit[0] != row:
                continue
            raw = raw_of(*unit)
            if last is not None:
                finish(*last)
            last = unit + (raw,)
        finish(*last)
        close_row(row)


def attention_call(lengths, tokens, bias, wo, projected):
    rows, length, width = tokens.shape
    return pl.pallas_call(
        attention_kernel,
        out_shape=jax.ShapeDtypeStruct(tokens.shape, f32),
        in_specs=[scalars, outside] + [whole] * (2 + len(projected)),
        out_specs=whole,
        scratch_shapes=[
            pltpu.VMEM(tokens.shape, f32),
            pltpu.VMEM((length, width), bf16),
            pltpu.VMEM((length, window), bf16),
            pltpu.VMEM((length, window), bf16),
            pltpu.SemaphoreType.DMA,
        ],
        compiler_params=pltpu.CompilerParams(vmem_limit_bytes=14 * mega),
        cost_estimate=pl.CostEstimate(
            flops=int(1e10), bytes_accessed=int(1e7), transcendentals=int(8e6)
        ),
        name="attention",
    )(lengths, tokens, bias, wo, *projected)


def feed_kernel(row, attended, gains, wi, wf, held, out, normed, total, sem):
    length, width = total.shape
    tile, chunk = 256, 512
    x = attended[row]
    normed[...] = (x * rms_factor(x) * as_row(gains, 1)).astype(bf16)
    total[...] = x

    def finish(t, c, ahead):
        total[t, :] += mm(gelu(ahead).astype(bf16), wf[c, :])

    last = None
    for c in range(wi.shape[1] // chunk):
        for t in range(length // tile):
            t_at, c_at = slice(t * tile, (t + 1) * tile), slice(c * chunk, (c + 1) * chunk)
            ahead = mm(normed[t_at, :], wi[:, c_at])
            if last is not None:
                finish(*last)
            last = (t_at, c_at, ahead)
    finish(*last)
    store = pltpu.make_async_copy(total, out.at[row], sem)
    store.start()
    store.wait()


def feed_call(row, attended, gain, wi, wf, held):
    rows, length, width = attended.shape
    extra = [] if held is None else [held]
    kernel = functools.partial(feed_kernel, row)
    if held is None:
        kernel = lambda a, g, i, f, *rest: feed_kernel(row, a, g, i, f, None, *rest)
    return pl.pallas_call(
        kernel,
        out_shape=jax.ShapeDtypeStruct(attended.shape, f32),
        in_specs=[whole] * 4 + [outside] * len(extra),
        out_specs=outside,
        input_output_aliases={4: 0} if extra else {},
        scratch_shapes=[
            pltpu.VMEM((length, width), bf16),
            pltpu.VMEM((length, width), f32),
            pltpu.SemaphoreType.DMA,
        ],
        compiler_params=pltpu.CompilerParams(vmem_limit_bytes=12 * mega),
        cost_estimate=pl.CostEstimate(
            flops=int(1e10), bytes_accessed=int(1e7), transcendentals=int(3e6)
        ),
        name=f"feed_{row}",
    )(attended, gain, wi, wf, *extra)


def spread_kernel(row, lengths, probs, dl, yk, yv, yq, out):
    pairs = lengths.shape[1]
    out[...] = jnp.zeros(out.shape, f32)
    starts = starts_of(lengths, row, pairs)
    for i, (at, size) in enumerate(starts):
        pair = row * pairs + i
        here = slice(pair * group, (pair + 1) * group)
        left = jnp.concatenate([dl[here, :], probs[here, :]], axis=0)
        right = jnp.concatenate([yk[here, :], yv[here, :]], axis=0)
        base = pl.multiple_of(at - (at & (group - 1)), group)
        out[pl.ds(base, reach), :] += mm_tn(left, right)[:reach]
    for i, (at, size) in enumerate(starts):
        pair = row * pairs + i
        out[pl.ds(at, 1), :] += yq[pair : pair + 1, :]


def spread_call(row, length, lengths, probs, dl, yk, yv, yq):
    return pl.pallas_call(
        functools.partial(spread_kernel, row),
        out_shape=jax.ShapeDtypeStruct((length + reach, yq.shape[1]), f32),
        in_specs=[scalars] + [whole] * 5,
        out_specs=whole,
        compiler_params=pltpu.CompilerParams(vmem_limit_bytes=8 * mega),
        cost_estimate=pl.CostEstimate(flops=int(1e9), bytes_accessed=int(2e6), transcendentals=0),
        name=f"spread_{row}",
    )(lengths, probs, dl, yk, yv, yq)


def tokens_grad_kernel(dims, lengths, tokens_in, g_own, ga, gains, *rest):
    rows, length, width, pairs = dims
    spreads = rest[:rows]
    out, first_sum, tokens, sems = rest[rows:]
    loads = [
        pltpu.make_async_copy(tokens_in.at[r], tokens.at[r], sems.at[r]) for r in range(rows)
    ]
    for load in loads:
        load.start()
    own = g_own[0:1, :]
    lane = iota((1, 128), 1)
    total = jnp.zeros((1, width), f32)
    gain_row = as_row(gains, 0)
    stores = []
    for r in range(rows):
        starts = starts_of(lengths, r, pairs)
        amounts = [
            jnp.sum(jnp.where(lane == r * pairs + i, own, 0.0), axis=1, keepdims=True)
            for i in range(pairs)
        ]
        loads[r].wait()

        def step(i, carry, r=r, starts=starts, amounts=amounts):
            at = pl.ds(pl.multiple_of(i * 64, 64), 64)
            spot = i * 64 + iota((64, 1), 0)
            amount = jnp.zeros((64, 1), f32)
            for (start, size), value in zip(starts, amounts):
                inside = jnp.logical_and(spot >= start, spot < start + size)
                amount = jnp.where(inside, value, amount)
            x = tokens[r, at, :]
            factor = rms_factor(x)
            hat = x * factor
            upstream = spreads[r][at, :] * amount
            tokens[r, at, :] = norm_back(hat, factor, upstream * gain_row)
            return carry + jnp.sum(hat * upstream, axis=0, keepdims=True)

        total = lax.fori_loop(0, length // 64, step, total)
        for i, (at, size) in enumerate(starts):
            pair = r * pairs + i
            tokens[r, pl.ds(at, 1), :] += ga[pair : pair + 1, :] * amounts[i]
        store = pltpu.make_async_copy(tokens.at[r], out.at[r], sems.at[r])
        store.start()
        stores.append(store)
    first_sum[...] = total
    for store in stores:
        store.wait()


def tokens_grad_call(lengths, tokens, g_own, ga, gains, spreads):
    rows, length, width = tokens.shape
    pairs = lengths.shape[1]
    return pl.pallas_call(
        functools.partial(tokens_grad_kernel, (rows, length, width, pairs)),
        out_shape=[
            jax.ShapeDtypeStruct(tokens.shape, f32),
            jax.ShapeDtypeStruct((1, width), f32),
        ],
        in_specs=[scalars, outside] + [whole] * (3 + rows),
        out_specs=[outside, whole],
        scratch_shapes=[
            pltpu.VMEM(tokens.shape, f32),
            pltpu.SemaphoreType.DMA((rows,)),
        ],
        compiler_params=pltpu.CompilerParams(vmem_limit_bytes=12 * mega),
        cost_estimate=pl.CostEstimate(flops=int(2e9), bytes_accessed=int(1e7), transcendentals=0),
        name="tokens_grad",
    )(lengths, tokens, g_own, ga, gains, *spreads)


def outer_kernel(dims, *rest):
    part, chunk, blocks = dims
    halves = rest[:2], rest[2:4]
    g_all, wi, wf = rest[4:7]
    rest = rest[9:] if part else rest[7:]
    factors, g, branch, inner, outer, flat, out_sems = rest[2 if part else 4 :][:7]
    width, hidden = wi.shape
    steps = hidden // chunk
    mine = ((0,), (1,), range(2, steps))[part]
    needed = (4, 5) if part else range(6)
    members = factors.shape[1] // 12
    main = members * 8
    span, half = 3 * width // 2, width // 2

    def scaled(i):
        return (factors[i].astype(f32) * g[...]).astype(bf16)

    def unpack(sources, b):
        near = iota((8, half), 0) < 4
        for i in needed:
            side, at = i // 3, slice((i % 3) * span, (i % 3 + 1) * span)
            held = []
            for d in range(members):
                if side:
                    d = (d & ~12) | ((d & 4) << 1) | ((d & 8) >> 1)
                source = sources[side][d // sources[side][0].shape[0]]
                held.append(source[d % source.shape[0], :, at].astype(f32))
            for k in range(0, members, 2):
                even, odd = held[k], held[k + 1]
                factors[i, k * 8 : (k + 2) * 8, :] = jnp.concatenate(
                    [even[:, :width], odd[:, :width]], axis=0
                ).astype(bf16)
            for k in range(0, members, 4):
                tiles = []
                for j in (k, k + 2):
                    even, odd = held[j][:, width:], held[j + 1][:, width:]
                    tiles.append(
                        jnp.concatenate(
                            [
                                jnp.where(near, even, pltpu.roll(odd, 4, 0)),
                                jnp.where(near, pltpu.roll(even, 4, 0), odd),
                            ],
                            axis=1,
                        )
                    )
                at = main + k * 4
                factors[i, at : at + 16, :] = jnp.concatenate(tiles, axis=0).astype(bf16)
        same = iota((8, 128), 1) == iota((8, 128), 0)
        more = iota((8, 128), 1) == 8 + (iota((8, 128), 0) & 3)
        for d in range(members):
            here = g_all[pl.ds(b * members + d, 1), :]
            g[d * 8 : (d + 1) * 8, :] = jnp.sum(jnp.where(same, here, 0.0), axis=1, keepdims=True)
        for d in range(0, members, 2):
            both = jnp.where(
                iota((8, 128), 0) < 4,
                g_all[pl.ds(b * members + d, 1), :],
                g_all[pl.ds(b * members + d + 1, 1), :],
            )
            at = main + d * 4
            g[at : at + 8, :] = jnp.sum(jnp.where(more, both, 0.0), axis=1, keepdims=True)
        branch[...] = scaled(5)

    def put(target, values, b):
        if blocks == 1:
            target[...] = values
        else:
            target[...] = jnp.where(b == 0, values, target[...] + values)

    def each_block(one):
        if blocks == 1:
            one(0, 0)
        else:
            arrived, sem = rest[-2], rest[-1]

            def step(b, carry):
                for side in range(2):
                    for i in range(2):

                        @pl.when((b < blocks // 2) == (i == 0))
                        def _(side=side, i=i):
                            at = b - i * (blocks // 2)
                            load = pltpu.make_async_copy(
                                halves[side][i].at[pl.ds(at * members, members)],
                                arrived.at[side], sem,
                            )
                            load.start()
                            load.wait()

                unpack([[arrived.at[0]], [arrived.at[1]]], b)
                return one(b, carry)

            lax.fori_loop(0, blocks, step, 0)

    stores = {}

    def save(source, target, sem):
        store = pltpu.make_async_copy(source, target, out_sems.at[sem])
        store.start()
        stores[sem] = store

    if blocks == 1:
        unpack(halves, 0)
    if not part:
        for i, j, slot, target in ((0, 1, 0, rest[2]), (2, 3, 1, rest[3])):

            def square(b, carry, i=i, j=j, slot=slot):
                put(flat.at[slot], mm_tn(factors[i], scaled(j)), b)
                return carry

            each_block(square)
            save(flat.at[slot], target, 4 + slot)
    for c in mine:
        slot = c % 2
        at = slice(c * chunk, (c + 1) * chunk)

        def one(b, carry, slot=slot, at=at):
            value, slope = gelu_pair(mm(factors[4], wi[:, at]))
            grad = (mm_nt(branch[...], wf[at, :]) * slope).astype(bf16)
            put(inner.at[slot], mm_tn(factors[4], grad), b)
            put(outer.at[slot], mm_tn(value.astype(bf16), branch[...]), b)
            return carry

        each_block(one)
        save(inner.at[slot], rest[0].at[:, pl.ds(c * chunk, chunk)], slot)
        save(outer.at[slot], rest[1].at[pl.ds(c * chunk, chunk), :], 2 + slot)
    for store in stores.values():
        store.wait()


def outer_call(part, held_rows, g_all, wi, wf, held):
    low = held_rows[0]
    devices = 2 * low.shape[0]
    width, hidden = wi.shape
    chunk = hidden // 4
    members = min(devices, 32)
    blocks = devices // members
    block = members * 12
    shape = jax.ShapeDtypeStruct
    wide = [shape((width, hidden), f32), shape((hidden, width), f32)]
    flat = [shape((width, width), f32)] * 2
    place = whole if blocks == 1 else outside
    more = [] if blocks == 1 else [
        pltpu.VMEM((2, members) + low.shape[1:], bf16), pltpu.SemaphoreType.DMA
    ]
    return pl.pallas_call(
        functools.partial(outer_kernel, (part, chunk, blocks)),
        out_shape=wide if part else wide + flat,
        in_specs=[place] * 4 + [whole] * 3 + [outside] * len(held),
        out_specs=[outside] * (2 if part else 4),
        input_output_aliases={7: 0, 8: 1} if held else {},
        scratch_shapes=[
            pltpu.VMEM((6, block, width), bf16),
            pltpu.VMEM((block, 1), f32),
            pltpu.VMEM((block, width), bf16),
            pltpu.VMEM((2, width, chunk), f32),
            pltpu.VMEM((2, chunk, width), f32),
            pltpu.VMEM((2, width, width), f32),
            pltpu.SemaphoreType.DMA((6,)),
        ] + more,
        compiler_params=pltpu.CompilerParams(vmem_limit_bytes=28 * mega),
        cost_estimate=pl.CostEstimate(
            flops=int(1e10), bytes_accessed=int(2e7), transcendentals=int(1e6)
        ),
        name=f"outer_{part}",
    )(*held_rows, g_all, wi, wf, *held)


def small_call(kernel, name, outs, *args):
    return pl.pallas_call(
        kernel,
        out_shape=outs,
        in_specs=[whole] * len(args),
        out_specs=[whole] * len(outs) if isinstance(outs, (list, tuple)) else whole,
        compiler_params=pltpu.CompilerParams(vmem_limit_bytes=8 * mega),
        cost_estimate=pl.CostEstimate(flops=1000, bytes_accessed=int(1e6), transcendentals=0),
        name=name,
    )(*args)


def join(mine, come):
    if mine.size > 1 << 21:
        return jnp.concatenate([mine, come], axis=0)

    def kernel(a, b, out):
        out[: a.shape[0]] = a[...]
        out[a.shape[0] :] = b[...]

    shape = (2 * mine.shape[0],) + mine.shape[1:]
    return small_call(kernel, "join", jax.ShapeDtypeStruct(shape, mine.dtype), mine, come)


def fold(keep, come):
    half = keep.shape[0] // 2

    def kernel(a, b, first, second):
        for i in range(half):
            first[i] = a[i] + b[i]
            second[i] = a[half + i] + b[half + i]

    out = jax.ShapeDtypeStruct((half,) + keep.shape[1:], keep.dtype)
    return small_call(kernel, "fold", [out, out], keep, come)


def fold_columns(keep, come):
    half = keep.shape[2] // 2

    def kernel(a, b, keep_left, send_left, keep_right, send_right):
        for i in range(8):
            first, second, third = i >> 2, (i >> 1) & 1, i & 1
            total = a[i] + b[i]
            (send_left if first else keep_left)[2 * second + third] = total[:, :half]
            (send_right if second else keep_right)[2 * first + third] = total[:, half:]

    out = jax.ShapeDtypeStruct((4, keep.shape[1], half), keep.dtype)
    return tuple(small_call(kernel, "fold_columns", [out] * 4, keep, come))


def fold_pair(left, come_left, right, come_right):
    half = left.shape[2]

    def kernel(a, b, c, d, first, second):
        for i, out in enumerate((first, second)):
            out[0, :, :half] = a[i] + b[i]
            out[0, :, half:] = c[i] + d[i]

    out = jax.ShapeDtypeStruct((1, left.shape[1], 2 * half), left.dtype)
    return small_call(kernel, "fold_pair", [out, out], left, come_left, right, come_right)


def split(mine, come):
    half = mine.shape[2] // 2

    def kernel(a, b, left, right):
        for i, part in enumerate((a, b)):
            at = slice(i * count, (i + 1) * count)
            left[at] = part[:, :, :half]
            right[at] = part[:, :, half:]

    count = mine.shape[0]
    out = jax.ShapeDtypeStruct((2 * count, mine.shape[1], half), mine.dtype)
    return small_call(kernel, "split", [out, out], mine, come)


def weave(left, come_left, right, come_right):
    half = left.shape[2]

    def kernel(a, b, c, d, out):
        for i in range(8):
            first, second, third = i >> 2, (i >> 1) & 1, i & 1
            out[i, :, :half] = (b if first else a)[2 * second + third]
            out[i, :, half:] = (d if second else c)[2 * first + third]

    out = jax.ShapeDtypeStruct((8,) + left.shape[1:2] + (2 * half,), left.dtype)
    return small_call(kernel, "weave", out, left, come_left, right, come_right)


def close(keep, come, smalls, first_sum):
    rows = keep.shape[1]

    def kernel(a, b, c, d, out):
        out[0, :rows, :] = a[0] + b[0]
        low = jnp.where(iota(c.shape, 0) == 4, d[...], c[...])
        tail = jnp.concatenate([low, jnp.zeros_like(low)], axis=0)
        out[0, rows:, :] = tail.astype(bf16)

    out = jax.ShapeDtypeStruct((1, rows + group, keep.shape[2]), keep.dtype)
    return small_call(kernel, "close", out, keep, come, smalls, first_sum)


def add(mine, come):
    def kernel(a, b, out):
        out[...] = a[...] + b[...]

    return small_call(kernel, "add", jax.ShapeDtypeStruct(mine.shape, mine.dtype), mine, come)


def last_kernel(dims, held, *rest):
    stages, part, piece, heads, buckets = dims
    half, _, width = held.shape
    if part:
        earlier, rest = rest[0], rest[3:]
    sides = rest[:2]
    values, sems = rest[-2:]
    me = own_code(stages)
    blocks = width // piece
    for i in range(half):
        owner = me ^ (part * half + i)
        at = pl.multiple_of((owner & (blocks - 1)) * piece, group)
        side_of = lax.shift_right_logical(owner, int(math.log2(blocks)))
        values[i] = held[i, :piece, :].astype(f32)
        for side in range(2):

            @pl.when(side_of == side)
            def _(side=side, at=at, i=i):
                pltpu.make_async_copy(
                    values.at[i], sides[side].at[pl.ds(at, piece), :], sems.at[i]
                ).start()

    total = sum(held[i, piece:, :].astype(f32)[:8] for i in range(half))
    if part:
        total = total + earlier[...]
        for i, out in zip((4, 0, 1, 2), rest[2:6]):
            out[...] = total[i : i + 1, :].reshape(width)
        spots = iota((width, 128), 0)
        by_bucket = jnp.where((spots & (buckets - 1)) == iota((width, 128), 1), 1.0, 0.0)
        by_head = jnp.where(
            lax.shift_right_logical(iota((group, width), 1), int(math.log2(buckets)))
            == iota((group, width), 0),
            total[3:4, :], 0.0,
        )
        table = lax.dot_general(
            by_head, by_bucket, (((1,), (0,)), ((), ())),
            precision=highest, preferred_element_type=f32,
        )
        rest[6][...] = table[:heads, :buckets]
    else:
        rest[2][...] = total
    for i in range(half):
        pltpu.make_async_copy(values.at[i], sides[0].at[pl.ds(0, piece), :], sems.at[i]).wait()


def last_call(stages, part, held, piece, buckets, heads, earlier):
    half, _, width = held.shape
    shape = jax.ShapeDtypeStruct
    squares = [shape((width, width), f32)] * 2
    more = (
        [shape((width,), f32)] * 4 + [shape((heads, buckets), f32)] if part else [shape((8, width), f32)]
    )
    return pl.pallas_call(
        functools.partial(last_kernel, (stages, part, piece, heads, buckets)),
        out_shape=squares + more,
        in_specs=[whole] * (2 if part else 1) + [outside] * (2 if part else 0),
        out_specs=[outside] * 2 + [whole] * len(more),
        input_output_aliases={2: 0, 3: 1} if part else {},
        scratch_shapes=[pltpu.VMEM((half, piece, width), f32), pltpu.SemaphoreType.DMA((half,))],
        compiler_params=pltpu.CompilerParams(vmem_limit_bytes=12 * mega),
        cost_estimate=pl.CostEstimate(flops=int(1e7), bytes_accessed=int(5e6), transcendentals=0),
        name=f"last_{part}",
    )(held, *earlier)


def shards(
    docs, lists,
    tokens, pair_lengths, list_ids, relevance,
    first_gain, query_weight, key_weight, value_weight, output_weight, bias_table,
    second_gain, inner_weight, outer_weight, final_gain, score_vector,
):
    row_count, length, width = tokens.shape[1:]
    pairs = pair_lengths.shape[2]
    buckets, heads = bias_table.shape
    devices = docs * lists
    sizes = {"docs": docs, "lists": lists}
    stages = tuple(("lists", 1 << b) for b in range(lists.bit_length() - 1)) + tuple(
        ("docs", 1 << b) for b in range(docs.bit_length() - 1)
    )

    def swap(values, stage):
        axis, mask = stage
        return lax.ppermute(values, axis, [(i, i ^ mask) for i in range(sizes[axis])])

    rows = tokens.reshape(row_count, length, width)
    lengths = pair_lengths.reshape(row_count, pairs)
    spot = lax.broadcasted_iota(jnp.int32, (group, width), 0)
    gains = jnp.pad(bias_table.T, ((4, group - 4 - heads), (0, width - buckets)))
    for i, vector in enumerate((first_gain, second_gain, final_gain, score_vector)):
        gains = jnp.where(spot == i, vector[None, :], gains)
    members = list_ids.shape[1]
    known = jnp.pad(list_ids, ((0, 0), (0, members))) + jnp.pad(relevance, ((0, 0), (members, 0)))
    outs = path_call(
        rows, lengths, known, gains, heads, buckets,
        (query_weight, key_weight, value_weight, output_weight, inner_weight, outer_weight),
    )
    pay, factors, n1, probs, dl, turned, yk, yv, qf, gctx, z, vz, ga, a2, fhat, yq = outs[:16]
    wq, wk, wv, wo, wi, wf, scores = outs[16:]

    tie = lax.optimization_barrier
    gather_order = tuple(reversed(stages))

    rows_left = list(gather_order)
    come = None
    projected, bias, spreads = [], None, []
    for i, stage in enumerate(gather_order):
        if i < row_count:
            n1, pay = tie((n1, pay))
            come_pay = swap(pay, stage)
            made = project_call(i, n1, wq, wk, wv)
            come_pay, made = tie((come_pay, tuple(made)))
            projected += made
        elif i == row_count:
            gains, pay = tie((gains, pay))
            come_pay = swap(pay, stage)
            bias = bias_call(heads, buckets, gains)
            come_pay, bias = tie((come_pay, bias))
        elif i == row_count + 1:
            probs, pay = tie((probs, pay))
            come_pay = swap(pay, stage)
            spreads.append(spread_call(0, length, lengths, probs, dl, yk, yv, yq))
            come_pay, spreads = tie((come_pay, spreads))
        else:
            come_pay = swap(pay, stage)
        pay = join(pay, come_pay)
        if i == 0:
            factors, pay = tie((factors, pay))
            come = swap(factors, rows_left.pop(0))
        elif i == 2:
            come, pay = tie((come, pay))
            factors = join(factors, come)
            come = swap(factors, rows_left.pop(0))
    come, pay = tie((come, pay))
    left, right = split(factors, come)
    count = row_count * pairs
    dims = (stages, docs, lists, docs // 2, count, heads, buckets)
    keep, send, g_all, g_own, smalls = terms_call(
        dims, pay, z, vz, qf, gctx, turned, a2, fhat, gains
    )
    piece = keep.shape[1]
    cut = cut_stages(stages, width)
    rest = stages[len(cut) :]
    for stage in cut[:-4]:
        keep, send = fold(keep, swap(send, stage))
    probs, send = tie((probs, send))
    arrived = swap(send, cut[-4])
    for r in range(1, row_count):
        spreads.append(spread_call(r, length, lengths, probs, dl, yk, yv, yq))
    arrived, spreads = tie((arrived, spreads))
    sums = fold_columns(keep, arrived)

    third, fourth = rows_left[:2]
    bias, sums, left, right = tie((bias, sums, left, right))
    arrived = swap(sums[1], cut[-3]), swap(sums[3], cut[-2])
    come = swap(left, third), swap(right, fourth)
    attended = attention_call(lengths, rows, bias, wo, projected)
    arrived, come, attended = tie((arrived, come, attended))
    keep_left, send_left = fold(sums[0], arrived[0])
    keep_right, send_right = fold(sums[2], arrived[1])
    left, right = join(left, come[0]), join(right, come[1])

    attended, send_left, send_right, left, right = tie(
        (attended, send_left, send_right, left, right)
    )
    arrived = swap(send_left, cut[-2]), swap(send_right, cut[-3])
    come = swap(left, fourth), swap(right, third)
    encoded = feed_call(0, attended, gains, wi, wf, None)
    arrived, encoded = tie((arrived, encoded))
    keep, send = fold_pair(keep_left, arrived[0], keep_right, arrived[1])

    spreads, send, encoded = tie((spreads, send, encoded))
    arrived = swap(send, cut[-1])
    grads, first_sum = tokens_grad_call(
        lengths, rows, g_own, ga, gains, spreads
    )
    arrived, grads, first_sum = tie((arrived, grads, first_sum))
    held = close(keep, arrived, smalls, first_sum)

    for stage in rest[:-1]:
        held = add(held, swap(held, stage))
    attended, held = tie((attended, held))
    arrived = swap(held, rest[-1])
    held, come = tie((held, come))
    left, right = join(left, come[0]), join(right, come[1])
    for stage in rows_left[2:-1]:
        left, right = join(left, swap(left, stage)), join(right, swap(right, stage))
    come = swap(left, rows_left[-1]), swap(right, rows_left[-1])
    attended, left = tie((attended, left))
    encoded = feed_call(1, attended, gains, wi, wf, encoded)
    arrived, encoded, come = tie((arrived, encoded, come))
    held = add(held, arrived)
    held_rows = (left, come[0], right, come[1])

    held, held_rows = tie((held, held_rows))
    arrived = swap(held, cut[-1])
    products = tuple(outer_call(0, held_rows, g_all, wi, wf, ()))
    products, arrived = tie((products, arrived))
    wide, (query_grad, output_grad) = products[:2], products[2:]
    left, right = split(held, arrived)

    left, right, wide = tie((left, right, wide))
    come = swap(left, cut[-2]), swap(right, cut[-3])
    wide = tuple(outer_call(1, held_rows, g_all, wi, wf, wide))
    wide, come = tie((wide, come))
    left, right = join(left, come[0]), join(right, come[1])

    left, right, wide = tie((left, right, wide))
    come = swap(left, cut[-3]), swap(right, cut[-2])
    wide = outer_call(2, held_rows, g_all, wi, wf, wide)
    wide, come = tie((tuple(wide), come))
    held = weave(left, come[0], right, come[1])

    for stage in reversed(cut[1:-3]):
        held = join(held, swap(held, stage))
    come = swap(held, cut[0])
    key_grad, value_grad, small_sums = last_call(cut, 0, held, piece, buckets, heads, ())
    (
        key_grad, value_grad, first_grad, second_grad, final_grad, vector_grad, table_grad
    ) = last_call(cut, 1, come, piece, buckets, heads, (small_sums, key_grad, value_grad))
    inner_grad, outer_grad = wide
    return (
        encoded.reshape(tokens.shape),
        scores.reshape(1, row_count, pairs),
        grads.reshape(tokens.shape),
        first_grad,
        query_grad,
        key_grad,
        value_grad,
        output_grad,
        table_grad.T,
        second_grad,
        inner_grad,
        outer_grad,
        final_grad,
        vector_grad,
    )


def solution(mesh):
    placed = P("lists", "docs", None, None)
    return jax.shard_map(
        functools.partial(shards, mesh.shape["docs"], mesh.shape["lists"]),
        mesh=mesh,
        in_specs=(placed, P("lists", "docs", None), P("lists", None), P("lists", None)) + (P(),) * 11,
        out_specs=(placed, P("lists", "docs", None), placed) + (P(),) * 11,
        check_vma=False,
    )
```

```python
import functools
import math

import jax
import jax.numpy as jnp
from jax import lax
from jax.experimental import pallas as pl
from jax.experimental.pallas import tpu as pltpu
from jax.sharding import PartitionSpec as P

epsilon = 1e-06
negative = -1000000000.0
highest = lax.Precision.HIGHEST
limits = (12, 16, 23, 32, 46, 64, 91)
f32 = jnp.float32
bf16 = jnp.bfloat16
window = 128
reach = 144
lanes_path = 256
group = 16
mega = 1 << 20
curve = math.sqrt(2.0 / math.pi)
cubic = 0.044715
whole = pl.BlockSpec(memory_space=pltpu.VMEM)
scalars = pl.BlockSpec(memory_space=pltpu.SMEM)
outside = pl.BlockSpec(memory_space=pl.ANY)


def mm(a, b):
    return lax.dot_general(a, b, (((1,), (0,)), ((), ())), preferred_element_type=f32)


def mm_nt(a, b):
    return lax.dot_general(a, b, (((1,), (1,)), ((), ())), preferred_element_type=f32)


def mm_tn(a, b):
    return lax.dot_general(a, b, (((0,), (0,)), ((), ())), preferred_element_type=f32)


def as_row(gains, i):
    return gains[i : i + 1, :]


def iota(shape, axis):
    return lax.broadcasted_iota(jnp.int32, shape, axis)


def bucket_of(offsets):
    upper_half = jnp.where(offsets > 0, 16, 0)
    distance = jnp.abs(offsets)
    beyond = jnp.full(offsets.shape, 8, jnp.int32)
    for border in limits:
        beyond = beyond + jnp.where(distance >= border, 1, 0)
    return upper_half + jnp.where(distance < 8, distance, beyond)


def rms_factor(values):
    return lax.rsqrt(jnp.mean(values * values, axis=-1, keepdims=True) + epsilon)


def norm_back(normed, factor, upstream):
    return factor * (upstream - normed * jnp.mean(upstream * normed, axis=-1, keepdims=True))


def half_bent(values, square):
    return 0.5 * jnp.tanh(values * (square * (curve * cubic) + curve)) + 0.5


def gelu(values):
    return values * half_bent(values, values * values)


def gelu_pair(values):
    square = values * values
    half = half_bent(values, square)
    value = half * values
    steep = (value - value * half) * (square * (6.0 * curve * cubic) + 2.0 * curve)
    return value, half + steep


def bias_vector(table, lanes, origin):
    buckets = table.shape[1]
    buckets_at = bucket_of(iota((buckets, lanes), 1) - origin)
    chosen = jnp.where(buckets_at == iota((buckets, lanes), 0), 1.0, 0.0)
    return lax.dot_general(
        table, chosen, (((1,), (0,)), ((), ())), precision=highest, preferred_element_type=f32
    )


def cast_rows(target, source, chunk):
    rows = source.shape[0]

    def step(i, carry):
        at = pl.ds(pl.multiple_of(i * chunk, chunk), chunk)
        target[at, :] = source[at, :].astype(bf16)
        return carry

    lax.fori_loop(0, rows // chunk, step, 0)


def starts_of(lengths, row, count):
    out, at = [], 0
    for i in range(count):
        out.append((at, lengths[row, i]))
        at = at + lengths[row, i]
    return out


def path_kernel(
    dims,
    lengths, known,
    tokens_in, gains,
    wq_in, wk_in, wv_in, wo_in, wi_in, wf_in,
    pay, factors, n1_out, probs_out, dl_out, turned_out, yk_out, yv_out, qf_out, gctx_out, z_out, vz_out,
    ga_out, a2_out, fhat_out, yq_out,
    wq, wk, wv, wo, wi, wf, scores_out,
    tokens, square, padded, first, gather_z, logits, expand, wide_z,
    in_sems, tokens_sem,
):
    rows, length, width, pairs, heads, buckets = dims
    members = known.shape[1] // 2
    count = rows * pairs
    parts = wi.shape[1] // width
    slots = square.shape[0]
    chunks = [(wq_in, wq), (wk_in, wk), (wv_in, wv), (wo_in, wo)]
    for i in range(parts):
        at = pl.ds(i * width, width)
        chunks.append((wi_in.at[:, at], wi.at[:, at]))
    for i in range(parts):
        at = pl.ds(i * width, width)
        chunks.append((wf_in.at[at, :], wf.at[at, :]))

    def load_of(i):
        return pltpu.make_async_copy(chunks[i][0], square.at[i % slots], in_sems.at[i % slots])

    tokens_load = pltpu.make_async_copy(tokens_in, tokens, tokens_sem)
    tokens_load.start()
    order = iter(range(slots))

    def request(count):
        for _ in range(count):
            load_of(next(order)).start()

    request(2)
    tokens_load.wait()
    request(2)

    gain = as_row(gains, 0)
    for r in range(rows):
        padded[r, length:, :] = jnp.zeros((reach, width), bf16)

        def norm_step(i, carry, r=r):
            at = pl.ds(pl.multiple_of(i * 64, 64), 64)
            x = tokens[r, at, :]
            n = (x * rms_factor(x) * gain).astype(bf16)
            n1_out[r, at, :] = n
            padded[r, at, :] = n
            return carry

        lax.fori_loop(0, length // 64, norm_step, 0)
        request(2)
    first[...] = jnp.zeros(first.shape, f32)
    pieces = []
    for r in range(rows):
        for at, size in starts_of(lengths, r, pairs):
            p = len(pieces)
            shift = at & (group - 1)
            pieces.append((r, pl.multiple_of(at - shift, group), shift, size))
            first[p : p + 1, :] = tokens[r, pl.ds(at, 1), :]

    def nearby(p):
        r, base, _, _ = pieces[p]
        return padded[r, pl.ds(base, reach), :]

    spots = [slice(p * group, (p + 1) * group) for p in range(count)]
    head_rows = iota((group, width), 0) == lax.shift_right_logical(
        iota((group, width), 1), int(math.log2(width // heads))
    )

    def widen(values):
        for p in range(count):
            expand[p * group : (p + 1) * group, :] = jnp.where(
                head_rows, values[p : p + 1, :], 0.0
            ).astype(bf16)

    def narrow(target):
        target[...] = jnp.zeros(target.shape, f32)
        for p in range(count):
            block = wide_z[p * group : (p + 1) * group, :]
            target[p : p + 1, :] = jnp.sum(
                jnp.where(head_rows, block, 0.0), axis=0, keepdims=True
            )

    def take(i):
        load_of(i).wait()
        cast_rows(chunks[i][1], square.at[i % slots], 64)
        if i < 4:
            request(1)

    take(0)
    n1_first = (first[...] * rms_factor(first[...]) * gain).astype(bf16)
    q_first = mm(n1_first, wq[...]).astype(bf16)
    qf_out[...] = q_first
    widen(q_first.astype(f32))
    take(1)
    yk_out[...] = mm_nt(expand[...], wk[...]).astype(bf16)
    position = bias_vector(gains[4 : 4 + heads, :buckets], lanes_path, 0)
    position = jnp.concatenate([position, jnp.zeros((group - heads, lanes_path), f32)], axis=0)
    lane = iota((group, lanes_path), 1)
    for p, (_, _, shift, size) in enumerate(pieces):
        logits[spots[p], :reach] = mm_nt(yk_out[spots[p], :], nearby(p))
        block = logits[spots[p], :] + pltpu.roll(position, shift, 1)
        inside = jnp.logical_and(lane >= shift, lane < shift + size)
        logits[spots[p], :] = jnp.where(inside, block, negative)
    take(2)
    take(3)
    scores_in = logits[...]
    peak = jnp.max(scores_in, axis=-1, keepdims=True)
    raised = jnp.exp(scores_in - peak)
    probs = raised / jnp.sum(raised, axis=-1, keepdims=True)
    probs_out[...] = probs.astype(bf16)
    for p in range(count):
        vz_out[spots[p], :] = mm(probs_out[spots[p], :reach], nearby(p)).astype(bf16)
    wide_z[...] = mm(vz_out[...], wv[...])
    narrow(gather_z)
    context = gather_z[...].astype(bf16)
    attended = first[...] + mm(context, wo[...])
    scale_two = rms_factor(attended)
    second = attended * scale_two
    normed_two = (second * as_row(gains, 1)).astype(bf16)
    for i in range(parts):
        take(4 + i)
    value, slope = gelu_pair(mm(normed_two, wi[...]))
    for i in range(parts):
        take(4 + parts + i)
    encoded = attended + mm(value.astype(bf16), wf[...])
    scale_final = rms_factor(encoded)
    final_hat = encoded * scale_final
    fhat_out[...] = final_hat
    unit = as_row(gains, 3) * as_row(gains, 2)
    score_col = jnp.sum(final_hat * unit, axis=-1, keepdims=True)
    square_lane = iota((group, 128), 1)
    row = jnp.sum(
        jnp.where(square_lane == iota((group, 128), 0), score_col, 0.0), axis=0, keepdims=True
    )
    for r in range(rows):
        scores_out[r : r + 1, :] = row[:, r * pairs : (r + 1) * pairs]
    row_lane = iota((1, 128), 1)
    place = lax.axis_index("docs") * count
    for i in range(count):
        row = jnp.where(row_lane == group + i, known[0, place + i].astype(f32), row)
        row = jnp.where(row_lane == 2 * group + i, known[0, members + place + i].astype(f32), row)
    pay[...] = row

    grad_encoded = norm_back(final_hat, scale_final, jnp.broadcast_to(unit, final_hat.shape))
    grad_branch = grad_encoded.astype(bf16)
    grad_preact = (mm_nt(grad_branch, wf[...]) * slope).astype(bf16)
    grad_normed_two = mm_nt(grad_preact, wi[...])
    a2_out[...] = second * grad_normed_two
    grad_attended = grad_encoded + norm_back(second, scale_two, grad_normed_two * as_row(gains, 1))
    ga_out[...] = grad_attended
    grad_attn = grad_attended.astype(bf16)
    grad_context = mm_nt(grad_attn, wo[...])
    gctx_out[...] = grad_context
    widen(grad_context)
    yv_out[...] = mm_nt(expand[...], wv[...]).astype(bf16)
    logits[...] = jnp.zeros(logits.shape, f32)
    for p in range(count):
        logits[spots[p], :reach] = mm_nt(yv_out[spots[p], :], nearby(p))
    grad_probs = logits[...]
    grad_logits = probs * (grad_probs - jnp.sum(probs * grad_probs, axis=-1, keepdims=True))
    dl_out[...] = grad_logits.astype(bf16)
    for p, (_, _, shift, _) in enumerate(pieces):
        rounded = dl_out[spots[p], :]
        z_out[spots[p], :] = mm(rounded[:, :reach], nearby(p))
        turned = pltpu.roll(rounded.astype(f32), (lanes_path - shift) & (lanes_path - 1), 1)
        turned_out[spots[p], :] = turned[:, :window]
    wide_z[...] = mm(z_out[...].astype(bf16), wk[...])
    narrow(gather_z)
    grad_query = gather_z[...].astype(bf16)
    yq_out[...] = mm_nt(grad_query, wq[...])
    span, half = 3 * width // 2, width // 2
    for i, member in enumerate((n1_first, grad_query, context, grad_attn, normed_two, grad_branch)):
        member = member.astype(f32)
        tail = member[8:, :]
        tail = jnp.where(
            iota((8, half), 0) < 4, tail[:, :half], pltpu.roll(tail[:, half:], 4, 0)
        )
        factors[0, :, i * span : i * span + width] = member[:8].astype(bf16)
        factors[0, :, i * span + width : (i + 1) * span] = tail.astype(bf16)


def path_call(tokens, lengths, known, gains, heads, buckets, weights):
    rows, length, width = tokens.shape
    pairs = lengths.shape[1]
    combos = rows * pairs * group
    shape = jax.ShapeDtypeStruct
    outs = [
        shape((1, 128), f32),
        shape((1, 8, 9 * width), bf16),
        shape((rows, length, width), bf16),
        shape((combos, lanes_path), bf16),
        shape((combos, lanes_path), bf16),
        shape((combos, window), f32),
        shape((combos, width), bf16),
        shape((combos, width), bf16),
        shape((group, width), bf16),
        shape((group, width), f32),
        shape((combos, width), f32),
        shape((combos, width), bf16),
        shape((group, width), f32),
        shape((group, width), f32),
        shape((group, width), f32),
        shape((group, width), f32),
    ]
    low = [shape(w.shape, bf16) for w in weights] + [shape((rows, pairs), f32)]
    return pl.pallas_call(
        functools.partial(path_kernel, (rows, length, width, pairs, heads, buckets)),
        out_shape=outs + low,
        in_specs=[scalars] * 2 + [outside, whole] + [outside] * 6,
        out_specs=[whole] * (len(outs) + len(low)),
        scratch_shapes=[
            pltpu.VMEM(tokens.shape, f32),
            pltpu.VMEM((12, width, width), f32),
            pltpu.VMEM((rows, length + reach, width), bf16),
            pltpu.VMEM((group, width), f32),
            pltpu.VMEM((group, width), f32),
            pltpu.VMEM((combos, lanes_path), f32),
            pltpu.VMEM((combos, width), bf16),
            pltpu.VMEM((combos, width), f32),
            pltpu.SemaphoreType.DMA((12,)),
            pltpu.SemaphoreType.DMA,
        ],
        compiler_params=pltpu.CompilerParams(vmem_limit_bytes=45 * mega),
        cost_estimate=pl.CostEstimate(flops=int(9e9), bytes_accessed=int(5e7), transcendentals=0),
        name="path",
    )(lengths, known, tokens, gains, *weights)


def code_of(stages, indices):
    total = len(stages)
    code = 0
    for s, (axis, mask) in enumerate(stages):
        bit = jnp.where((indices[axis] & mask) != 0, 1, 0) if not isinstance(
            indices[axis], int
        ) else (1 if indices[axis] & mask else 0)
        code = code + bit * (1 << (total - 1 - s))
    return code


def cut_stages(stages, width):
    count = 3 + sum(axis == "lists" for axis, _ in stages)
    while (2 * width) % (group << count):
        count -= 1
    return stages[:count]


def own_code(stages):
    return code_of(stages, {axis: lax.axis_index(axis) for axis in ("docs", "lists")})


def terms_kernel(
    dims,
    pay, z, vz, qf, gctx, dl, a2, fhat, gains,
    keep, send, g_all, g_own, smalls,
    term, left, right,
):
    stages, docs, lists, list_count, count, heads, buckets = dims
    width = z.shape[1]
    everything = pay[...]
    lane = iota(everything.shape, 1)
    score = everything
    names = pltpu.roll(everything, 128 - group, 1)
    label = pltpu.roll(everything, 128 - 2 * group, 1)
    used = lane < count
    part = lax.shift_right_logical(iota(everything.shape, 0), int(math.log2(docs)))
    key = jnp.where(used, part * list_count + names.astype(jnp.int32), -1)

    def total_of(values):
        return jnp.sum(jnp.sum(values, axis=1, keepdims=True), axis=0, keepdims=True)

    def top_step(k, top):
        member = key == k
        best = jnp.max(
            jnp.max(jnp.where(member, score, negative), axis=1, keepdims=True),
            axis=0, keepdims=True,
        )
        return jnp.where(member, best, top)

    keys = lists * list_count
    unroll = keys if keys <= 16 else 4
    top = lax.fori_loop(0, keys, top_step, score, unroll=unroll)
    raised = jnp.exp(score - top)

    def sum_step(k, carry):
        total, gain = carry
        member = key == k
        return (
            jnp.where(member, total_of(jnp.where(member, raised, 0.0)), total),
            jnp.where(member, total_of(jnp.where(member, label, 0.0)), gain),
        )

    ones = jnp.ones(everything.shape, f32)
    total, gain = lax.fori_loop(0, keys, sum_step, (ones, ones), unroll=unroll)
    grads = jnp.where(used, raised / total * gain - label, 0.0)
    g_all[...] = grads
    own = grads[0:1, :]
    g_own[...] = jnp.broadcast_to(own, g_own.shape)

    combos = count * group
    pair_of = lax.shift_right_logical(iota((combos, 128), 0), int(math.log2(group)))
    g_combo = jnp.sum(jnp.where(iota((combos, 128), 1) == pair_of, own, 0.0), axis=1, keepdims=True)
    g_pair = jnp.sum(
        jnp.where(iota((group, 128), 1) == iota((group, 128), 0), own, 0.0), axis=1, keepdims=True
    )
    head_rows = iota((group, width), 0) == lax.shift_right_logical(
        iota((group, width), 1), int(math.log2(width // heads))
    )
    queries = qf[...].astype(f32)
    upstream = gctx[...] * g_pair
    for p in range(count):
        at = slice(p * group, (p + 1) * group)
        right[0, at, :] = jnp.where(head_rows, queries[p : p + 1, :], 0.0).astype(bf16)
        right[1, at, :] = jnp.where(head_rows, upstream[p : p + 1, :], 0.0).astype(bf16)
    left[...] = (z[...] * g_combo).astype(bf16)
    term[0:width, :] = mm_tn(left[...], right[0])
    term[width : 2 * width, :] = mm_tn(vz[...], right[1])

    half, piece = keep.shape[0], keep.shape[1]
    blocks = width // piece
    mine = own_code(stages[: half.bit_length()])

    def piece_step(r, carry, target, base):
        owner = mine ^ (base + r)
        side = lax.shift_right_logical(owner, int(math.log2(blocks)))
        at = side * width + (owner & (blocks - 1)) * piece
        target[r] = term[pl.ds(pl.multiple_of(at, group), piece), :].astype(bf16)
        return carry

    lax.fori_loop(0, half, functools.partial(piece_step, target=send, base=half), 0)
    lax.fori_loop(0, half, functools.partial(piece_step, target=keep, base=0), 0)

    smalls[...] = jnp.zeros(smalls.shape, f32)
    smalls[0:1, :] = jnp.sum(a2[...] * g_pair, axis=0, keepdims=True)
    hats = jnp.sum(fhat[...] * g_pair, axis=0, keepdims=True)
    smalls[1:2, :] = hats * as_row(gains, 3)
    smalls[2:3, :] = hats * as_row(gains, 2)
    weighted = dl[...] * g_combo
    summed = weighted[0:group, :]
    for p in range(1, count):
        summed = summed + weighted[p * group : (p + 1) * group, :]
    spots = iota((window, width), 1)
    hot = jnp.where(bucket_of(iota((window, width), 0)) == (spots & (buckets - 1)), 1.0, 0.0)
    spread = lax.dot_general(
        summed, hot, (((1,), (0,)), ((), ())), precision=highest, preferred_element_type=f32
    )
    row_of = lax.shift_right_logical(iota((group, width), 1), int(math.log2(buckets)))
    smalls[3:4, :] = jnp.sum(
        jnp.where(row_of == iota((group, width), 0), spread, 0.0), axis=0, keepdims=True
    )


def terms_call(dims, pay, z, vz, qf, gctx, dl, a2, fhat, gains):
    stages, docs, lists, list_count, count, heads, buckets = dims
    devices = docs * lists
    combos, width = z.shape
    pieces = 1 << len(cut_stages(stages, width))
    piece = 2 * width // pieces
    shape = jax.ShapeDtypeStruct
    half = shape((pieces // 2, piece, width), bf16)
    return pl.pallas_call(
        functools.partial(terms_kernel, dims),
        out_shape=[
            half, half,
            shape((devices, 128), f32),
            shape((8, 128), f32),
            shape((8, width), f32),
        ],
        in_specs=[whole] * 9,
        out_specs=[whole] * 5,
        scratch_shapes=[
            pltpu.VMEM((2 * width, width), f32),
            pltpu.VMEM((combos, width), bf16),
            pltpu.VMEM((2, combos, width), bf16),
        ],
        compiler_params=pltpu.CompilerParams(vmem_limit_bytes=10 * mega),
        cost_estimate=pl.CostEstimate(flops=int(4e9), bytes_accessed=int(1e7), transcendentals=0),
        name="terms",
    )(pay, z, vz, qf, gctx, dl, a2, fhat, gains)


def project_kernel(row, n1, wq, wk, wv, q, k, v):
    for target, low in ((q, wq), (k, wk), (v, wv)):
        target[...] = mm(n1[row], low[...]).astype(bf16)


def project_call(row, n1, wq, wk, wv):
    return pl.pallas_call(
        functools.partial(project_kernel, row),
        out_shape=[jax.ShapeDtypeStruct(n1.shape[1:], bf16)] * 3,
        in_specs=[whole] * 4,
        out_specs=[whole] * 3,
        compiler_params=pltpu.CompilerParams(vmem_limit_bytes=12 * mega),
        cost_estimate=pl.CostEstimate(flops=int(2e9), bytes_accessed=int(4e6), transcendentals=0),
        name=f"project_{row}",
    )(n1, wq, wk, wv)


def bias_kernel(heads, buckets, gains, bias):
    lanes = 4 * window
    vector = bias_vector(gains[4 : 4 + heads, :buckets], lanes, window)
    for h in range(heads):
        bias[h] = pltpu.roll(
            jnp.broadcast_to(vector[h : h + 1, :], (window, lanes)), 0, 1, stride=1, stride_axis=0
        )[:, : 3 * window]


def bias_call(heads, buckets, gains):
    return small_call(
        functools.partial(bias_kernel, heads, buckets), "bias",
        jax.ShapeDtypeStruct((heads, window, 3 * window), f32), gains,
    )


def attention_kernel(
    lengths, tokens_in, bias, wo, *rest
):
    out, tokens, ctx, qseg, kseg, sem = rest[-6:]
    rows, length, width = tokens.shape
    heads = bias.shape[0]
    pairs = lengths.shape[1]
    load = pltpu.make_async_copy(tokens_in, tokens, sem)
    load.start()
    tiles = length // window
    half = iota((2 * window, window), 1) < (width // heads)
    left = half[:window]
    upper = iota((2 * window, window), 0) < window
    chosen = half == upper

    def segment(positions, ends):
        total = jnp.zeros(positions.shape, jnp.int32)
        for end in ends:
            total = total + jnp.where(positions >= end, 1, 0)
        return total

    wide = iota((length, window), 1)
    units = []
    for row in range(rows):
        for j in range(tiles):
            for pair in range(heads // 2):
                units.append((row, j, pair))
    ones = jnp.ones((3 * window, window), bf16)

    def begin(row):
        ends = [at + size for at, size in starts_of(lengths, row, pairs)]
        seg = segment(iota((length, 1), 0), ends)
        qseg[...] = jnp.where(seg == wide, 1.0, 0.0).astype(bf16)
        kseg[...] = jnp.where(jnp.logical_and(seg != wide, wide <= pairs), negative, 0.0).astype(bf16)

    def spans(j):
        t0 = j * window
        k0 = max(j - 1, 0) * window
        k1 = min(j + 2, tiles) * window
        return t0, k0, k1

    def raw_of(row, j, pair):
        t0, k0, k1 = spans(j)
        cols = slice(pair * window, (pair + 1) * window)
        both = rest[3 * row][t0 : t0 + window, cols]
        stacked = jnp.concatenate([both, both], axis=0)
        stacked = jnp.where(chosen, stacked, jnp.zeros_like(stacked))
        mark = qseg[t0 : t0 + window, :]
        return mm_nt(
            jnp.concatenate([stacked, jnp.concatenate([mark, mark], axis=0)], axis=1),
            jnp.concatenate([rest[3 * row + 1][k0:k1, cols], kseg[k0:k1, :]], axis=1),
        )

    def finish(row, j, pair, raw):
        t0, k0, k1 = spans(j)
        off = k0 - (t0 - window)
        cols = slice(pair * window, (pair + 1) * window)
        probs = []
        for side in range(2):
            part = raw[side * window : (side + 1) * window]
            part = part + bias[2 * pair + side, :, off : off + k1 - k0]
            peak = jnp.max(part, axis=-1, keepdims=True)
            probs.append(jnp.exp(part - peak).astype(bf16))
        mixed = mm(
            jnp.concatenate(probs, axis=0),
            jnp.concatenate([rest[3 * row + 2][k0:k1, cols], ones[: k1 - k0]], axis=1),
        )
        ctx[t0 : t0 + window, cols] = jnp.where(
            left,
            mixed[:window, :window] / mixed[:window, window:],
            mixed[window:, :window] / mixed[window:, window:],
        ).astype(bf16)

    def close_row(row):
        if row == 0:
            load.wait()
        out[row] = tokens[row] + mm(ctx[...], wo[...])

    for row in range(rows):
        begin(row)
        last = None
        for unit in units:
            if unit[0] != row:
                continue
            raw = raw_of(*unit)
            if last is not None:
                finish(*last)
            last = unit + (raw,)
        finish(*last)
        close_row(row)


def attention_call(lengths, tokens, bias, wo, projected):
    rows, length, width = tokens.shape
    return pl.pallas_call(
        attention_kernel,
        out_shape=jax.ShapeDtypeStruct(tokens.shape, f32),
        in_specs=[scalars, outside] + [whole] * (2 + len(projected)),
        out_specs=whole,
        scratch_shapes=[
            pltpu.VMEM(tokens.shape, f32),
            pltpu.VMEM((length, width), bf16),
            pltpu.VMEM((length, window), bf16),
            pltpu.VMEM((length, window), bf16),
            pltpu.SemaphoreType.DMA,
        ],
        compiler_params=pltpu.CompilerParams(vmem_limit_bytes=14 * mega),
        cost_estimate=pl.CostEstimate(
            flops=int(1e10), bytes_accessed=int(1e7), transcendentals=int(8e6)
        ),
        name="attention",
    )(lengths, tokens, bias, wo, *projected)


def feed_kernel(row, attended, gains, wi, wf, held, out, normed, total, sem):
    length, width = total.shape
    tile, chunk = 256, 512
    x = attended[row]
    normed[...] = (x * rms_factor(x) * as_row(gains, 1)).astype(bf16)
    total[...] = x

    def finish(t, c, ahead):
        total[t, :] += mm(gelu(ahead).astype(bf16), wf[c, :])

    last = None
    for c in range(wi.shape[1] // chunk):
        for t in range(length // tile):
            t_at, c_at = slice(t * tile, (t + 1) * tile), slice(c * chunk, (c + 1) * chunk)
            ahead = mm(normed[t_at, :], wi[:, c_at])
            if last is not None:
                finish(*last)
            last = (t_at, c_at, ahead)
    finish(*last)
    store = pltpu.make_async_copy(total, out.at[row], sem)
    store.start()
    store.wait()


def feed_call(row, attended, gain, wi, wf, held):
    rows, length, width = attended.shape
    extra = [] if held is None else [held]
    kernel = functools.partial(feed_kernel, row)
    if held is None:
        kernel = lambda a, g, i, f, *rest: feed_kernel(row, a, g, i, f, None, *rest)
    return pl.pallas_call(
        kernel,
        out_shape=jax.ShapeDtypeStruct(attended.shape, f32),
        in_specs=[whole] * 4 + [outside] * len(extra),
        out_specs=outside,
        input_output_aliases={4: 0} if extra else {},
        scratch_shapes=[
            pltpu.VMEM((length, width), bf16),
            pltpu.VMEM((length, width), f32),
            pltpu.SemaphoreType.DMA,
        ],
        compiler_params=pltpu.CompilerParams(vmem_limit_bytes=12 * mega),
        cost_estimate=pl.CostEstimate(
            flops=int(1e10), bytes_accessed=int(1e7), transcendentals=int(3e6)
        ),
        name=f"feed_{row}",
    )(attended, gain, wi, wf, *extra)


def spread_kernel(row, lengths, probs, dl, yk, yv, yq, out):
    pairs = lengths.shape[1]
    out[...] = jnp.zeros(out.shape, f32)
    starts = starts_of(lengths, row, pairs)
    for i, (at, size) in enumerate(starts):
        pair = row * pairs + i
        here = slice(pair * group, (pair + 1) * group)
        left = jnp.concatenate([dl[here, :], probs[here, :]], axis=0)
        right = jnp.concatenate([yk[here, :], yv[here, :]], axis=0)
        base = pl.multiple_of(at - (at & (group - 1)), group)
        out[pl.ds(base, reach), :] += mm_tn(left, right)[:reach]
    for i, (at, size) in enumerate(starts):
        pair = row * pairs + i
        out[pl.ds(at, 1), :] += yq[pair : pair + 1, :]


def spread_call(row, length, lengths, probs, dl, yk, yv, yq):
    return pl.pallas_call(
        functools.partial(spread_kernel, row),
        out_shape=jax.ShapeDtypeStruct((length + reach, yq.shape[1]), f32),
        in_specs=[scalars] + [whole] * 5,
        out_specs=whole,
        compiler_params=pltpu.CompilerParams(vmem_limit_bytes=8 * mega),
        cost_estimate=pl.CostEstimate(flops=int(1e9), bytes_accessed=int(2e6), transcendentals=0),
        name=f"spread_{row}",
    )(lengths, probs, dl, yk, yv, yq)


def tokens_grad_kernel(dims, lengths, tokens_in, g_own, ga, gains, *rest):
    rows, length, width, pairs = dims
    spreads = rest[:rows]
    out, first_sum, tokens, sems = rest[rows:]
    loads = [
        pltpu.make_async_copy(tokens_in.at[r], tokens.at[r], sems.at[r]) for r in range(rows)
    ]
    for load in loads:
        load.start()
    own = g_own[0:1, :]
    lane = iota((1, 128), 1)
    total = jnp.zeros((1, width), f32)
    gain_row = as_row(gains, 0)
    stores = []
    for r in range(rows):
        starts = starts_of(lengths, r, pairs)
        amounts = [
            jnp.sum(jnp.where(lane == r * pairs + i, own, 0.0), axis=1, keepdims=True)
            for i in range(pairs)
        ]
        loads[r].wait()

        def step(i, carry, r=r, starts=starts, amounts=amounts):
            at = pl.ds(pl.multiple_of(i * 64, 64), 64)
            spot = i * 64 + iota((64, 1), 0)
            amount = jnp.zeros((64, 1), f32)
            for (start, size), value in zip(starts, amounts):
                inside = jnp.logical_and(spot >= start, spot < start + size)
                amount = jnp.where(inside, value, amount)
            x = tokens[r, at, :]
            factor = rms_factor(x)
            hat = x * factor
            upstream = spreads[r][at, :] * amount
            tokens[r, at, :] = norm_back(hat, factor, upstream * gain_row)
            return carry + jnp.sum(hat * upstream, axis=0, keepdims=True)

        total = lax.fori_loop(0, length // 64, step, total)
        for i, (at, size) in enumerate(starts):
            pair = r * pairs + i
            tokens[r, pl.ds(at, 1), :] += ga[pair : pair + 1, :] * amounts[i]
        store = pltpu.make_async_copy(tokens.at[r], out.at[r], sems.at[r])
        store.start()
        stores.append(store)
    first_sum[...] = total
    for store in stores:
        store.wait()


def tokens_grad_call(lengths, tokens, g_own, ga, gains, spreads):
    rows, length, width = tokens.shape
    pairs = lengths.shape[1]
    return pl.pallas_call(
        functools.partial(tokens_grad_kernel, (rows, length, width, pairs)),
        out_shape=[
            jax.ShapeDtypeStruct(tokens.shape, f32),
            jax.ShapeDtypeStruct((1, width), f32),
        ],
        in_specs=[scalars, outside] + [whole] * (3 + rows),
        out_specs=[outside, whole],
        scratch_shapes=[
            pltpu.VMEM(tokens.shape, f32),
            pltpu.SemaphoreType.DMA((rows,)),
        ],
        compiler_params=pltpu.CompilerParams(vmem_limit_bytes=12 * mega),
        cost_estimate=pl.CostEstimate(flops=int(2e9), bytes_accessed=int(1e7), transcendentals=0),
        name="tokens_grad",
    )(lengths, tokens, g_own, ga, gains, *spreads)


def outer_kernel(dims, *rest):
    part, chunk, blocks = dims
    halves = rest[:2], rest[2:4]
    g_all, wi, wf = rest[4:7]
    rest = rest[9:] if part else rest[7:]
    factors, g, branch, inner, outer, flat, out_sems = rest[2 if part else 4 :][:7]
    width, hidden = wi.shape
    steps = hidden // chunk
    mine = ((0,), (1,), range(2, steps))[part]
    needed = (4, 5) if part else range(6)
    members = factors.shape[1] // 12
    main = members * 8
    span, half = 3 * width // 2, width // 2

    def scaled(i):
        return (factors[i].astype(f32) * g[...]).astype(bf16)

    def unpack(sources, b):
        near = iota((8, half), 0) < 4
        for i in needed:
            side, at = i // 3, slice((i % 3) * span, (i % 3 + 1) * span)
            held = []
            for d in range(members):
                if side:
                    d = (d & ~12) | ((d & 4) << 1) | ((d & 8) >> 1)
                source = sources[side][d // sources[side][0].shape[0]]
                held.append(source[d % source.shape[0], :, at].astype(f32))
            for k in range(0, members, 2):
                even, odd = held[k], held[k + 1]
                factors[i, k * 8 : (k + 2) * 8, :] = jnp.concatenate(
                    [even[:, :width], odd[:, :width]], axis=0
                ).astype(bf16)
            for k in range(0, members, 4):
                tiles = []
                for j in (k, k + 2):
                    even, odd = held[j][:, width:], held[j + 1][:, width:]
                    tiles.append(
                        jnp.concatenate(
                            [
                                jnp.where(near, even, pltpu.roll(odd, 4, 0)),
                                jnp.where(near, pltpu.roll(even, 4, 0), odd),
                            ],
                            axis=1,
                        )
                    )
                at = main + k * 4
                factors[i, at : at + 16, :] = jnp.concatenate(tiles, axis=0).astype(bf16)
        same = iota((8, 128), 1) == iota((8, 128), 0)
        more = iota((8, 128), 1) == 8 + (iota((8, 128), 0) & 3)
        for d in range(members):
            here = g_all[pl.ds(b * members + d, 1), :]
            g[d * 8 : (d + 1) * 8, :] = jnp.sum(jnp.where(same, here, 0.0), axis=1, keepdims=True)
        for d in range(0, members, 2):
            both = jnp.where(
                iota((8, 128), 0) < 4,
                g_all[pl.ds(b * members + d, 1), :],
                g_all[pl.ds(b * members + d + 1, 1), :],
            )
            at = main + d * 4
            g[at : at + 8, :] = jnp.sum(jnp.where(more, both, 0.0), axis=1, keepdims=True)
        branch[...] = scaled(5)

    def put(target, values, b):
        if blocks == 1:
            target[...] = values
        else:
            target[...] = jnp.where(b == 0, values, target[...] + values)

    def each_block(one):
        if blocks == 1:
            one(0, 0)
        else:
            arrived, sem = rest[-2], rest[-1]

            def step(b, carry):
                for side in range(2):
                    for i in range(2):

                        @pl.when((b < blocks // 2) == (i == 0))
                        def _(side=side, i=i):
                            at = b - i * (blocks // 2)
                            load = pltpu.make_async_copy(
                                halves[side][i].at[pl.ds(at * members, members)],
                                arrived.at[side], sem,
                            )
                            load.start()
                            load.wait()

                unpack([[arrived.at[0]], [arrived.at[1]]], b)
                return one(b, carry)

            lax.fori_loop(0, blocks, step, 0)

    stores = {}

    def save(source, target, sem):
        store = pltpu.make_async_copy(source, target, out_sems.at[sem])
        store.start()
        stores[sem] = store

    if blocks == 1:
        unpack(halves, 0)
    if not part:
        for i, j, slot, target in ((0, 1, 0, rest[2]), (2, 3, 1, rest[3])):

            def square(b, carry, i=i, j=j, slot=slot):
                put(flat.at[slot], mm_tn(factors[i], scaled(j)), b)
                return carry

            each_block(square)
            save(flat.at[slot], target, 4 + slot)
    for c in mine:
        slot = c % 2
        at = slice(c * chunk, (c + 1) * chunk)

        def one(b, carry, slot=slot, at=at):
            value, slope = gelu_pair(mm(factors[4], wi[:, at]))
            grad = (mm_nt(branch[...], wf[at, :]) * slope).astype(bf16)
            put(inner.at[slot], mm_tn(factors[4], grad), b)
            if blocks == 1:
                save(inner.at[slot], rest[0].at[:, pl.ds(c * chunk, chunk)], slot)
            put(outer.at[slot], mm_tn(value.astype(bf16), branch[...]), b)
            return carry

        each_block(one)
        if blocks > 1:
            save(inner.at[slot], rest[0].at[:, pl.ds(c * chunk, chunk)], slot)
        save(outer.at[slot], rest[1].at[pl.ds(c * chunk, chunk), :], 2 + slot)
    for store in stores.values():
        store.wait()


def outer_call(part, held_rows, g_all, wi, wf, held):
    low = held_rows[0]
    devices = 2 * low.shape[0]
    width, hidden = wi.shape
    chunk = hidden // 4
    members = min(devices, 32)
    blocks = devices // members
    block = members * 12
    shape = jax.ShapeDtypeStruct
    wide = [shape((width, hidden), f32), shape((hidden, width), f32)]
    flat = [shape((width, width), f32)] * 2
    place = whole if blocks == 1 else outside
    more = [] if blocks == 1 else [
        pltpu.VMEM((2, members) + low.shape[1:], bf16), pltpu.SemaphoreType.DMA
    ]
    return pl.pallas_call(
        functools.partial(outer_kernel, (part, chunk, blocks)),
        out_shape=wide if part else wide + flat,
        in_specs=[place] * 4 + [whole] * 3 + [outside] * len(held),
        out_specs=[outside] * (2 if part else 4),
        input_output_aliases={7: 0, 8: 1} if held else {},
        scratch_shapes=[
            pltpu.VMEM((6, block, width), bf16),
            pltpu.VMEM((block, 1), f32),
            pltpu.VMEM((block, width), bf16),
            pltpu.VMEM((2, width, chunk), f32),
            pltpu.VMEM((2, chunk, width), f32),
            pltpu.VMEM((2, width, width), f32),
            pltpu.SemaphoreType.DMA((6,)),
        ] + more,
        compiler_params=pltpu.CompilerParams(vmem_limit_bytes=28 * mega),
        cost_estimate=pl.CostEstimate(
            flops=int(1e10), bytes_accessed=int(2e7), transcendentals=int(1e6)
        ),
        name=f"outer_{part}",
    )(*held_rows, g_all, wi, wf, *held)


def small_call(kernel, name, outs, *args):
    return pl.pallas_call(
        kernel,
        out_shape=outs,
        in_specs=[whole] * len(args),
        out_specs=[whole] * len(outs) if isinstance(outs, (list, tuple)) else whole,
        compiler_params=pltpu.CompilerParams(vmem_limit_bytes=8 * mega),
        cost_estimate=pl.CostEstimate(flops=1000, bytes_accessed=int(1e6), transcendentals=0),
        name=name,
    )(*args)


def join(mine, come):
    if mine.size > 1 << 21:
        return jnp.concatenate([mine, come], axis=0)

    def kernel(a, b, out):
        out[: a.shape[0]] = a[...]
        out[a.shape[0] :] = b[...]

    shape = (2 * mine.shape[0],) + mine.shape[1:]
    return small_call(kernel, "join", jax.ShapeDtypeStruct(shape, mine.dtype), mine, come)


def fold(keep, come):
    half = keep.shape[0] // 2

    def kernel(a, b, first, second):
        for i in range(half):
            first[i] = a[i] + b[i]
            second[i] = a[half + i] + b[half + i]

    out = jax.ShapeDtypeStruct((half,) + keep.shape[1:], keep.dtype)
    return small_call(kernel, "fold", [out, out], keep, come)


def fold_columns(keep, come):
    half = keep.shape[2] // 2

    def kernel(a, b, keep_left, send_left, keep_right, send_right):
        for i in range(8):
            first, second, third = i >> 2, (i >> 1) & 1, i & 1
            total = a[i] + b[i]
            (send_left if first else keep_left)[2 * second + third] = total[:, :half]
            (send_right if second else keep_right)[2 * first + third] = total[:, half:]

    out = jax.ShapeDtypeStruct((4, keep.shape[1], half), keep.dtype)
    return tuple(small_call(kernel, "fold_columns", [out] * 4, keep, come))


def fold_pair(left, come_left, right, come_right):
    half = left.shape[2]

    def kernel(a, b, c, d, first, second):
        for i, out in enumerate((first, second)):
            out[0, :, :half] = a[i] + b[i]
            out[0, :, half:] = c[i] + d[i]

    out = jax.ShapeDtypeStruct((1, left.shape[1], 2 * half), left.dtype)
    return small_call(kernel, "fold_pair", [out, out], left, come_left, right, come_right)


def split(mine, come):
    half = mine.shape[2] // 2

    def kernel(a, b, left, right):
        for i, part in enumerate((a, b)):
            at = slice(i * count, (i + 1) * count)
            left[at] = part[:, :, :half]
            right[at] = part[:, :, half:]

    count = mine.shape[0]
    out = jax.ShapeDtypeStruct((2 * count, mine.shape[1], half), mine.dtype)
    return small_call(kernel, "split", [out, out], mine, come)


def weave(left, come_left, right, come_right):
    half = left.shape[2]

    def kernel(a, b, c, d, out):
        for i in range(8):
            first, second, third = i >> 2, (i >> 1) & 1, i & 1
            out[i, :, :half] = (b if first else a)[2 * second + third]
            out[i, :, half:] = (d if second else c)[2 * first + third]

    out = jax.ShapeDtypeStruct((8,) + left.shape[1:2] + (2 * half,), left.dtype)
    return small_call(kernel, "weave", out, left, come_left, right, come_right)


def close(keep, come, smalls, first_sum):
    rows = keep.shape[1]

    def kernel(a, b, c, d, out):
        out[0, :rows, :] = a[0] + b[0]
        low = jnp.where(iota(c.shape, 0) == 4, d[...], c[...])
        tail = jnp.concatenate([low, jnp.zeros_like(low)], axis=0)
        out[0, rows:, :] = tail.astype(bf16)

    out = jax.ShapeDtypeStruct((1, rows + group, keep.shape[2]), keep.dtype)
    return small_call(kernel, "close", out, keep, come, smalls, first_sum)


def add(mine, come):
    def kernel(a, b, out):
        out[...] = a[...] + b[...]

    return small_call(kernel, "add", jax.ShapeDtypeStruct(mine.shape, mine.dtype), mine, come)


def last_kernel(dims, held, *rest):
    stages, part, piece, heads, buckets = dims
    half, _, width = held.shape
    if part:
        earlier, rest = rest[0], rest[3:]
    sides = rest[:2]
    values, sems = rest[-2:]
    me = own_code(stages)
    blocks = width // piece
    for i in range(half):
        owner = me ^ (part * half + i)
        at = pl.multiple_of((owner & (blocks - 1)) * piece, group)
        side_of = lax.shift_right_logical(owner, int(math.log2(blocks)))
        values[i] = held[i, :piece, :].astype(f32)
        for side in range(2):

            @pl.when(side_of == side)
            def _(side=side, at=at, i=i):
                pltpu.make_async_copy(
                    values.at[i], sides[side].at[pl.ds(at, piece), :], sems.at[i]
                ).start()

    total = sum(held[i, piece:, :].astype(f32)[:8] for i in range(half))
    if part:
        total = total + earlier[...]
        for i, out in zip((4, 0, 1, 2), rest[2:6]):
            out[...] = total[i : i + 1, :].reshape(width)
        spots = iota((width, 128), 0)
        by_bucket = jnp.where((spots & (buckets - 1)) == iota((width, 128), 1), 1.0, 0.0)
        by_head = jnp.where(
            lax.shift_right_logical(iota((group, width), 1), int(math.log2(buckets)))
            == iota((group, width), 0),
            total[3:4, :], 0.0,
        )
        by_bucket = by_bucket.astype(bf16)
        high = by_head.astype(bf16)
        rough = (by_head - high.astype(f32)).astype(bf16)
        table = mm(high, by_bucket) + mm(rough, by_bucket)
        rest[6][...] = table[:heads, :buckets]
    else:
        rest[2][...] = total
    for i in range(half):
        pltpu.make_async_copy(values.at[i], sides[0].at[pl.ds(0, piece), :], sems.at[i]).wait()


def last_call(stages, part, held, piece, buckets, heads, earlier):
    half, _, width = held.shape
    shape = jax.ShapeDtypeStruct
    squares = [shape((width, width), f32)] * 2
    more = (
        [shape((width,), f32)] * 4 + [shape((heads, buckets), f32)] if part else [shape((8, width), f32)]
    )
    return pl.pallas_call(
        functools.partial(last_kernel, (stages, part, piece, heads, buckets)),
        out_shape=squares + more,
        in_specs=[whole] * (2 if part else 1) + [outside] * (2 if part else 0),
        out_specs=[outside] * 2 + [whole] * len(more),
        input_output_aliases={2: 0, 3: 1} if part else {},
        scratch_shapes=[pltpu.VMEM((half, piece, width), f32), pltpu.SemaphoreType.DMA((half,))],
        compiler_params=pltpu.CompilerParams(vmem_limit_bytes=12 * mega),
        cost_estimate=pl.CostEstimate(flops=int(1e7), bytes_accessed=int(5e6), transcendentals=0),
        name=f"last_{part}",
    )(held, *earlier)


def shards(
    docs, lists,
    tokens, pair_lengths, list_ids, relevance,
    first_gain, query_weight, key_weight, value_weight, output_weight, bias_table,
    second_gain, inner_weight, outer_weight, final_gain, score_vector,
):
    row_count, length, width = tokens.shape[1:]
    pairs = pair_lengths.shape[2]
    buckets, heads = bias_table.shape
    devices = docs * lists
    sizes = {"docs": docs, "lists": lists}
    stages = tuple(("lists", 1 << b) for b in range(lists.bit_length() - 1)) + tuple(
        ("docs", 1 << b) for b in range(docs.bit_length() - 1)
    )

    def swap(values, stage):
        axis, mask = stage
        return lax.ppermute(values, axis, [(i, i ^ mask) for i in range(sizes[axis])])

    rows = tokens.reshape(row_count, length, width)
    lengths = pair_lengths.reshape(row_count, pairs)
    spot = lax.broadcasted_iota(jnp.int32, (group, width), 0)
    gains = jnp.pad(bias_table.T, ((4, group - 4 - heads), (0, width - buckets)))
    for i, vector in enumerate((first_gain, second_gain, final_gain, score_vector)):
        gains = jnp.where(spot == i, vector[None, :], gains)
    members = list_ids.shape[1]
    known = jnp.pad(list_ids, ((0, 0), (0, members))) + jnp.pad(relevance, ((0, 0), (members, 0)))
    outs = path_call(
        rows, lengths, known, gains, heads, buckets,
        (query_weight, key_weight, value_weight, output_weight, inner_weight, outer_weight),
    )
    pay, factors, n1, probs, dl, turned, yk, yv, qf, gctx, z, vz, ga, a2, fhat, yq = outs[:16]
    wq, wk, wv, wo, wi, wf, scores = outs[16:]

    tie = lax.optimization_barrier
    gather_order = tuple(reversed(stages))

    rows_left = list(gather_order)
    come = None
    projected, bias, spreads = [], None, []
    for i, stage in enumerate(gather_order):
        if i < row_count:
            n1, pay = tie((n1, pay))
            come_pay = swap(pay, stage)
            made = project_call(i, n1, wq, wk, wv)
            come_pay, made = tie((come_pay, tuple(made)))
            projected += made
        elif i == row_count:
            gains, pay = tie((gains, pay))
            come_pay = swap(pay, stage)
            bias = bias_call(heads, buckets, gains)
            come_pay, bias = tie((come_pay, bias))
        elif i == row_count + 1:
            probs, pay = tie((probs, pay))
            come_pay = swap(pay, stage)
            spreads.append(spread_call(0, length, lengths, probs, dl, yk, yv, yq))
            come_pay, spreads = tie((come_pay, spreads))
        else:
            come_pay = swap(pay, stage)
        pay = join(pay, come_pay)
        if i == 0:
            factors, pay = tie((factors, pay))
            come = swap(factors, rows_left.pop(0))
        elif i == 2:
            come, pay = tie((come, pay))
            factors = join(factors, come)
            come = swap(factors, rows_left.pop(0))
    come, pay = tie((come, pay))
    left, right = split(factors, come)
    count = row_count * pairs
    dims = (stages, docs, lists, docs // 2, count, heads, buckets)
    keep, send, g_all, g_own, smalls = terms_call(
        dims, pay, z, vz, qf, gctx, turned, a2, fhat, gains
    )
    piece = keep.shape[1]
    cut = cut_stages(stages, width)
    rest = stages[len(cut) :]
    for stage in cut[:-4]:
        keep, send = fold(keep, swap(send, stage))
    probs, send = tie((probs, send))
    arrived = swap(send, cut[-4])
    for r in range(1, row_count):
        spreads.append(spread_call(r, length, lengths, probs, dl, yk, yv, yq))
    arrived, spreads = tie((arrived, spreads))
    sums = fold_columns(keep, arrived)

    third, fourth = rows_left[:2]
    bias, sums, left, right = tie((bias, sums, left, right))
    arrived = swap(sums[1], cut[-3]), swap(sums[3], cut[-2])
    come = swap(left, third), swap(right, fourth)
    attended = attention_call(lengths, rows, bias, wo, projected)
    arrived, come, attended = tie((arrived, come, attended))
    keep_left, send_left = fold(sums[0], arrived[0])
    keep_right, send_right = fold(sums[2], arrived[1])
    left, right = join(left, come[0]), join(right, come[1])

    attended, send_left, send_right, left, right = tie(
        (attended, send_left, send_right, left, right)
    )
    arrived = swap(send_left, cut[-2]), swap(send_right, cut[-3])
    come = swap(left, fourth), swap(right, third)
    encoded = feed_call(0, attended, gains, wi, wf, None)
    arrived, encoded = tie((arrived, encoded))
    keep, send = fold_pair(keep_left, arrived[0], keep_right, arrived[1])

    spreads, send, encoded = tie((spreads, send, encoded))
    arrived = swap(send, cut[-1])
    grads, first_sum = tokens_grad_call(
        lengths, rows, g_own, ga, gains, spreads
    )
    arrived, grads, first_sum = tie((arrived, grads, first_sum))
    held = close(keep, arrived, smalls, first_sum)

    for stage in rest[:-1]:
        held = add(held, swap(held, stage))
    attended, held = tie((attended, held))
    arrived = swap(held, rest[-1])
    held, come = tie((held, come))
    left, right = join(left, come[0]), join(right, come[1])
    for stage in rows_left[2:-1]:
        left, right = join(left, swap(left, stage)), join(right, swap(right, stage))
    come = swap(left, rows_left[-1]), swap(right, rows_left[-1])
    attended, left = tie((attended, left))
    encoded = feed_call(1, attended, gains, wi, wf, encoded)
    arrived, encoded, come = tie((arrived, encoded, come))
    held = add(held, arrived)
    held_rows = (left, come[0], right, come[1])

    held, held_rows = tie((held, held_rows))
    arrived = swap(held, cut[-1])
    products = tuple(outer_call(0, held_rows, g_all, wi, wf, ()))
    products, arrived = tie((products, arrived))
    wide, (query_grad, output_grad) = products[:2], products[2:]
    left, right = split(held, arrived)

    left, right, wide = tie((left, right, wide))
    come = swap(left, cut[-2]), swap(right, cut[-3])
    wide = tuple(outer_call(1, held_rows, g_all, wi, wf, wide))
    wide, come = tie((wide, come))
    left, right = join(left, come[0]), join(right, come[1])

    left, right, wide = tie((left, right, wide))
    come = swap(left, cut[-3]), swap(right, cut[-2])
    wide = outer_call(2, held_rows, g_all, wi, wf, wide)
    wide, come = tie((tuple(wide), come))
    held = weave(left, come[0], right, come[1])

    for stage in reversed(cut[1:-3]):
        held = join(held, swap(held, stage))
    come = swap(held, cut[0])
    key_grad, value_grad, small_sums = last_call(cut, 0, held, piece, buckets, heads, ())
    (
        key_grad, value_grad, first_grad, second_grad, final_grad, vector_grad, table_grad
    ) = last_call(cut, 1, come, piece, buckets, heads, (small_sums, key_grad, value_grad))
    inner_grad, outer_grad = wide
    return (
        encoded.reshape(tokens.shape),
        scores.reshape(1, row_count, pairs),
        grads.reshape(tokens.shape),
        first_grad,
        query_grad,
        key_grad,
        value_grad,
        output_grad,
        table_grad.T,
        second_grad,
        inner_grad,
        outer_grad,
        final_grad,
        vector_grad,
    )


def solution(mesh):
    placed = P("lists", "docs", None, None)
    return jax.shard_map(
        functools.partial(shards, mesh.shape["docs"], mesh.shape["lists"]),
        mesh=mesh,
        in_specs=(placed, P("lists", "docs", None), P("lists", None), P("lists", None)) + (P(),) * 11,
        out_specs=(placed, P("lists", "docs", None), placed) + (P(),) * 11,
        check_vma=False,
    )
```
